128 devices in a mesh: emb: 16 (over x, y), score: 8 (over z, core).
Axes of the slice: x: 4, y: 4, z: 4, core: 2. Of those that a mesh axis runs over, the one named last changes fastest.
Arguments:
- table: float32 [262144, 200], P(('emb', 'score')), may hold values from -4 to 4
- accum: float32 [262144, 200], P(('emb', 'score')), may hold values from 1e-06 to 0.001
- request: int32 [128, 128, 64], P(('emb', 'score')), may hold values from 0 to 2047, as said below
- head_slot: int32 [16384], P(('emb', 'score')), may hold values from 0 to 8191, as said below
- rel_ids: int32 [16384], P(('emb', 'score')), may hold values from 0 to 1344
- tail_slot: int32 [16384, 65], P(('emb', 'score')), may hold values from 0 to 8191, as said below
- relations: float32 [1345, 200], replicated, may hold values from -4 to 4
- kernel: float32 [9, 32], replicated, may hold values from -2 to 2
- conv_bias: float32 [32], replicated, may hold values from -3 to 3
- fc_weight: bfloat16 [10368, 200], replicated, may hold values from -0.0625 to 0.0625
- fc_bias: float32 [200], replicated, may hold values from -3 to 3
Outputs:
- new_table: float32 [262144, 200], P(('emb', 'score'))
- new_accum: float32 [262144, 200], P(('emb', 'score'))
- fc_grad: float32 [10368, 200], P(('emb', 'score'))
- kernel_grad: float32 [9, 32], replicated
- conv_bias_grad: float32 [32], replicated
- fc_bias_grad: float32 [200], replicated
- rel_grad: float32 [1345, 200], replicated
The draws below stay inside these ranges and needn't reach their ends.
Inputs may be any that keep to these rules, and one draw needn't show every extreme that they name: request[r, o, c] is a row index local to owner o; slots of one (r, o) pair beyond its used count hold some valid index and are named by no triple; every requester uses all 64 slots of at least one owner, and there is one owner whose 64 slots are all used by every requester. `head_slot`: the slot of a triple of requester r is o * 64 + c with c below the used count of the pair (r, o). `tail_slot`: as head_slot, for every candidate tail.
All inputs are finite; a program needn't handle non-finite values.
Results may differ from the reference program's by a relative error of at most 0.0027.
Values may be sent and summed in bfloat16 or wider, within the bound.
No kernel may reach another device: no remote copies, remote signals or barrier semaphores. Data moves between devices by JAX's collectives and lax.ppermute only.
A program may use at most 192 MiB of HBM per device.

```python
import math
import jax
import jax.numpy as jnp
import numpy as np
from jax import lax

IMG_H = 10
IMG_W = 20
D = 200
CH = 32
FEAT = 10368
NREL = 1345
NEG = 64
TRIP_DEV = 128
CAP = 64
ROWS_DEV = 2048
TRIPLES = 16384
ROWS = 262144
N_EMB = 16
N_SCORE = 8


def used_counts(key):
    devs = N_EMB * N_SCORE
    key_raw, key_weight, key_mine, key_full = jax.random.split(jax.random.fold_in(key, 101), 4)
    raw = jax.random.randint(key_raw, (devs, devs), 1, CAP + 1)
    weight = jax.random.randint(key_weight, (1, devs), 1, 4)
    counts = jnp.clip(raw * weight // 2, 1, CAP)
    mine = jax.random.randint(key_mine, (devs, 1), 0, devs)
    full = jax.random.randint(key_full, (), 0, devs)
    cols = jnp.arange(devs)[None, :]
    counts = jnp.where((cols == mine) | (cols == full), CAP, counts)
    counts = counts.at[devs - 1, devs - 1].set(CAP)
    return counts.astype(jnp.int32)


def pick_owner(running, value):
    return jnp.searchsorted(running, value, side='right')


def slots_of(key, salt, shape):
    devs = N_EMB * N_SCORE
    counts = used_counts(key)
    running = jnp.cumsum(counts, axis=1).astype(jnp.int32)
    totals = running[:, -1]
    key = jax.random.fold_in(key, salt)
    entries = 1
    for extent in shape:
        entries = entries * extent
    per_dev = entries // devs
    pick = jax.random.randint(key, (devs, per_dev), 0, totals[:, None]).astype(jnp.int32)
    owner = jax.vmap(pick_owner)(running, pick).astype(jnp.int32)
    before = jnp.take_along_axis(running - counts, owner, axis=1)
    within = (pick - before).astype(jnp.int32)
    slots = (owner * CAP + within).astype(jnp.int32)
    flat = slots.reshape(-1).at[-1].set(devs * CAP - 1)
    return flat.reshape(shape).astype(jnp.int32)


def draw_request(key, part):
    key = jax.random.fold_in(key, 3)
    devs = N_EMB * N_SCORE
    key_base, key_step = jax.random.split(key)
    base = jax.random.randint(key_base, (devs, devs, 1), 0, ROWS_DEV)
    step = 2 * jax.random.randint(key_step, (devs, devs, 1), 0, max(ROWS_DEV // 2, 1)) + 1
    offsets = jnp.arange(CAP, dtype=jnp.int32)[None, None, :]
    return ((base + offsets * step) % ROWS_DEV).astype(jnp.int32)


def draw_head_slot(key, part):
    return slots_of(key, 5, (TRIPLES,))


def draw_tail_slot(key, part):
    return slots_of(key, 7, (TRIPLES, NEG + 1))


def with_ends(values, own_key, low, high):
    longest = values.shape.index(max(values.shape))
    spots = []
    for shift in (0, 1):
        where = [jax.random.randint(jax.random.fold_in(own_key, axis), (), 0, length) for axis, length in enumerate(values.shape)]
        where[longest] = (where[longest] + shift) % values.shape[longest]
        spots.append(tuple(where))
    return values.at[spots[0]].set(low).at[spots[1]].set(high)


def levels(stream_key, dims, cuts, smallest, largest):
    def one(axis_at, shards_of):
        heights = jax.random.uniform(jax.random.fold_in(jax.random.fold_in(stream_key, 6), axis_at), (shards_of,), jnp.float32, smallest / len(cuts), largest / len(cuts))
        return jnp.repeat(jnp.exp(heights), dims[axis_at] // shards_of).reshape((-1,) + (1,) * (len(dims) - axis_at - 1))

    factor_of = one(*cuts[0])
    for cut in cuts[1:]:
        factor_of = factor_of * one(*cut)
    return factor_of


def rank_bounds(amount, slope):
    loads = [(1 << 20) // math.isqrt(rank ** slope) + 1 for rank in range(1, amount + 1)]
    scale = 1 + sum(loads) // (1 << 30)
    return np.cumsum(np.array([max(1, weight // scale) for weight in loads]))


def skewed_ids(stream_key, shape, number_of, lean):
    grid = rank_bounds(number_of, lean)
    lot = jax.random.randint(jax.random.fold_in(stream_key, 1), shape, 0, int(grid[number_of - 1]))
    standing = jnp.searchsorted(jnp.asarray(grid, jnp.int32), lot, side="right")
    return jax.random.permutation(jax.random.fold_in(stream_key, 2), number_of)[standing].astype(jnp.int32)


def gaussian(rng, shape, scale, bound, cuts=(), kind=jnp.bfloat16):
    factor_of = levels(rng, shape, cuts, -0.22, 0.18) if cuts else 1.0
    values = jax.random.normal(rng, shape, jnp.float32) * scale * factor_of
    return jnp.minimum(jnp.maximum(values, -bound), bound).astype(kind)


def setup_inputs(seed: int = 0) -> dict:
    splits = jax.random.split(jax.random.key(seed), 12)
    return {
        "table": gaussian(splits[0], (ROWS, D), 0.5, 4.0, ((0, 128),), jnp.float32),
        "accum": jnp.clip(jnp.exp(math.log(0.001) - 6.9077553 * jax.random.uniform(splits[1], (ROWS, D), jnp.float32) ** levels(splits[1], (ROWS, D), ((0, 128),), -0.2, 0.2)), 9.999999974752427e-07, 0.001),
        "request": draw_request(jax.random.fold_in(splits[11], 71), 0),
        "head_slot": draw_head_slot(jax.random.fold_in(splits[11], 71), 0),
        "rel_ids": with_ends(skewed_ids(splits[4], (TRIPLES,), NREL, 2), jax.random.fold_in(splits[4], 3), 0, NREL - 1).astype(jnp.int32),
        "tail_slot": draw_tail_slot(jax.random.fold_in(splits[11], 71), 0),
        "relations": gaussian(splits[6], (NREL, D), 0.5, 4.0, (), jnp.float32),
        "kernel": gaussian(splits[7], (9, CH), 9 ** -0.5, 2.0, (), jnp.float32),
        "conv_bias": gaussian(splits[8], (CH,), 0.5, 3.0, (), jnp.float32),
        "fc_weight": gaussian(splits[9], (FEAT, D), FEAT ** -0.5, 0.0625),
        "fc_bias": gaussian(splits[10], (D,), 0.5, 3.0, (), jnp.float32),
    }


HIGH = lax.Precision.HIGHEST
LEARN = 0.1
EPS = 1e-10

def silu_slope(value):
    sig = jax.nn.sigmoid(value)
    return sig * (1.0 + value * (1.0 - sig))

def conv_taps(image, kernel, out_h, out_w):
    total = jnp.zeros((image.shape[0], out_h, out_w, kernel.shape[1]), jnp.float32)
    for tap in range(9):
        row_off, col_off = divmod(tap, 3)
        total = total + image[:, row_off:row_off + out_h, col_off:col_off + out_w, None] * kernel[tap]
    return total

def local_step(rows_buf, head_slot, rel_ids, tail_slot, relations, kernel, conv_bias, fc_weight, fc_bias):
    count = head_slot.shape[0]
    width = rows_buf.shape[1]
    out_h = 2 * IMG_H - 2
    out_w = IMG_W - 2
    onehot = (rel_ids[:, None] == jnp.arange(relations.shape[0], dtype=jnp.int32)[None, :]).astype(jnp.float32)
    rel = jnp.dot(onehot, relations, precision=HIGH)
    heads = rows_buf[head_slot].astype(jnp.float32)
    image = jnp.concatenate([heads.reshape(count, IMG_H, IMG_W), rel.reshape(count, IMG_H, IMG_W)], axis=1)
    conv = conv_taps(image, kernel, out_h, out_w) + conv_bias
    feat = jax.nn.silu(conv).reshape(count, -1).astype(jnp.bfloat16)
    pre = jnp.dot(feat, fc_weight, preferred_element_type=jnp.float32) + fc_bias
    query = jax.nn.silu(pre)
    tails = rows_buf[tail_slot].astype(jnp.float32)
    scores = jnp.einsum('td,tkd->tk', query, tails, precision=HIGH)
    label = (jnp.arange(scores.shape[1]) == 0).astype(jnp.float32)
    dscore = (jax.nn.sigmoid(scores) - label) / scores.shape[1]
    dquery = jnp.einsum('tk,tkd->td', dscore, tails, precision=HIGH)
    dtails = dscore[:, :, None] * query[:, None, :]
    dpre = dquery * silu_slope(pre)
    fb_grad = lax.optimization_barrier(jnp.sum(dpre, axis=0))
    dpre_b = dpre.astype(jnp.bfloat16)
    dfeat = lax.dot_general(dpre_b, fc_weight, (((1,), (1,)), ((), ())), preferred_element_type=jnp.float32)
    dconv = dfeat.reshape(conv.shape) * silu_slope(conv)
    cb_grad = lax.optimization_barrier(jnp.sum(dconv, axis=(0, 1, 2)))
    tap_rows = []
    dimage = jnp.zeros(image.shape, jnp.float32)
    for tap in range(9):
        row_off, col_off = divmod(tap, 3)
        window = image[:, row_off:row_off + out_h, col_off:col_off + out_w]
        tap_rows.append(jnp.einsum('tij,tijc->c', window, dconv, precision=HIGH))
        spread = jnp.einsum('tijc,c->tij', dconv, kernel[tap], precision=HIGH)
        dimage = dimage.at[:, row_off:row_off + out_h, col_off:col_off + out_w].add(spread)
    kernel_grad = jnp.stack(tap_rows, axis=0)
    dheads = dimage[:, :IMG_H].reshape(count, width)
    drel = dimage[:, IMG_H:].reshape(count, width)
    rel_grad = lax.dot_general(onehot, drel, (((0,), (0,)), ((), ())), precision=HIGH)
    slot_grad = jnp.zeros(rows_buf.shape, jnp.float32).at[head_slot].add(dheads)
    slot_grad = slot_grad.at[tail_slot.reshape(-1)].add(dtails.reshape(-1, width))
    return (slot_grad, feat, dpre_b, kernel_grad, cb_grad, fb_grad, rel_grad)

def reference(table, accum, request, head_slot, rel_ids, tail_slot, relations, kernel, conv_bias, fc_weight, fc_bias):
    devs = N_EMB * N_SCORE
    owners = jnp.arange(devs, dtype=jnp.int32)[None, :, None] * ROWS_DEV
    global_ids = (owners + request).astype(jnp.int32).reshape(devs, devs * CAP)
    heads = head_slot.reshape(devs, TRIP_DEV)
    rels = rel_ids.reshape(devs, TRIP_DEV)
    tails = tail_slot.reshape(devs, TRIP_DEV, NEG + 1)

    def one_requester(carry, inputs):
        table_grad, fc_total, kernel_total, cb_total, fb_total, rel_total = carry
        ids, head_part, rel_part, tail_part = inputs
        rows_buf = table[ids].astype(jnp.bfloat16)
        slot_grad, feat, dpre_b, kernel_grad, cb_grad, fb_grad, rel_grad = local_step(rows_buf, head_part, rel_part, tail_part, relations, kernel, conv_bias, fc_weight, fc_bias)
        fc_part = lax.dot_general(feat, dpre_b, (((0,), (0,)), ((), ())), preferred_element_type=jnp.float32)
        table_grad = table_grad.at[ids].add(slot_grad)
        return ((table_grad, fc_total + fc_part, kernel_total + kernel_grad, cb_total + cb_grad, fb_total + fb_grad, rel_total + rel_grad), None)
    start = (jnp.zeros(table.shape, jnp.float32), jnp.zeros(fc_weight.shape, jnp.float32), jnp.zeros(kernel.shape, jnp.float32), jnp.zeros(conv_bias.shape, jnp.float32), jnp.zeros(fc_bias.shape, jnp.float32), jnp.zeros(relations.shape, jnp.float32))
    result, _ = lax.scan(one_requester, start, (global_ids, heads, rels, tails))
    row_grad, fc_grad, kernel_grad, cb_grad, fb_grad, rel_grad = result
    new_accum = accum + row_grad * row_grad
    new_table = table - LEARN * row_grad / (jnp.sqrt(new_accum) + EPS)
    return (new_table, new_accum, fc_grad, kernel_grad, cb_grad, fb_grad, rel_grad)
```

```python
import functools

import jax
import jax.numpy as jnp
import numpy as np
from jax import lax
from jax.experimental import pallas as pl
from jax.experimental.pallas import tpu as pltpu
from jax.sharding import PartitionSpec as P

AXES = ("emb", "score")
DEVS = 128
N_EMB = 16
N_SCORE = 8
SLOTS = 64
ALL_SLOTS = DEVS * SLOTS
OWNED = 2048
D = 200
DP = 208
HALF = DP // 2
TRIPS = 128
CAND = 65
IMG_W = 20
OUT_W = 18
CH = 32
FEAT = 10368
BAND = 1152
BANDS = 9
WIN = 80
STEP = 40
NREL = 1345
RELP = 1408
REL_TILES = 25 * 11
RED_ROWS = 24
LEARN = 0.1
EPS = 1e-10
F32 = jnp.float32
BF16 = jnp.bfloat16
I32 = jnp.int32
NT = (((1,), (1,)), ((), ()))
VMEM_LIMIT = 56 * 1024 * 1024

OFFSETS = [20 * a + b for a in range(3) for b in range(3)]
BIAS_MARK = 500


def offset_map():
    feature = np.arange(BAND)
    place = feature // CH
    origin = (place // OUT_W) * IMG_W + place % OUT_W
    lane = np.arange(256)
    offset = lane[None, :] % WIN - origin[:, None]
    offset = np.where(lane[None, :] < 2 * WIN, offset, -1000)
    offset[:, 3 * WIN] = BIAS_MARK
    return offset.astype(np.int32)


def params():
    return pltpu.CompilerParams(vmem_limit_bytes=VMEM_LIMIT)


def cost(flops, moved):
    return pl.CostEstimate(flops=flops, bytes_accessed=moved, transcendentals=0)


def dot(a, b):
    return jnp.dot(a, b, preferred_element_type=F32)


def dot_nt(a, b):
    return lax.dot_general(a, b, NT, preferred_element_type=F32)


def split(x):
    high = x.astype(BF16)
    low = (x - high.astype(F32)).astype(BF16)
    return high, low


def silu_slope(value):
    sig = jax.nn.sigmoid(value)
    return sig * (1.0 + value * (1.0 - sig))


def to_messages(x):
    top, bottom = x[:HALF], x[HALF:]
    left = lax.broadcasted_iota(I32, (HALF, 128), 1) < SLOTS
    first = jnp.where(left, top, pltpu.roll(bottom, SLOTS, 1))
    second = jnp.where(left, pltpu.roll(top, SLOTS, 1), bottom)
    return first, second


def from_messages(first, second):
    left = lax.broadcasted_iota(I32, (HALF, 128), 1) < SLOTS
    top = jnp.where(left, first, pltpu.roll(second, SLOTS, 1))
    bottom = jnp.where(left, pltpu.roll(first, SLOTS, 1), second)
    return jnp.concatenate([top, bottom], axis=0)


def gather_kernel(want_ref, table_ref, out_ref, rows_ref):
    @pl.when(pl.program_id(0) == 0)
    def _():
        rows_ref[...] = jnp.concatenate(
            [table_ref[...], jnp.zeros((DP - D, OWNED), F32)], axis=0
        ).astype(BF16)

    for q in range(4):
        want = want_ref[:, 256 * q : 256 * q + 256]
        total = jnp.zeros((DP, 256), F32)
        for kb in range(OWNED // 256):
            row = lax.broadcasted_iota(I32, (256, 256), 0) + 256 * kb
            hot = jnp.where(row == want, 1.0, 0.0).astype(BF16)
            total = total + dot(rows_ref[:, 256 * kb : 256 * kb + 256], hot)
        for half in range(2):
            first, second = to_messages(total[:, 128 * half : 128 * half + 128])
            out_ref[4 * q + 2 * half] = first.astype(BF16)
            out_ref[4 * q + 2 * half + 1] = second.astype(BF16)


def gather_rows(want, table_t):
    return pl.pallas_call(
        gather_kernel,
        grid=(8,),
        in_specs=[
            pl.BlockSpec((1, 1024), lambda i: (0, i)),
            pl.BlockSpec((D, OWNED), lambda i: (0, 0)),
        ],
        out_specs=pl.BlockSpec((16, HALF, 128), lambda i: (i, 0, 0)),
        out_shape=jax.ShapeDtypeStruct((DEVS, HALF, 128), BF16),
        scratch_shapes=[pltpu.VMEM((DP, OWNED), BF16)],
        compiler_params=params(),
        cost_estimate=cost(2 * DP * OWNED * ALL_SLOTS, 6 << 20),
        name="gather_rows",
    )(want, table_t)


def counts_kernel(tail_ref, out_ref, buf_ref):
    high_row = lax.broadcasted_iota(I32, (64, 128), 0)
    low_row = lax.broadcasted_iota(I32, (128, 128), 0)

    def one(t, carry):
        slot = tail_ref[pl.ds(t, 1), :]
        high = jnp.where(high_row == (slot >> 7), 1.0, 0.0).astype(BF16)
        low = jnp.where(low_row == (slot & 127), 1.0, 0.0).astype(BF16)
        buf_ref[pl.ds(pl.multiple_of(t * 64, 64), 64), :] = dot_nt(high, low)
        return carry

    lax.fori_loop(0, TRIPS, one, 0, unroll=8)
    for high in range(64):
        out_ref[:, 128 * high : 128 * high + 128] = buf_ref[
            pl.ds(high, TRIPS, stride=64), :
        ].astype(BF16)


def count_tails(tails):
    return pl.pallas_call(
        counts_kernel,
        out_shape=jax.ShapeDtypeStruct((TRIPS, ALL_SLOTS), BF16),
        scratch_shapes=[pltpu.VMEM((ALL_SLOTS, 128), F32)],
        compiler_params=params(),
        cost_estimate=cost(TRIPS * 2 * 64 * 128 * 128, 2 << 20),
        name="count_tails",
    )(tails)


def window_parts(image_ref, p):
    win = image_ref[pl.ds(pl.multiple_of(p * STEP, 8), WIN), :]
    high = win.astype(BF16).astype(F32)
    ones = jnp.ones((256 - 3 * WIN, TRIPS), F32)
    return high, win - high, ones


def forward_kernel(
    msg_ref, head_ref, rel_ref, taps_ref, weight_ref, rows_ref, feat_ref, image_ref, pre_ref
):
    def unpack(kb, head):
        for k in range(4):
            pair = 4 * kb + k
            both = from_messages(
                msg_ref[2 * pair].astype(F32), msg_ref[2 * pair + 1].astype(F32)
            ).astype(BF16)
            rows_ref[:, pl.ds(pl.multiple_of(pair * 128, 128), 128)] = both
            slot = lax.broadcasted_iota(I32, (128, TRIPS), 0) + pair * 128
            hot = jnp.where(slot == head_ref[...], 1.0, 0.0).astype(BF16)
            head = head + dot(both, hot)
        return head

    head = lax.fori_loop(0, 16, unpack, jnp.zeros((DP, TRIPS), F32))
    image_ref[0:D, :] = head[:D]
    image_ref[D : 2 * D, :] = rel_ref[...]

    def band(p, pre):
        high, low, ones = window_parts(image_ref, p)
        stack = jnp.concatenate([high, low, high, ones], axis=0).astype(BF16)
        conv = dot(taps_ref[...], stack)
        feat = (conv * jax.nn.sigmoid(conv)).astype(BF16)
        feat_ref[pl.ds(pl.multiple_of(p * BAND, BAND), BAND), :] = feat
        return pre + dot(weight_ref[:, pl.ds(pl.multiple_of(p * BAND, 128), BAND)], feat)

    pre_ref[...] = lax.fori_loop(0, BANDS, band, jnp.zeros((D, TRIPS), F32))


def forward(msgs, head_row, rel_t, taps, weight_t):
    return pl.pallas_call(
        forward_kernel,
        out_shape=(
            jax.ShapeDtypeStruct((DP, ALL_SLOTS), BF16),
            jax.ShapeDtypeStruct((FEAT, TRIPS), BF16),
            jax.ShapeDtypeStruct((2 * D, TRIPS), F32),
            jax.ShapeDtypeStruct((D, TRIPS), F32),
        ),
        compiler_params=params(),
        cost_estimate=cost(2 * FEAT * TRIPS * (256 + D), 14 << 20),
        name="forward",
    )(msgs, head_row, rel_t, taps, weight_t)


def score_kernel(
    rows_ref, count_ref, true_ref, pre_ref, bias_ref, part_ref, dpre_ref, bias_grad_ref, query_ref
):
    pre = pre_ref[...] + bias_ref[...]
    query = pre * jax.nn.sigmoid(pre)
    pad = jnp.zeros((DP - D, TRIPS), F32)
    query = jnp.concatenate([query, pad], axis=0)
    query_ref[...] = query
    wide = jnp.concatenate([query, jnp.zeros((256 - DP, TRIPS), F32)], axis=0).T[:, :DP]
    high = wide.astype(BF16).astype(F32)
    both = jnp.concatenate([high, wide - high], axis=0).astype(BF16)

    def block(nb, total):
        cols = pl.ds(pl.multiple_of(nb * 256, 256), 256)
        rows = rows_ref[:, cols]
        scores = dot(both, rows)
        scores = scores[:TRIPS] + scores[TRIPS:]
        lane = lax.broadcasted_iota(I32, (TRIPS, 256), 1) + nb * 256
        label = jnp.where(lane == true_ref[...], 1.0, 0.0)
        grad = count_ref[:, cols].astype(F32) * jax.nn.sigmoid(scores) - label
        part = jnp.concatenate(split(grad), axis=0)
        part_ref[:, cols] = part
        return total + dot_nt(rows, part)

    total = lax.fori_loop(0, ALL_SLOTS // 256, block, jnp.zeros((DP, 256), F32))
    dquery = (total[:D, :TRIPS] + total[:D, TRIPS:]) * (1.0 / CAND)
    dpre = dquery * silu_slope(pre)
    bias_grad_ref[...] = jnp.sum(dpre, axis=1, keepdims=True)
    dpre_ref[...] = jnp.concatenate([dpre, pad], axis=0).astype(BF16)


def score(rows_t, counts, true_col, pre, bias_col):
    return pl.pallas_call(
        score_kernel,
        out_shape=(
            jax.ShapeDtypeStruct((2 * TRIPS, ALL_SLOTS), BF16),
            jax.ShapeDtypeStruct((DP, TRIPS), BF16),
            jax.ShapeDtypeStruct((D, 1), F32),
            jax.ShapeDtypeStruct((DP, TRIPS), F32),
        ),
        compiler_params=params(),
        cost_estimate=cost(8 * 256 * DP * ALL_SLOTS, 10 << 20),
        name="score",
    )(rows_t, counts, true_col, pre, bias_col)


def backward_kernel(
    image_ref,
    taps_ref,
    spread_ref,
    weight_ref,
    dpre_ref,
    offset_ref,
    rel_ref,
    dhead_ref,
    red_ref,
    small_ref,
    dimage_ref,
    grad_ref,
):
    dimage_ref[...] = jnp.zeros_like(dimage_ref)
    grad_ref[...] = jnp.zeros_like(grad_ref)

    def band(p, carry):
        high, low, ones = window_parts(image_ref, p)
        stack = jnp.concatenate([high, low, high, ones], axis=0).astype(BF16)
        stack_high = jnp.concatenate([high, jnp.zeros_like(low), high, ones], axis=0).astype(BF16)
        conv = dot(taps_ref[...], stack)
        dfeat = dot(weight_ref[pl.ds(pl.multiple_of(p * BAND, BAND), BAND), :], dpre_ref[...])
        dconv = jnp.concatenate(split(dfeat * silu_slope(conv)), axis=1)
        grad_ref[...] += dot_nt(dconv, jnp.concatenate([stack, stack_high], axis=1))
        spread = dot(spread_ref[...], dconv)
        spread = spread[:WIN] + spread[WIN:]
        spread = spread[:, :TRIPS] + spread[:, TRIPS:]
        dimage_ref[pl.ds(pl.multiple_of(p * STEP, 8), WIN), :] += spread
        return carry

    lax.fori_loop(0, BANDS, band, 0)
    dhead_ref[...] = dimage_ref[0:D, :]

    drel = dimage_ref[D : 2 * D, :]
    high = drel.astype(BF16).astype(F32)
    both = jnp.concatenate([high, drel - high], axis=0).astype(BF16)
    for j in range(RELP // 128):
        lane = lax.broadcasted_iota(I32, (TRIPS, 128), 1) + 128 * j
        hot = jnp.where(lane == rel_ref[...], 1.0, 0.0).astype(BF16)
        part = dot(both, hot)
        part = part[:D] + part[D:]
        for i in range(D // 8):
            tile = 11 * i + j
            red_ref[8 * tile : 8 * tile + 8, :] = part[8 * i : 8 * i + 8]
    red_ref[8 * REL_TILES :, :] = jnp.zeros((DEVS * RED_ROWS - 8 * REL_TILES, 128), F32)

    lane = lax.broadcasted_iota(I32, (CH, 128), 1)
    small = jnp.zeros((CH, 128), F32)
    for k, mark in enumerate(OFFSETS + [BIAS_MARK]):
        total = jnp.zeros((CH, 256), F32)
        for g in range(BAND // CH):
            at = slice(CH * g, CH * g + CH)
            total = total + jnp.where(offset_ref[at] == mark, grad_ref[at], 0.0)
        small = jnp.where(lane == k, jnp.sum(total, axis=1, keepdims=True), small)
    small_ref[...] = small


def backward(image, taps, spread, weight, dpre, offsets, rel_col):
    return pl.pallas_call(
        backward_kernel,
        out_shape=(
            jax.ShapeDtypeStruct((D, TRIPS), F32),
            jax.ShapeDtypeStruct((DEVS * RED_ROWS, 128), F32),
            jax.ShapeDtypeStruct((CH, 128), F32),
        ),
        scratch_shapes=[pltpu.VMEM((2 * D, TRIPS), F32), pltpu.VMEM((BAND, 256), F32)],
        compiler_params=params(),
        cost_estimate=cost(8 * 256 * FEAT * TRIPS, 14 << 20),
        name="backward",
    )(image, taps, spread, weight, dpre, offsets, rel_col)


def slots_kernel(query_ref, part_ref, dhead_ref, head_ref, out_ref):
    q_high, q_low = split(query_ref[...] * (1.0 / CAND))
    dhead = jnp.concatenate([dhead_ref[...], jnp.zeros((DP - D, TRIPS), F32)], axis=0)
    left = jnp.concatenate([q_high, q_low, q_high, *split(dhead)], axis=1)

    def block(nb, carry):
        cols = pl.ds(pl.multiple_of(nb * 256, 256), 256)
        high = part_ref[0:TRIPS, cols]
        low = part_ref[TRIPS:, cols]
        lane = lax.broadcasted_iota(I32, (TRIPS, 256), 1) + nb * 256
        hot = jnp.where(lane == head_ref[...], 1.0, 0.0).astype(BF16)
        grad = dot(left, jnp.concatenate([high, high, low, hot, hot], axis=0))
        most = jnp.max(jnp.abs(grad), axis=0, keepdims=True)
        power = jnp.clip(jnp.ceil(jnp.log2(jnp.maximum(most, 1e-30))), -90.0, 90.0)
        fixed = jnp.floor(grad * jnp.exp2(14.0 - power) + 0.5)
        row = lax.broadcasted_iota(I32, (DP, 256), 0)
        fixed = jnp.where(row == D, power, fixed)
        for half in range(2):
            first, second = to_messages(fixed[:, 128 * half : 128 * half + 128])
            out_ref[4 * nb + 2 * half] = first.astype(I32).astype(jnp.int16)
            out_ref[4 * nb + 2 * half + 1] = second.astype(I32).astype(jnp.int16)
        return carry

    lax.fori_loop(0, ALL_SLOTS // 256, block, 0)


def slot_grads(query, part, dhead, head_col):
    return pl.pallas_call(
        slots_kernel,
        out_shape=jax.ShapeDtypeStruct((DEVS, HALF, 128), jnp.int16),
        compiler_params=params(),
        cost_estimate=cost(2 * DP * 640 * ALL_SLOTS, 8 << 20),
        name="slot_grads",
    )(query, part, dhead, head_col)


def update_kernel(want_ref, msg_ref, table_ref, accum_ref, table_out, accum_out, part_ref):
    nb = pl.program_id(0)

    @pl.when(nb == 0)
    def _():
        def unpack(pair, carry):
            fixed = from_messages(
                msg_ref[2 * pair].astype(I32).astype(F32),
                msg_ref[2 * pair + 1].astype(I32).astype(F32),
            )
            grad = fixed * jnp.exp2(fixed[D : D + 1] - 14.0)
            high, low = split(grad)
            cols = pl.ds(pl.multiple_of(pair * 128, 128), 128)
            part_ref[0:DP, cols] = high
            part_ref[DP:, cols] = low
            return carry

        lax.fori_loop(0, DEVS // 2, unpack, 0)

    def block(kb, total):
        cols = pl.ds(pl.multiple_of(kb * 512, 512), 512)
        row = lax.broadcasted_iota(I32, (256, 512), 0) + nb * 256
        hot = jnp.where(row == want_ref[:, cols], 1.0, 0.0).astype(BF16)
        return total + dot_nt(part_ref[:, cols], hot)

    total = lax.fori_loop(0, ALL_SLOTS // 512, block, jnp.zeros((2 * DP, 256), F32))
    grad = total[:D] + total[DP : DP + D]
    accum = accum_ref[...] + grad * grad
    accum_out[...] = accum
    table_out[...] = table_ref[...] - LEARN * grad / (jnp.sqrt(accum) + EPS)


def update(want, msgs, table_t, accum_t):
    rows = pl.BlockSpec((D, 256), lambda i: (0, i))
    return pl.pallas_call(
        update_kernel,
        grid=(OWNED // 256,),
        in_specs=[
            pl.BlockSpec((1, ALL_SLOTS), lambda i: (0, 0)),
            pl.BlockSpec((DEVS, HALF, 128), lambda i: (0, 0, 0)),
            rows,
            rows,
        ],
        out_specs=(rows, rows),
        out_shape=(
            jax.ShapeDtypeStruct((D, OWNED), F32),
            jax.ShapeDtypeStruct((D, OWNED), F32),
        ),
        scratch_shapes=[pltpu.VMEM((2 * DP, ALL_SLOTS), BF16)],
        compiler_params=params(),
        cost_estimate=cost(4 * DP * OWNED * ALL_SLOTS, 10 << 20),
        name="update",
    )(want, msgs, table_t, accum_t)


def projection_kernel(feat_ref, dpre_ref, out_ref):
    total = jnp.zeros((FEAT // N_EMB, DP), F32)
    for e in range(0, N_EMB, 2):
        total = total + dot_nt(
            jnp.concatenate([feat_ref[e], feat_ref[e + 1]], axis=1),
            jnp.concatenate([dpre_ref[e], dpre_ref[e + 1]], axis=1),
        )
    out_ref[...] = total[:, :D]


def projection(feats, dpres):
    return pl.pallas_call(
        projection_kernel,
        out_shape=jax.ShapeDtypeStruct((FEAT // N_EMB, D), F32),
        compiler_params=params(),
        cost_estimate=cost(2 * FEAT * TRIPS * DP, 4 << 20),
        name="projection",
    )(feats, dpres)


def exchange(x, axes):
    return lax.all_to_all(x, axes, split_axis=0, concat_axis=0, tiled=True)


def rounded(x):
    return lax.reduce_precision(x, 8, 7)


def tap_matrices(kernel, conv_bias):
    offsets = jnp.asarray(offset_map()[:, :WIN])
    per_feature = jnp.tile(kernel, (1, BAND // CH))
    taps = jnp.zeros((BAND, WIN), F32)
    for k, offset in enumerate(OFFSETS):
        taps = taps + jnp.where(offsets == offset, per_feature[k][:, None], 0.0)
    high = rounded(taps)
    low = taps - high
    bias = jnp.tile(conv_bias, BAND // CH)
    b0 = rounded(bias)
    b1 = rounded(bias - b0)
    b2 = bias - b0 - b1
    rest = jnp.zeros((BAND, 256 - 3 * WIN - 3), F32)
    columns = [high, high, low, b0[:, None], b1[:, None], b2[:, None], rest]
    stacked = jnp.concatenate(columns, axis=1).astype(BF16)
    spread = jnp.concatenate([high, low], axis=1).T.astype(BF16)
    return stacked, spread


def shards(
    table,
    accum,
    request,
    head_slot,
    rel_ids,
    tail_slot,
    relations,
    kernel,
    conv_bias,
    fc_weight,
    fc_bias,
):
    table_t = table.T
    want = exchange(request[0], AXES).reshape(1, ALL_SLOTS)
    outgoing = gather_rows(want, table_t)
    incoming = exchange(outgoing, AXES)

    tails = jnp.pad(tail_slot, ((0, 0), (0, 128 - CAND)), constant_values=-1)
    counts = count_tails(tails)
    hot = (jnp.arange(NREL, dtype=I32)[:, None] == rel_ids[None, :]).astype(F32)
    rel_t = jnp.dot(relations.T, hot, precision=lax.Precision.HIGHEST)
    taps, spread = tap_matrices(kernel, conv_bias)
    weight = jnp.pad(fc_weight, ((0, 0), (0, DP - D)))

    rows_t, feat, image, pre = forward(incoming, head_slot[None, :], rel_t, taps, fc_weight.T)
    feats = exchange(feat.reshape(N_EMB, FEAT // N_EMB, TRIPS), "emb")
    part, dpre, bias_grad, query = score(
        rows_t, counts, tail_slot[:, :1], pre, fc_bias[:, None]
    )
    dpres = exchange(jnp.broadcast_to(dpre[None], (N_EMB, DP, TRIPS)), "emb")
    dhead, packed, small = backward(
        image, taps, spread, weight, dpre, jnp.asarray(offset_map()), rel_ids[:, None]
    )
    returned = exchange(slot_grads(query, part, dhead, head_slot[:, None]), AXES)

    smalls = jnp.concatenate([small[:, :10].T.reshape(-1), bias_grad[:, 0]])
    smalls = jnp.pad(smalls, (0, 1024 - smalls.shape[0])).reshape(8, 128)
    packed = lax.dynamic_update_slice(packed, smalls, (8 * REL_TILES, 0))
    shares = exchange(packed.reshape(DEVS, RED_ROWS, 128), AXES)
    share = jnp.sum(shares, axis=0)
    sums = exchange(jnp.broadcast_to(share[None], (DEVS, RED_ROWS, 128)), AXES)
    sums = sums.reshape(DEVS * RED_ROWS, 128)

    partial = projection(feats, dpres).reshape(N_SCORE, FEAT // DEVS, D)
    fc_grad = jnp.sum(exchange(partial, "score"), axis=0)

    new_table, new_accum = update(want, returned, table_t, accum.T)
    rel_sum = sums[: 8 * REL_TILES].reshape(25, 11, 8, 128).transpose(0, 2, 1, 3)
    rel_sum = rel_sum.reshape(D, RELP)[:, :NREL].T
    rest = sums[8 * REL_TILES : 8 * REL_TILES + 8].reshape(-1)
    kernel_sum = rest[: 9 * CH].reshape(9, CH)
    return (
        new_table.T,
        new_accum.T,
        fc_grad,
        kernel_sum,
        rest[9 * CH : 10 * CH],
        rest[10 * CH : 10 * CH + D],
        rel_sum,
    )


def solution(mesh):
    rows = P(AXES, None)
    in_specs = (rows, rows, P(AXES, None, None), P(AXES), P(AXES), rows) + (P(),) * 5
    out_specs = (rows, rows, rows) + (P(),) * 4
    return jax.shard_map(shards, mesh=mesh, in_specs=in_specs, out_specs=out_specs, check_vma=False)
```

```python
import jax
import jax.numpy as jnp
import numpy as np
from jax import lax
from jax.experimental import pallas as pl
from jax.experimental.pallas import tpu as pltpu
from jax.sharding import PartitionSpec as P

AXES = ("emb", "score")
DEVS = 128
N_EMB = 16
N_SCORE = 8
SLOTS = 64
ALL_SLOTS = DEVS * SLOTS
OWNED = 2048
D = 200
DP = 208
HALF = DP // 2
TRIPS = 128
CAND = 65
IMG_W = 20
OUT_W = 18
CH = 32
FEAT = 10368
BAND = 1152
BANDS = 9
WIN = 80
STEP = 40
NREL = 1345
RELP = 1408
REL_ROWS = 200 * 11
SHARE = 18
SHARE_ROWS = 24
SMALL_DEV = 124
MSG_ROWS = HALF + SHARE_ROWS
CHUNK = FEAT // N_EMB
OWN_FEAT = FEAT // DEVS
CHUNK_WIN = 104
LEARN = 0.1
EPS = 1e-10
F32 = jnp.float32
BF16 = jnp.bfloat16
I32 = jnp.int32
NT = (((1,), (1,)), ((), ()))
FILL = 0.9999
VMEM_LIMIT = 56 * 1024 * 1024

OFFSETS = [20 * a + b for a in range(3) for b in range(3)]
BIAS_MARK = 500
LOW = 1000


def offset_map():
    feature = np.arange(BAND)
    place = feature // CH
    origin = (place // OUT_W) * IMG_W + place % OUT_W
    lane = np.arange(256)
    offset = lane[None, :] % WIN - origin[:, None]
    offset = np.where((offset >= 0) & (offset < 43), offset, -1)
    offset = np.where(lane[None, :] < 2 * WIN, offset, offset + LOW)
    for part in range(16):
        offset[:, 3 * WIN + part] = BIAS_MARK + part
    return offset.astype(np.int32)


def params():
    return pltpu.CompilerParams(vmem_limit_bytes=VMEM_LIMIT)


def cost(flops, moved):
    return pl.CostEstimate(flops=flops, bytes_accessed=moved, transcendentals=0)


def dot(a, b):
    return jnp.dot(a, b, preferred_element_type=F32)


def dot_nt(a, b):
    return lax.dot_general(a, b, NT, preferred_element_type=F32)


def split(x):
    high = x.astype(BF16)
    low = (x - high.astype(F32)).astype(BF16)
    return high, low


def sigmoid(value):
    return 0.5 * jnp.tanh(0.5 * value) + 0.5


def silu_slope(value):
    sig = sigmoid(value)
    return sig * (1.0 + value * (1.0 - sig))


def to_messages(x):
    top, bottom = x[:HALF], x[HALF:]
    left = lax.broadcasted_iota(I32, (HALF, 128), 1) < SLOTS
    first = jnp.where(left, top, pltpu.roll(bottom, SLOTS, 1))
    second = jnp.where(left, pltpu.roll(top, SLOTS, 1), bottom)
    return first, second


def from_messages(first, second):
    left = lax.broadcasted_iota(I32, (HALF, 128), 1) < SLOTS
    top = jnp.where(left, first, pltpu.roll(second, SLOTS, 1))
    bottom = jnp.where(left, pltpu.roll(first, SLOTS, 1), second)
    return jnp.concatenate([top, bottom], axis=0)


def code_share(x):
    most = jnp.max(jnp.abs(x))
    power = jnp.clip(jnp.ceil(jnp.log2(jnp.maximum(jnp.full((1, 128), most), 1e-30))), -90.0, 90.0)
    scaled = x * (jnp.exp2(15.0 - power) * FILL)
    fixed = jnp.floor(scaled + 0.5)
    rest = jnp.floor((scaled - fixed) * 16384.0 + 0.5)
    row = lax.broadcasted_iota(I32, (SHARE_ROWS, 128), 0)
    tail = jnp.where(row == SHARE, power, pltpu.roll(rest, SHARE + 1, 0))
    return jnp.where(row < SHARE, fixed, tail)


def decode_share(coded):
    row = lax.broadcasted_iota(I32, (SHARE_ROWS, 128), 0)
    rest = pltpu.roll(coded, SHARE_ROWS - SHARE - 1, 0) * (1.0 / 16384.0)
    first = SHARE_ROWS - SHARE - 1
    value = coded + jnp.where(row < first, rest, 0.0)
    return jnp.where(row < SHARE, value, 0.0) * (jnp.exp2(coded[SHARE : SHARE + 1] - 15.0) * (1.0 / FILL))


def gather_kernel(want_ref, table_ref, out_ref, rows_ref):
    @pl.when(pl.program_id(0) == 0)
    def _():
        rows_ref[...] = jnp.concatenate(
            [table_ref[...], jnp.zeros((DP - D, OWNED), F32)], axis=0
        ).astype(BF16)

    for q in range(4):
        want = want_ref[:, 256 * q : 256 * q + 256]
        total = jnp.zeros((DP, 256), F32)
        for kb in range(OWNED // 256):
            row = lax.broadcasted_iota(I32, (256, 256), 0) + 256 * kb
            hot = jnp.where(row == want, 1.0, 0.0).astype(BF16)
            total = total + dot(rows_ref[:, 256 * kb : 256 * kb + 256], hot)
        for half in range(2):
            first, second = to_messages(total[:, 128 * half : 128 * half + 128])
            out_ref[4 * q + 2 * half] = first.astype(BF16)
            out_ref[4 * q + 2 * half + 1] = second.astype(BF16)


def gather_rows(want, table_t):
    return pl.pallas_call(
        gather_kernel,
        grid=(8,),
        in_specs=[
            pl.BlockSpec((1, 1024), lambda i: (0, i)),
            pl.BlockSpec((D, OWNED), lambda i: (0, 0)),
        ],
        out_specs=pl.BlockSpec((16, HALF, 128), lambda i: (i, 0, 0)),
        out_shape=jax.ShapeDtypeStruct((DEVS, HALF, 128), BF16),
        scratch_shapes=[pltpu.VMEM((DP, OWNED), BF16)],
        compiler_params=params(),
        cost_estimate=cost(2 * DP * OWNED * ALL_SLOTS, 6 << 20),
        name="gather_rows",
    )(want, table_t)


def counts_kernel(tail_ref, out_ref, buf_ref):
    high_row = lax.broadcasted_iota(I32, (64, 128), 0)
    low_row = lax.broadcasted_iota(I32, (128, 128), 0)

    def one(t, carry):
        slot = tail_ref[pl.ds(t, 1), :]
        high = jnp.where(high_row == (slot >> 7), 1.0, 0.0).astype(BF16)
        low = jnp.where(low_row == (slot & 127), 1.0, 0.0).astype(BF16)
        buf_ref[pl.ds(pl.multiple_of(t * 64, 64), 64), :] = dot_nt(high, low)
        return carry

    lax.fori_loop(0, TRIPS, one, 0, unroll=8)
    for high in range(64):
        out_ref[:, 128 * high : 128 * high + 128] = buf_ref[
            pl.ds(high, TRIPS, stride=64), :
        ].astype(BF16)


def count_tails(tails):
    return pl.pallas_call(
        counts_kernel,
        out_shape=jax.ShapeDtypeStruct((TRIPS, ALL_SLOTS), BF16),
        scratch_shapes=[pltpu.VMEM((ALL_SLOTS, 128), F32)],
        compiler_params=params(),
        cost_estimate=cost(TRIPS * 2 * 64 * 128 * 128, 2 << 20),
        name="count_tails",
    )(tails)


def window_parts(image_ref, p):
    win = image_ref[pl.ds(pl.multiple_of(p * STEP, 8), WIN), :]
    high = win.astype(BF16).astype(F32)
    ones = jnp.ones((256 - 3 * WIN, TRIPS), F32)
    return high, win - high, ones


def heads_kernel(msg_ref, head_ref, rows_ref, out_ref, own_ref):
    def unpack(kb, head):
        for k in range(2):
            both = []
            for pair in (4 * kb + 2 * k, 4 * kb + 2 * k + 1):
                first = msg_ref[2 * pair].astype(F32)
                second = msg_ref[2 * pair + 1].astype(F32)
                both.append(from_messages(first, second))
            both = jnp.concatenate(both, axis=1).astype(BF16)
            base = pl.multiple_of(kb * 512 + k * 256, 256)
            rows_ref[:, pl.ds(base, 256)] = both
            slot = lax.broadcasted_iota(I32, (256, TRIPS), 0) + base
            hot = jnp.where(slot == head_ref[...], 1.0, 0.0).astype(BF16)
            head = head + dot(both, hot)
        return head

    head = lax.fori_loop(0, 16, unpack, jnp.zeros((DP, TRIPS), F32), unroll=4).astype(BF16)
    own_ref[...] = head
    for e in range(N_EMB):
        out_ref[e] = head


def unpack_heads(msgs, head_row):
    return pl.pallas_call(
        heads_kernel,
        out_shape=(
            jax.ShapeDtypeStruct((DP, ALL_SLOTS), BF16),
            jax.ShapeDtypeStruct((N_EMB, DP, TRIPS), BF16),
            jax.ShapeDtypeStruct((DP, TRIPS), BF16),
        ),
        compiler_params=params(),
        cost_estimate=cost(2 * DP * TRIPS * ALL_SLOTS, 8 << 20),
        name="unpack_heads",
    )(msgs, head_row)


def forward_kernel(head_ref, rel_ref, taps_ref, weight_ref, image_ref, pre_ref):
    image_ref[0:D, :] = head_ref[...].astype(F32)[:D]
    image_ref[D : 2 * D, :] = rel_ref[...]

    def band(p, pre):
        high, low, ones = window_parts(image_ref, p)
        stack = jnp.concatenate([high, low, high, ones], axis=0).astype(BF16)
        conv = dot(taps_ref[...], stack)
        feat = (conv * sigmoid(conv)).astype(BF16)
        return pre + dot(weight_ref[:, pl.ds(pl.multiple_of(p * BAND, 128), BAND)], feat)

    pre_ref[...] = lax.fori_loop(0, BANDS, band, jnp.zeros((D, TRIPS), F32), unroll=True)


def forward(head, rel_t, taps, weight_t):
    return pl.pallas_call(
        forward_kernel,
        out_shape=(
            jax.ShapeDtypeStruct((2 * D, TRIPS), F32),
            jax.ShapeDtypeStruct((D, TRIPS), F32),
        ),
        compiler_params=params(),
        cost_estimate=cost(2 * FEAT * TRIPS * (256 + D), 5 << 20),
        name="forward",
    )(head, rel_t, taps, weight_t)


def score_kernel(
    rows_ref, count_ref, true_ref, pre_ref, bias_ref,
    part_ref, send_ref, dpre_ref, bias_grad_ref, query_ref,
):
    pre = pre_ref[...] + bias_ref[...]
    query = pre * sigmoid(pre)
    pad = jnp.zeros((DP - D, TRIPS), F32)
    query = jnp.concatenate([query, pad], axis=0)
    query_ref[...] = query
    wide = jnp.concatenate([query, jnp.zeros((256 - DP, TRIPS), F32)], axis=0).T[:, :DP]
    high = wide.astype(BF16).astype(F32)
    both = jnp.concatenate([high, wide - high], axis=0).astype(BF16)

    def block(nb, total):
        cols = pl.ds(pl.multiple_of(nb * 256, 256), 256)
        rows = rows_ref[:, cols]
        scores = dot(both, rows)
        scores = scores[:TRIPS] + scores[TRIPS:]
        lane = lax.broadcasted_iota(I32, (TRIPS, 256), 1) + nb * 256
        label = jnp.where(lane == true_ref[...], 1.0, 0.0)
        grad = count_ref[:, cols].astype(F32) * sigmoid(scores) - label
        part = jnp.concatenate(split(grad), axis=0)
        part_ref[:, cols] = part
        return total + dot_nt(rows, part)

    total = lax.fori_loop(0, ALL_SLOTS // 256, block, jnp.zeros((DP, 256), F32), unroll=8)
    dquery = (total[:D, :TRIPS] + total[:D, TRIPS:]) * (1.0 / CAND)
    dpre = dquery * silu_slope(pre)
    bias_grad_ref[...] = jnp.sum(dpre, axis=1, keepdims=True)
    dpre_ref[...] = dpre.astype(BF16)
    dpre = jnp.concatenate([dpre, pad], axis=0).astype(BF16)
    for e in range(N_EMB):
        send_ref[e] = dpre


def score(rows_t, counts, true_col, pre, bias_col):
    return pl.pallas_call(
        score_kernel,
        out_shape=(
            jax.ShapeDtypeStruct((2 * TRIPS, ALL_SLOTS), BF16),
            jax.ShapeDtypeStruct((N_EMB, DP, TRIPS), BF16),
            jax.ShapeDtypeStruct((D, TRIPS), BF16),
            jax.ShapeDtypeStruct((D, 1), F32),
            jax.ShapeDtypeStruct((DP, TRIPS), F32),
        ),
        compiler_params=params(),
        cost_estimate=cost(8 * 256 * DP * ALL_SLOTS, 10 << 20),
        name="score",
    )(rows_t, counts, true_col, pre, bias_col)


def backward_kernel(
    image_ref,
    taps_ref,
    spread_ref,
    weight_ref,
    dpre_ref,
    offset_ref,
    rel_ref,
    bias_grad_ref,
    dhead_ref,
    share_ref,
    dimage_ref,
    grad_ref,
    flat_ref,
):
    dimage_ref[...] = jnp.zeros_like(dimage_ref)
    grad_ref[...] = jnp.zeros_like(grad_ref)

    def band(p, carry):
        high, low, ones = window_parts(image_ref, p)
        stack = jnp.concatenate([high, low, high, ones], axis=0).astype(BF16)
        stack_high = jnp.concatenate([high, jnp.zeros_like(low), high, ones], axis=0).astype(BF16)
        conv = dot(taps_ref[...], stack)
        dfeat = dot(weight_ref[pl.ds(pl.multiple_of(p * BAND, BAND), BAND), :], dpre_ref[...])
        dconv = jnp.concatenate(split(dfeat * silu_slope(conv)), axis=1)
        grad_ref[...] += dot_nt(dconv, jnp.concatenate([stack, stack_high], axis=1))
        spread = dot(spread_ref[...], dconv)
        spread = spread[:WIN] + spread[WIN:]
        spread = spread[:, :TRIPS] + spread[:, TRIPS:]
        dimage_ref[pl.ds(pl.multiple_of(p * STEP, 8), WIN), :] += spread
        return carry

    lax.fori_loop(0, BANDS, band, 0, unroll=3)
    dhead_ref[...] = dimage_ref[0:D, :]

    drel = dimage_ref[D : 2 * D, :]
    high = drel.astype(BF16).astype(F32)
    both = jnp.concatenate([high, drel - high], axis=0).astype(BF16)
    for j in range(RELP // 128):
        lane = lax.broadcasted_iota(I32, (TRIPS, 128), 1) + 128 * j
        hot = jnp.where(lane == rel_ref[...], 1.0, 0.0).astype(BF16)
        part = dot(both, hot)
        part = part[:D] + part[D:]
        for i in range(D // 8):
            tile = 11 * i + j
            flat_ref[8 * tile : 8 * tile + 8, :] = part[8 * i : 8 * i + 8]

    lane = lax.broadcasted_iota(I32, (CH, 128), 1)
    totals = [jnp.zeros((CH, 128), F32) for _ in range(10)]
    for g in range(BAND // CH):
        at = slice(CH * g, CH * g + CH)
        whole = grad_ref[at]
        both = whole[:, :128] + pltpu.roll(whole, 256 - WIN, 1)[:, :128]
        mark = offset_ref[at, 0:128]
        for k, offset in enumerate(OFFSETS):
            here = (mark == offset) & (lane < WIN)
            totals[k] = totals[k] + jnp.where(here, both, 0.0)
        totals[9] = totals[9] + jnp.where(lane == 3 * WIN - 128, whole[:, 128:], 0.0)
    small = jnp.zeros((CH, 128), F32)
    for k in range(10):
        small = jnp.where(lane == k, jnp.sum(totals[k], axis=1, keepdims=True), small)
    small = jnp.concatenate([small, jnp.zeros((128 - CH, 128), F32)], axis=0).T[:16]
    bias = jnp.concatenate([bias_grad_ref[...], jnp.zeros((256 - D, 1), F32)], axis=0)
    bias = jnp.broadcast_to(bias, (256, 128)).T[:8]
    row = lax.broadcasted_iota(I32, (8, 128), 0)
    lane = lax.broadcasted_iota(I32, (8, 128), 1)
    tail = jnp.zeros((8, 128), F32)
    for k in range(10):
        at = CH * (k % 4)
        moved = small[k : k + 1] if at == 0 else pltpu.roll(small[k : k + 1], at, 1)
        here = (row == k // 4) & (lane >= at) & (lane < at + CH)
        tail = jnp.where(here, moved, tail)
    tail = jnp.where(row == 3, bias[0:1, :128], tail)
    tail = jnp.where(row == 4, bias[0:1, 128:], tail)

    flat_ref[REL_ROWS:, :] = jnp.zeros((DEVS * SHARE - REL_ROWS, 128), F32)
    flat_ref[SMALL_DEV * SHARE : SMALL_DEV * SHARE + 8, :] = tail
    blank = jnp.zeros((SHARE_ROWS - SHARE, 128), F32)
    for dev in range(DEVS):
        mine = flat_ref[dev * SHARE : dev * SHARE + SHARE, :]
        share_ref[dev] = jnp.concatenate([mine, blank], axis=0)


def backward(image, taps, spread, weight, dpre, offsets, rel_col, bias_grad):
    return pl.pallas_call(
        backward_kernel,
        out_shape=(
            jax.ShapeDtypeStruct((D, TRIPS), F32),
            jax.ShapeDtypeStruct((DEVS, SHARE_ROWS, 128), F32),
        ),
        scratch_shapes=[
            pltpu.VMEM((2 * D, TRIPS), F32),
            pltpu.VMEM((BAND, 256), F32),
            pltpu.VMEM((DEVS * SHARE, 128), F32),
        ],
        compiler_params=params(),
        cost_estimate=cost(8 * 256 * FEAT * TRIPS, 14 << 20),
        name="backward",
    )(image, taps, spread, weight, dpre, offsets, rel_col, bias_grad)


def slots_kernel(query_ref, part_ref, dhead_ref, head_ref, share_ref, out_ref):
    q_high, q_low = split(query_ref[...] * (1.0 / CAND))
    dhead = jnp.concatenate([dhead_ref[...], jnp.zeros((DP - D, TRIPS), F32)], axis=0)
    left = jnp.concatenate([q_high, q_low, q_high, *split(dhead)], axis=1)

    def block(nb, carry):
        cols = pl.ds(pl.multiple_of(nb * 256, 256), 256)
        high = part_ref[0:TRIPS, cols]
        low = part_ref[TRIPS:, cols]
        lane = lax.broadcasted_iota(I32, (TRIPS, 256), 1) + nb * 256
        hot = jnp.where(lane == head_ref[...], 1.0, 0.0).astype(BF16)
        grad = dot(left, jnp.concatenate([high, high, low, hot, hot], axis=0))
        most = jnp.max(jnp.abs(grad), axis=0, keepdims=True)
        power = jnp.clip(jnp.ceil(jnp.log2(jnp.maximum(most, 1e-30))), -90.0, 90.0)
        fixed = jnp.floor(grad * (jnp.exp2(15.0 - power) * FILL) + 0.5)
        row = lax.broadcasted_iota(I32, (DP, 256), 0)
        fixed = jnp.where(row == D, power, fixed)
        for half in range(2):
            pair = to_messages(fixed[:, 128 * half : 128 * half + 128])
            for k in range(2):
                dev = 4 * nb + 2 * half + k
                whole = jnp.concatenate([pair[k], code_share(share_ref[dev])], axis=0)
                out_ref[dev] = whole.astype(I32).astype(jnp.int16)
        return carry

    lax.fori_loop(0, ALL_SLOTS // 256, block, 0, unroll=8)


def slot_grads(query, part, dhead, head_col, shares):
    return pl.pallas_call(
        slots_kernel,
        out_shape=jax.ShapeDtypeStruct((DEVS, MSG_ROWS, 128), jnp.int16),
        compiler_params=params(),
        cost_estimate=cost(2 * DP * 640 * ALL_SLOTS, 8 << 20),
        name="slot_grads",
    )(query, part, dhead, head_col, shares)


def update_kernel(
    want_ref, msg_ref, table_ref, accum_ref, table_out, accum_out, part_ref, column_ref
):
    nb = pl.program_id(0)

    @pl.when(nb == 0)
    def _():
        def unpack(pair, carry):
            cols = pl.ds(pl.multiple_of(pair * 128, 128), 128)
            fixed = from_messages(
                msg_ref[2 * pair].astype(I32).astype(F32)[:HALF],
                msg_ref[2 * pair + 1].astype(I32).astype(F32)[:HALF],
            )
            grad = fixed * (jnp.exp2(fixed[D : D + 1] - 15.0) * (1.0 / FILL))
            high, low = split(grad)
            part_ref[0:DP, cols] = high
            part_ref[DP:, cols] = low
            column_ref[cols, :] = jnp.broadcast_to(want_ref[:, cols], (128, 128)).T
            return carry

        lax.fori_loop(0, DEVS // 2, unpack, 0, unroll=4)

    def block(kb, total):
        slots = pl.ds(pl.multiple_of(kb * 2048, 2048), 2048)
        lane = lax.broadcasted_iota(I32, (2048, 128), 1) + nb * 256
        column = column_ref[slots, :]
        hot = jnp.concatenate(
            [
                jnp.where(column == lane, 1.0, 0.0).astype(BF16),
                jnp.where(column == lane + 128, 1.0, 0.0).astype(BF16),
            ],
            axis=1,
        )
        return total + dot(part_ref[:, slots], hot)

    total = lax.fori_loop(0, ALL_SLOTS // 2048, block, jnp.zeros((2 * DP, 256), F32), unroll=True)
    grad = total[:D] + total[DP : DP + D]
    accum = accum_ref[...] + grad * grad
    accum_out[...] = accum
    table_out[...] = table_ref[...] - LEARN * grad / (jnp.sqrt(accum) + EPS)


def update(want, msgs, table_t, accum_t):
    rows = pl.BlockSpec((D, 256), lambda i: (0, i))
    return pl.pallas_call(
        update_kernel,
        grid=(OWNED // 256,),
        in_specs=[
            pl.BlockSpec((1, ALL_SLOTS), lambda i: (0, 0)),
            pl.BlockSpec((DEVS, MSG_ROWS, 128), lambda i: (0, 0, 0)),
            rows,
            rows,
        ],
        out_specs=(rows, rows),
        out_shape=(
            jax.ShapeDtypeStruct((D, OWNED), F32),
            jax.ShapeDtypeStruct((D, OWNED), F32),
        ),
        scratch_shapes=[
            pltpu.VMEM((2 * DP, ALL_SLOTS), BF16),
            pltpu.VMEM((ALL_SLOTS, 128), I32),
        ],
        compiler_params=params(),
        cost_estimate=cost(4 * DP * OWNED * ALL_SLOTS, 10 << 20),
        name="update",
    )(want, msgs, table_t, accum_t)


def share_kernel(msg_ref, out_ref):
    def one(dev, total):
        coded = msg_ref[dev].astype(I32).astype(F32)
        return total + decode_share(coded[32 - SHARE_ROWS :])

    total = lax.fori_loop(0, DEVS, one, jnp.zeros((SHARE_ROWS, 128), F32), unroll=4)
    coded = code_share(total).astype(I32).astype(jnp.int16)
    for dev in range(DEVS):
        out_ref[dev] = coded


def sum_shares(msgs):
    return pl.pallas_call(
        share_kernel,
        grid=(1,),
        in_specs=[pl.BlockSpec((DEVS, 32, 128), lambda i: (0, MSG_ROWS // 32 - 1, 0))],
        out_specs=pl.BlockSpec((DEVS, SHARE_ROWS, 128), lambda i: (0, 0, 0)),
        out_shape=jax.ShapeDtypeStruct((DEVS, SHARE_ROWS, 128), jnp.int16),
        compiler_params=params(),
        cost_estimate=cost(1 << 20, 2 << 20),
        name="sum_shares",
    )(msgs)


def spread_kernel(sum_ref, rel_ref, kernel_ref, conv_ref, fc_ref, flat_ref):
    for dev in range(DEVS):
        value = decode_share(sum_ref[dev].astype(I32).astype(F32))
        flat_ref[dev * SHARE : dev * SHARE + SHARE, :] = value[:SHARE]
    for i in range(D // 8):
        for j in range(11):
            tile = flat_ref[8 * (11 * i + j) : 8 * (11 * i + j) + 8, :]
            last = min(128, NREL - 128 * j)
            rel_ref[8 * i : 8 * i + 8, 128 * j : 128 * j + last] = tile[:, :last]
    small = flat_ref[SMALL_DEV * SHARE : SMALL_DEV * SHARE + 8, :]
    for k in range(10):
        at = CH * (k % 4)
        row = small[k // 4 : k // 4 + 1]
        row = (row if at == 0 else pltpu.roll(row, 128 - at, 1))[:, :CH]
        if k < 9:
            kernel_ref[k : k + 1, :] = row
        else:
            conv_ref[...] = row
    fc_ref[...] = jnp.concatenate([small[3:4], small[4:5]], axis=1)[:, :D]


def spread_sums(sums):
    return pl.pallas_call(
        spread_kernel,
        out_shape=(
            jax.ShapeDtypeStruct((D, NREL), F32),
            jax.ShapeDtypeStruct((9, CH), F32),
            jax.ShapeDtypeStruct((1, CH), F32),
            jax.ShapeDtypeStruct((1, D), F32),
        ),
        scratch_shapes=[pltpu.VMEM((DEVS * SHARE, 128), F32)],
        compiler_params=params(),
        cost_estimate=cost(1 << 20, 2 << 20),
        name="spread_sums",
    )(sums)


def relations_kernel(ids_ref, rel_ref, out_ref):
    rel = rel_ref[...]
    high = rel.astype(BF16).astype(F32)
    both = jnp.concatenate([high, rel - high], axis=0).astype(BF16)
    for e in range(0, N_EMB, 2):
        cols = slice(128 * e, 128 * e + 256)
        row = lax.broadcasted_iota(I32, (RELP, 256), 0)
        hot = jnp.where(row == ids_ref[:, cols], 1.0, 0.0).astype(BF16)
        out_ref[:, cols] = dot(both, hot).astype(BF16)


def group_relations(ids, relations_t):
    return pl.pallas_call(
        relations_kernel,
        out_shape=jax.ShapeDtypeStruct((2 * D, N_EMB * TRIPS), BF16),
        compiler_params=params(),
        cost_estimate=cost(4 * D * RELP * N_EMB * TRIPS, 3 << 20),
        name="group_relations",
    )(ids, relations_t)


def projection_kernel(start_ref, head_ref, rel_ref, taps_ref, dpre_ref, out_ref, high_ref, low_ref):
    start = pl.multiple_of(start_ref[0] * STEP, 8)
    blank = jnp.zeros((24, 256), F32)
    total = jnp.zeros((CHUNK, DP), F32)
    for e in range(0, N_EMB, 2):
        cols = slice(128 * e, 128 * e + 256)
        head = jnp.concatenate([head_ref[e], head_ref[e + 1]], axis=1).astype(F32)
        rel = rel_ref[:, cols].astype(F32)
        high_ref[...] = jnp.concatenate([head[:D], rel[:D], blank], axis=0)
        low_ref[...] = jnp.concatenate([jnp.zeros((D, 256), F32), rel[D:], blank], axis=0)
        high = high_ref[pl.ds(start, CHUNK_WIN), :]
        low = low_ref[pl.ds(start, CHUNK_WIN), :]
        rest = (128 - CHUNK_WIN, 256)
        ones, none = jnp.ones(rest, F32), jnp.zeros(rest, F32)
        stack = jnp.concatenate([high, ones, low, none, high, none], axis=0).astype(BF16)
        conv = dot(taps_ref[...], stack)
        feat = (conv * sigmoid(conv)).astype(BF16)
        total = total + dot_nt(feat, jnp.concatenate([dpre_ref[e], dpre_ref[e + 1]], axis=1))
    for s in range(N_SCORE):
        out_ref[s] = total[OWN_FEAT * s : OWN_FEAT * s + OWN_FEAT, :D]


def projection(start, heads, rels, taps, dpres):
    vmem = pl.BlockSpec(memory_space=pltpu.VMEM)
    return pl.pallas_call(
        projection_kernel,
        in_specs=[pl.BlockSpec(memory_space=pltpu.SMEM), vmem, vmem, vmem, vmem],
        out_specs=vmem,
        out_shape=jax.ShapeDtypeStruct((N_SCORE, OWN_FEAT, D), F32),
        scratch_shapes=[pltpu.VMEM((2 * D + 24, 256), F32), pltpu.VMEM((2 * D + 24, 256), F32)],
        compiler_params=params(),
        cost_estimate=cost(2 * FEAT * TRIPS * 640, 4 << 20),
        name="projection",
    )(start, heads, rels, taps, dpres)


def exchange(x, axes):
    return lax.all_to_all(x, axes, split_axis=0, concat_axis=0, tiled=True)


def high_part(x):
    return x.astype(BF16).astype(F32)


def taps_kernel(place_ref, small_ref, offset_ref, taps_ref, spread_ref, chunk_ref, twice_ref, all_ref):
    columns = small_ref[...].T
    twice_ref[0:CH, :] = columns[:CH]
    twice_ref[CH : 2 * CH, :] = columns[:CH]
    columns = columns[:CH]

    def one_of(codes, columns):
        value = jnp.zeros(codes.shape, F32)
        for k, offset in enumerate(OFFSETS):
            value = jnp.where(codes == offset, columns[:, k : k + 1], value)
        return value

    def bias_parts(columns):
        bias = columns[:, 9:10]
        first = high_part(bias)
        second = high_part(bias - first)
        return first, second, bias - first - second

    for g in range(BAND // CH):
        at = slice(CH * g, CH * g + CH)
        codes = offset_ref[at]
        low = codes >= LOW - 1
        value = one_of(jnp.where(low, codes - LOW, codes), columns)
        value = jnp.where(low, value - high_part(value), value)
        for part, column in enumerate(bias_parts(columns)):
            value = jnp.where(codes == BIAS_MARK + part, column, value)
        all_ref[at, :] = value
    whole = all_ref[...]
    taps_ref[...] = whole.astype(BF16)
    high = whole[:, :128].T[:WIN]
    low = pltpu.roll(whole, 256 - 2 * WIN, 1)[:, :128].T[:WIN]
    spread_ref[...] = jnp.concatenate([high, low], axis=0).astype(BF16)

    first = place_ref[0] * CHUNK
    base = place_ref[1] * STEP
    columns = twice_ref[pl.ds(pl.multiple_of((place_ref[0] % 4) * 8, 8), CH), :]
    parts = bias_parts(columns)
    lane = lax.broadcasted_iota(I32, (CH, 128), 1)
    for g in range(CHUNK // CH + 1):
        size = min(CH, CHUNK - CH * g)
        feature = lax.broadcasted_iota(I32, (CH, 128), 0) + (first + CH * g)
        place = feature >> 5
        row = ((place.astype(F32) + 0.5) * (1.0 / OUT_W)).astype(I32)
        origin = row * IMG_W + (place - row * OUT_W) - base
        value = jnp.where(lane < CHUNK_WIN, one_of(lane - origin, columns), 0.0)
        high = high_part(value)
        biased = high
        for part in range(3):
            biased = jnp.where(lane == CHUNK_WIN + part, parts[part], biased)
        whole = jnp.concatenate([biased, high, value - high], axis=1).astype(BF16)
        chunk_ref[CH * g : CH * g + size, :] = whole[:size]


def build_taps(place, small, offsets):
    vmem = pl.BlockSpec(memory_space=pltpu.VMEM)
    return pl.pallas_call(
        taps_kernel,
        in_specs=[pl.BlockSpec(memory_space=pltpu.SMEM), vmem, vmem],
        out_specs=(vmem,) * 3,
        out_shape=(
            jax.ShapeDtypeStruct((BAND, 256), BF16),
            jax.ShapeDtypeStruct((2 * WIN, BAND), BF16),
            jax.ShapeDtypeStruct((CHUNK, 384), BF16),
        ),
        scratch_shapes=[pltpu.VMEM((2 * CH, 128), F32), pltpu.VMEM((BAND, 256), F32)],
        compiler_params=params(),
        cost_estimate=cost(1 << 20, 3 << 20),
        name="build_taps",
    )(place, small, offsets)


def shards(
    table,
    accum,
    request,
    head_slot,
    rel_ids,
    tail_slot,
    relations,
    kernel,
    conv_bias,
    fc_weight,
    fc_bias,
):
    table_t = table.T
    asked = jnp.concatenate(
        [
            request[0],
            jnp.zeros((DEVS, SLOTS), I32),
            jnp.broadcast_to(rel_ids[None], (DEVS, TRIPS)),
        ],
        axis=1,
    )
    asked = exchange(asked, AXES)
    want = asked[:, :SLOTS].reshape(1, ALL_SLOTS)
    group = asked[:, 128:].reshape(N_EMB, N_SCORE, TRIPS)
    group = lax.dynamic_index_in_dim(group, lax.axis_index("score"), 1, keepdims=False)
    outgoing = gather_rows(want, table_t)
    incoming = exchange(outgoing, AXES)

    tails = jnp.pad(tail_slot, ((0, 0), (0, 128 - CAND)), constant_values=-1)
    counts = count_tails(tails)
    hot = (jnp.arange(NREL, dtype=I32)[:, None] == rel_ids[None, :]).astype(F32)
    rel_t = jnp.dot(relations.T, hot, precision=lax.Precision.HIGHEST)
    emb = lax.axis_index("emb")
    start = emb * CHUNK // (OUT_W * CH) // 2
    small = jnp.concatenate([kernel, conv_bias[None]], axis=0)
    small = jnp.pad(small, ((0, 118), (0, 128 - CH)))
    offsets = jnp.asarray(offset_map())
    taps, spread, chunk_taps = build_taps(jnp.stack([emb, start]), small, offsets)
    rels = group_relations(
        group.reshape(1, N_EMB * TRIPS), jnp.pad(relations.T, ((0, 0), (0, RELP - NREL)))
    )
    columns = (tail_slot[:, :1], fc_bias[:, None], rel_ids[:, None], head_slot[:, None])
    ready = (counts, rel_t, taps, spread, chunk_taps, fc_weight, rels, columns)
    incoming, ready = lax.optimization_barrier((incoming, ready))
    counts, rel_t, taps, spread, chunk_taps, weight, rels, columns = ready
    true_col, bias_col, rel_col, head_col = columns

    rows_t, head_send, head = unpack_heads(incoming, head_slot[None, :])
    heads = exchange(head_send, "emb")
    image, pre = forward(head, rel_t, taps, fc_weight.T)
    part, dpre_send, dpre, bias_grad, query = score(rows_t, counts, true_col, pre, bias_col)
    dpre_send, heads = lax.optimization_barrier((dpre_send, heads))
    dpres = exchange(dpre_send, "emb")
    dhead, shares = backward(
        image, taps, spread, weight, dpre, offsets, rel_col, bias_grad
    )
    returned = exchange(slot_grads(query, part, dhead, head_col, shares), AXES)

    partial = projection(start.reshape(1), heads, rels, chunk_taps, dpres)
    here = lax.axis_index("score")
    fc_grad = lax.dynamic_index_in_dim(partial, here, 0, keepdims=False)
    for step in range(1, N_SCORE):
        there = lax.rem(here + step, N_SCORE)
        part_there = lax.dynamic_index_in_dim(partial, there, 0, keepdims=False)
        ring = [(i, (i + step) % N_SCORE) for i in range(N_SCORE)]
        fc_grad = fc_grad + lax.ppermute(part_there, "score", ring)

    sums = exchange(sum_shares(returned), AXES)
    new_table, new_accum = update(want, returned, table_t, accum.T)
    rel_sum, kernel_sum, conv_sum, fc_sum = spread_sums(sums)
    return (
        new_table.T,
        new_accum.T,
        fc_grad,
        kernel_sum,
        conv_sum[0],
        fc_sum[0],
        rel_sum.T,
    )


def solution(mesh):
    rows = P(AXES, None)
    in_specs = (rows, rows, P(AXES, None, None), P(AXES), P(AXES), rows) + (P(),) * 5
    out_specs = (rows, rows, rows) + (P(),) * 4
    return jax.shard_map(shards, mesh=mesh, in_specs=in_specs, out_specs=out_specs, check_vma=False)
```

```python
import jax
import jax.numpy as jnp
import numpy as np
from jax import lax
from jax.experimental import pallas as pl
from jax.experimental.pallas import tpu as pltpu
from jax.sharding import PartitionSpec as P

AXES = ("emb", "score")
DEVS = 128
N_EMB = 16
N_SCORE = 8
SLOTS = 64
ALL_SLOTS = DEVS * SLOTS
OWNED = 2048
D = 200
DP = 208
HALF = DP // 2
TRIPS = 128
CAND = 65
IMG_W = 20
OUT_W = 18
CH = 32
FEAT = 10368
BAND = 1152
BANDS = 9
WIN = 80
STEP = 40
NREL = 1345
RELP = 1408
REL_ROWS = 200 * 11
SHARE = 18
SHARE_ROWS = 24
SMALL_DEV = 124
MSG_ROWS = HALF + SHARE_ROWS
CHUNK = FEAT // N_EMB
OWN_FEAT = FEAT // DEVS
CHUNK_WIN = 104
LEARN = 0.1
EPS = 1e-10
F32 = jnp.float32
BF16 = jnp.bfloat16
I32 = jnp.int32
NT = (((1,), (1,)), ((), ()))
FILL = 0.9999
VMEM_LIMIT = 56 * 1024 * 1024

OFFSETS = [20 * a + b for a in range(3) for b in range(3)]
BIAS_MARK = 500
LOW = 1000


def offset_map():
    feature = np.arange(BAND)
    place = feature // CH
    origin = (place // OUT_W) * IMG_W + place % OUT_W
    lane = np.arange(256)
    offset = lane[None, :] % WIN - origin[:, None]
    offset = np.where((offset >= 0) & (offset < 43), offset, -1)
    offset = np.where(lane[None, :] < 2 * WIN, offset, offset + LOW)
    for part in range(16):
        offset[:, 3 * WIN + part] = BIAS_MARK + part
    return offset.astype(np.int32)


def params():
    return pltpu.CompilerParams(vmem_limit_bytes=VMEM_LIMIT)


def cost(flops, moved):
    return pl.CostEstimate(flops=flops, bytes_accessed=moved, transcendentals=0)


def dot(a, b):
    return jnp.dot(a, b, preferred_element_type=F32)


def dot_nt(a, b):
    return lax.dot_general(a, b, NT, preferred_element_type=F32)


def split(x):
    high = x.astype(BF16)
    low = (x - high.astype(F32)).astype(BF16)
    return high, low


def sigmoid(value):
    return 0.5 * jnp.tanh(0.5 * value) + 0.5


def silu_slope(value):
    sig = sigmoid(value)
    return sig * (1.0 + value * (1.0 - sig))


def as_column(row):
    return jnp.broadcast_to(row, (128, row.shape[1])).T


def to_messages(x):
    top, bottom = x[:HALF], x[HALF:]
    left = lax.broadcasted_iota(I32, (HALF, 128), 1) < SLOTS
    first = jnp.where(left, top, pltpu.roll(bottom, SLOTS, 1))
    second = jnp.where(left, pltpu.roll(top, SLOTS, 1), bottom)
    return first, second


def from_messages(first, second):
    left = lax.broadcasted_iota(I32, (HALF, 128), 1) < SLOTS
    top = jnp.where(left, first, pltpu.roll(second, SLOTS, 1))
    bottom = jnp.where(left, pltpu.roll(first, SLOTS, 1), second)
    return jnp.concatenate([top, bottom], axis=0)


def code_share(x):
    most = jnp.max(jnp.abs(x), axis=0, keepdims=True)
    power = jnp.clip(jnp.ceil(jnp.log2(jnp.maximum(most, 1e-30))), -90.0, 90.0)
    scaled = x * (jnp.exp2(15.0 - power) * FILL)
    fixed = jnp.floor(scaled + 0.5)
    rest = jnp.floor((scaled - fixed) * 16384.0 + 0.5)
    row = lax.broadcasted_iota(I32, (SHARE_ROWS, 128), 0)
    tail = jnp.where(row == SHARE, power, pltpu.roll(rest, SHARE + 1, 0))
    return jnp.where(row < SHARE, fixed, tail)


def decode_share(coded):
    row = lax.broadcasted_iota(I32, (SHARE_ROWS, 128), 0)
    rest = pltpu.roll(coded, SHARE_ROWS - SHARE - 1, 0) * (1.0 / 16384.0)
    first = SHARE_ROWS - SHARE - 1
    value = coded + jnp.where(row < first, rest, 0.0)
    return jnp.where(row < SHARE, value, 0.0) * (jnp.exp2(coded[SHARE : SHARE + 1] - 15.0) * (1.0 / FILL))


def gather_kernel(want_ref, table_ref, out_ref, rows_ref):
    @pl.when(pl.program_id(0) == 0)
    def _():
        rows_ref[...] = jnp.concatenate(
            [table_ref[...], jnp.zeros((DP - D, OWNED), F32)], axis=0
        ).astype(BF16)

    for q in range(4):
        want = want_ref[:, 256 * q : 256 * q + 256]
        total = jnp.zeros((DP, 256), F32)
        for kb in range(OWNED // 256):
            row = lax.broadcasted_iota(I32, (256, 256), 0) + 256 * kb
            hot = jnp.where(row == want, 1.0, 0.0).astype(BF16)
            total = total + dot(rows_ref[:, 256 * kb : 256 * kb + 256], hot)
        for half in range(2):
            first, second = to_messages(total[:, 128 * half : 128 * half + 128])
            out_ref[4 * q + 2 * half] = first.astype(BF16)
            out_ref[4 * q + 2 * half + 1] = second.astype(BF16)


def gather_rows(want, table_t):
    return pl.pallas_call(
        gather_kernel,
        grid=(8,),
        in_specs=[
            pl.BlockSpec((1, 1024), lambda i: (0, i)),
            pl.BlockSpec((D, OWNED), lambda i: (0, 0)),
        ],
        out_specs=pl.BlockSpec((16, HALF, 128), lambda i: (i, 0, 0)),
        out_shape=jax.ShapeDtypeStruct((DEVS, HALF, 128), BF16),
        scratch_shapes=[pltpu.VMEM((DP, OWNED), BF16)],
        compiler_params=params(),
        cost_estimate=cost(2 * DP * OWNED * ALL_SLOTS, 6 << 20),
        name="gather_rows",
    )(want, table_t)


def counts_kernel(tail_ref, out_ref, buf_ref):
    high_row = lax.broadcasted_iota(I32, (64, 128), 0)
    low_row = lax.broadcasted_iota(I32, (128, 128), 0)

    def one(t, carry):
        slot = tail_ref[pl.ds(t, 1), :]
        high = jnp.where(high_row == (slot >> 7), 1.0, 0.0).astype(BF16)
        low = jnp.where(low_row == (slot & 127), 1.0, 0.0).astype(BF16)
        buf_ref[pl.ds(pl.multiple_of(t * 64, 64), 64), :] = dot_nt(high, low)
        return carry

    lax.fori_loop(0, TRIPS, one, 0, unroll=8)
    for high in range(64):
        out_ref[:, 128 * high : 128 * high + 128] = buf_ref[
            pl.ds(high, TRIPS, stride=64), :
        ].astype(BF16)


def count_tails(tails):
    return pl.pallas_call(
        counts_kernel,
        out_shape=jax.ShapeDtypeStruct((TRIPS, ALL_SLOTS), BF16),
        scratch_shapes=[pltpu.VMEM((ALL_SLOTS, 128), F32)],
        compiler_params=params(),
        cost_estimate=cost(TRIPS * 2 * 64 * 128 * 128, 2 << 20),
        name="count_tails",
    )(tails)


def window_parts(image_ref, p):
    win = image_ref[pl.ds(pl.multiple_of(p * STEP, 8), WIN), :]
    high = win.astype(BF16).astype(F32)
    ones = jnp.ones((256 - 3 * WIN, TRIPS), F32)
    return high, win - high, ones


def heads_kernel(msg_ref, head_ref, rows_ref, own_ref):
    def unpack(kb, head):
        for k in range(2):
            both = []
            for pair in (4 * kb + 2 * k, 4 * kb + 2 * k + 1):
                first = msg_ref[2 * pair].astype(F32)
                second = msg_ref[2 * pair + 1].astype(F32)
                both.append(from_messages(first, second))
            both = jnp.concatenate(both, axis=1).astype(BF16)
            base = pl.multiple_of(kb * 512 + k * 256, 256)
            rows_ref[:, pl.ds(base, 256)] = both
            slot = lax.broadcasted_iota(I32, (256, TRIPS), 0) + base
            hot = jnp.where(slot == head_ref[...], 1.0, 0.0).astype(BF16)
            head = head + dot(both, hot)
        return head

    head = lax.fori_loop(0, 16, unpack, jnp.zeros((DP, TRIPS), F32), unroll=4)
    own_ref[...] = head.astype(BF16)


def unpack_heads(msgs, head_row):
    return pl.pallas_call(
        heads_kernel,
        out_shape=(
            jax.ShapeDtypeStruct((DP, ALL_SLOTS), BF16),
            jax.ShapeDtypeStruct((DP, TRIPS), BF16),
        ),
        compiler_params=params(),
        cost_estimate=cost(2 * DP * TRIPS * ALL_SLOTS, 8 << 20),
        name="unpack_heads",
    )(msgs, head_row)


def forward_kernel(head_ref, rel_ref, taps_ref, weight_ref, image_ref, pre_ref):
    image_ref[0:D, :] = head_ref[...].astype(F32)[:D]
    image_ref[D : 2 * D, :] = rel_ref[...]

    def band(p, pre):
        high, low, ones = window_parts(image_ref, p)
        stack = jnp.concatenate([high, low, high, ones], axis=0).astype(BF16)
        conv = dot(taps_ref[...], stack)
        feat = (conv * sigmoid(conv)).astype(BF16)
        return pre + dot(weight_ref[:, pl.ds(pl.multiple_of(p * BAND, 128), BAND)], feat)

    pre_ref[...] = lax.fori_loop(0, BANDS, band, jnp.zeros((D, TRIPS), F32), unroll=True)


def forward(head, rel_t, taps, weight_t):
    return pl.pallas_call(
        forward_kernel,
        out_shape=(
            jax.ShapeDtypeStruct((2 * D, TRIPS), F32),
            jax.ShapeDtypeStruct((D, TRIPS), F32),
        ),
        compiler_params=params(),
        cost_estimate=cost(2 * FEAT * TRIPS * (256 + D), 5 << 20),
        name="forward",
    )(head, rel_t, taps, weight_t)


def score_kernel(
    rows_ref, count_ref, true_ref, pre_ref, bias_ref, own_ref,
    part_ref, send_ref, dpre_ref, bias_grad_ref, query_ref,
):
    bias = jnp.concatenate([bias_ref[...], jnp.zeros((1, 256 - D), F32)], axis=1)
    pre = pre_ref[...] + as_column(bias)[:D]
    true = as_column(true_ref[...])
    true = jnp.concatenate([true, true], axis=1)
    query = pre * sigmoid(pre)
    pad = jnp.zeros((DP - D, TRIPS), F32)
    query = jnp.concatenate([query, pad], axis=0)
    query_ref[...] = query
    wide = jnp.concatenate([query, jnp.zeros((256 - DP, TRIPS), F32)], axis=0).T[:, :DP]
    high = wide.astype(BF16).astype(F32)
    both = jnp.concatenate([high, wide - high], axis=0).astype(BF16)

    def block(nb, total):
        cols = pl.ds(pl.multiple_of(nb * 256, 256), 256)
        rows = rows_ref[:, cols]
        scores = dot(both, rows)
        scores = scores[:TRIPS] + scores[TRIPS:]
        lane = lax.broadcasted_iota(I32, (TRIPS, 256), 1) + nb * 256
        label = jnp.where(lane == true, 1.0, 0.0)
        grad = count_ref[:, cols].astype(F32) * sigmoid(scores) - label
        part = jnp.concatenate(split(grad), axis=0)
        part_ref[:, cols] = part
        return total + dot_nt(rows, part)

    total = lax.fori_loop(0, ALL_SLOTS // 256, block, jnp.zeros((DP, 256), F32), unroll=8)
    dquery = (total[:D, :TRIPS] + total[:D, TRIPS:]) * (1.0 / CAND)
    dpre = dquery * silu_slope(pre)
    bias_grad_ref[...] = jnp.sum(dpre, axis=1, keepdims=True)
    dpre_ref[...] = dpre.astype(BF16)
    dpre = jnp.concatenate([dpre, pad], axis=0).astype(BF16)
    for e in range(N_EMB):
        send_ref[e, 0:DP] = own_ref[...]
        send_ref[e, DP:] = dpre


def score(rows_t, counts, true_row, pre, bias_row, head):
    return pl.pallas_call(
        score_kernel,
        out_shape=(
            jax.ShapeDtypeStruct((2 * TRIPS, ALL_SLOTS), BF16),
            jax.ShapeDtypeStruct((N_EMB, 2 * DP, TRIPS), BF16),
            jax.ShapeDtypeStruct((D, TRIPS), BF16),
            jax.ShapeDtypeStruct((D, 1), F32),
            jax.ShapeDtypeStruct((DP, TRIPS), F32),
        ),
        compiler_params=params(),
        cost_estimate=cost(8 * 256 * DP * ALL_SLOTS, 10 << 20),
        name="score",
    )(rows_t, counts, true_row, pre, bias_row, head)


def backward_kernel(
    image_ref,
    taps_ref,
    spread_ref,
    weight_ref,
    dpre_ref,
    offset_ref,
    rel_ref,
    bias_grad_ref,
    dhead_ref,
    share_ref,
    dimage_ref,
    grad_ref,
    flat_ref,
):
    dimage_ref[...] = jnp.zeros_like(dimage_ref)
    grad_ref[...] = jnp.zeros_like(grad_ref)

    def band(p, carry):
        high, low, ones = window_parts(image_ref, p)
        stack = jnp.concatenate([high, low, high, ones], axis=0).astype(BF16)
        stack_high = jnp.concatenate([high, jnp.zeros_like(low), high, ones], axis=0).astype(BF16)
        conv = dot(taps_ref[...], stack)
        dfeat = dot(weight_ref[pl.ds(pl.multiple_of(p * BAND, BAND), BAND), :], dpre_ref[...])
        dconv = jnp.concatenate(split(dfeat * silu_slope(conv)), axis=1)
        grad_ref[...] += dot_nt(dconv, jnp.concatenate([stack, stack_high], axis=1))
        spread = dot(spread_ref[...], dconv)
        spread = spread[:WIN] + spread[WIN:]
        spread = spread[:, :TRIPS] + spread[:, TRIPS:]
        dimage_ref[pl.ds(pl.multiple_of(p * STEP, 8), WIN), :] += spread
        return carry

    lax.fori_loop(0, BANDS, band, 0, unroll=3)
    dhead_ref[...] = dimage_ref[0:D, :]

    drel = dimage_ref[D : 2 * D, :]
    high = drel.astype(BF16).astype(F32)
    both = jnp.concatenate([high, drel - high], axis=0).astype(BF16)
    rel = as_column(rel_ref[...])
    for j in range(RELP // 128):
        lane = lax.broadcasted_iota(I32, (TRIPS, 128), 1) + 128 * j
        hot = jnp.where(lane == rel, 1.0, 0.0).astype(BF16)
        part = dot(both, hot)
        part = part[:D] + part[D:]
        for i in range(D // 8):
            tile = 11 * i + j
            flat_ref[8 * tile : 8 * tile + 8, :] = part[8 * i : 8 * i + 8]

    lane = lax.broadcasted_iota(I32, (CH, 128), 1)
    totals = [jnp.zeros((CH, 128), F32) for _ in range(10)]
    for g in range(BAND // CH):
        at = slice(CH * g, CH * g + CH)
        whole = grad_ref[at]
        both = whole[:, :128] + pltpu.roll(whole, 256 - WIN, 1)[:, :128]
        mark = offset_ref[at, 0:128]
        for k, offset in enumerate(OFFSETS):
            here = (mark == offset) & (lane < WIN)
            totals[k] = totals[k] + jnp.where(here, both, 0.0)
        totals[9] = totals[9] + jnp.where(lane == 3 * WIN - 128, whole[:, 128:], 0.0)
    small = jnp.zeros((CH, 128), F32)
    for k in range(10):
        small = jnp.where(lane == k, jnp.sum(totals[k], axis=1, keepdims=True), small)
    small = jnp.concatenate([small, jnp.zeros((128 - CH, 128), F32)], axis=0).T[:16]
    bias = jnp.concatenate([bias_grad_ref[...], jnp.zeros((256 - D, 1), F32)], axis=0)
    bias = jnp.broadcast_to(bias, (256, 128)).T[:8]
    row = lax.broadcasted_iota(I32, (8, 128), 0)
    lane = lax.broadcasted_iota(I32, (8, 128), 1)
    tail = jnp.zeros((8, 128), F32)
    for k in range(10):
        at = CH * (k % 4)
        moved = small[k : k + 1] if at == 0 else pltpu.roll(small[k : k + 1], at, 1)
        here = (row == k // 4) & (lane >= at) & (lane < at + CH)
        tail = jnp.where(here, moved, tail)
    tail = jnp.where(row == 3, bias[0:1, :128], tail)
    tail = jnp.where(row == 4, bias[0:1, 128:], tail)

    flat_ref[REL_ROWS:, :] = jnp.zeros((DEVS * SHARE - REL_ROWS, 128), F32)
    flat_ref[SMALL_DEV * SHARE : SMALL_DEV * SHARE + 8, :] = tail
    blank = jnp.zeros((SHARE_ROWS - SHARE, 128), F32)
    for dev in range(DEVS):
        mine = flat_ref[dev * SHARE : dev * SHARE + SHARE, :]
        share_ref[dev] = jnp.concatenate([mine, blank], axis=0)


def backward(image, taps, spread, weight, dpre, offsets, rel_col, bias_grad):
    return pl.pallas_call(
        backward_kernel,
        out_shape=(
            jax.ShapeDtypeStruct((D, TRIPS), F32),
            jax.ShapeDtypeStruct((DEVS, SHARE_ROWS, 128), F32),
        ),
        scratch_shapes=[
            pltpu.VMEM((2 * D, TRIPS), F32),
            pltpu.VMEM((BAND, 256), F32),
            pltpu.VMEM((DEVS * SHARE, 128), F32),
        ],
        compiler_params=params(),
        cost_estimate=cost(8 * 256 * FEAT * TRIPS, 14 << 20),
        name="backward",
    )(image, taps, spread, weight, dpre, offsets, rel_col, bias_grad)


def slots_kernel(query_ref, part_ref, dhead_ref, head_ref, share_ref, out_ref):
    owner = as_column(head_ref[...])
    owner = jnp.concatenate([owner, owner], axis=1)
    q_high, q_low = split(query_ref[...] * (1.0 / CAND))
    dhead = jnp.concatenate([dhead_ref[...], jnp.zeros((DP - D, TRIPS), F32)], axis=0)
    left = jnp.concatenate([q_high, q_low, q_high, *split(dhead)], axis=1)

    def block(nb, carry):
        cols = pl.ds(pl.multiple_of(nb * 256, 256), 256)
        high = part_ref[0:TRIPS, cols]
        low = part_ref[TRIPS:, cols]
        lane = lax.broadcasted_iota(I32, (TRIPS, 256), 1) + nb * 256
        hot = jnp.where(lane == owner, 1.0, 0.0).astype(BF16)
        grad = dot(left, jnp.concatenate([high, high, low, hot, hot], axis=0))
        most = jnp.max(jnp.abs(grad), axis=0, keepdims=True)
        power = jnp.clip(jnp.ceil(jnp.log2(jnp.maximum(most, 1e-30))), -90.0, 90.0)
        fixed = jnp.floor(grad * (jnp.exp2(15.0 - power) * FILL) + 0.5)
        row = lax.broadcasted_iota(I32, (DP, 256), 0)
        fixed = jnp.where(row == D, power, fixed)
        for half in range(2):
            pair = to_messages(fixed[:, 128 * half : 128 * half + 128])
            for k in range(2):
                dev = 4 * nb + 2 * half + k
                whole = jnp.concatenate([pair[k], code_share(share_ref[dev])], axis=0)
                out_ref[dev] = whole.astype(I32).astype(jnp.int16)
        return carry

    lax.fori_loop(0, ALL_SLOTS // 256, block, 0, unroll=8)


def slot_grads(query, part, dhead, head_col, shares):
    return pl.pallas_call(
        slots_kernel,
        out_shape=jax.ShapeDtypeStruct((DEVS, MSG_ROWS, 128), jnp.int16),
        compiler_params=params(),
        cost_estimate=cost(2 * DP * 640 * ALL_SLOTS, 8 << 20),
        name="slot_grads",
    )(query, part, dhead, head_col, shares)


def update_kernel(
    want_ref, msg_ref, table_ref, accum_ref, table_out, accum_out, part_ref, column_ref
):
    nb = pl.program_id(0)

    @pl.when(nb == 0)
    def _():
        def unpack(pair, carry):
            cols = pl.ds(pl.multiple_of(pair * 128, 128), 128)
            fixed = from_messages(
                msg_ref[2 * pair].astype(I32).astype(F32)[:HALF],
                msg_ref[2 * pair + 1].astype(I32).astype(F32)[:HALF],
            )
            grad = fixed * (jnp.exp2(fixed[D : D + 1] - 15.0) * (1.0 / FILL))
            high, low = split(grad)
            part_ref[0:DP, cols] = high
            part_ref[DP:, cols] = low
            column_ref[cols, :] = as_column(want_ref[:, cols])
            return carry

        lax.fori_loop(0, DEVS // 2, unpack, 0, unroll=4)

    def block(kb, total):
        slots = pl.ds(pl.multiple_of(kb * 2048, 2048), 2048)
        lane = lax.broadcasted_iota(I32, (2048, 128), 1) + nb * 256
        column = column_ref[slots, :]
        hot = jnp.concatenate(
            [
                jnp.where(column == lane, 1.0, 0.0).astype(BF16),
                jnp.where(column == lane + 128, 1.0, 0.0).astype(BF16),
            ],
            axis=1,
        )
        return total + dot(part_ref[:, slots], hot)

    total = lax.fori_loop(0, ALL_SLOTS // 2048, block, jnp.zeros((2 * DP, 256), F32), unroll=True)
    grad = total[:D] + total[DP : DP + D]
    accum = accum_ref[...] + grad * grad
    accum_out[...] = accum
    table_out[...] = table_ref[...] - LEARN * grad / (jnp.sqrt(accum) + EPS)


def update(want, msgs, table_t, accum_t):
    rows = pl.BlockSpec((D, 256), lambda i: (0, i))
    return pl.pallas_call(
        update_kernel,
        grid=(OWNED // 256,),
        in_specs=[
            pl.BlockSpec((1, ALL_SLOTS), lambda i: (0, 0)),
            pl.BlockSpec((DEVS, MSG_ROWS, 128), lambda i: (0, 0, 0)),
            rows,
            rows,
        ],
        out_specs=(rows, rows),
        out_shape=(
            jax.ShapeDtypeStruct((D, OWNED), F32),
            jax.ShapeDtypeStruct((D, OWNED), F32),
        ),
        scratch_shapes=[
            pltpu.VMEM((2 * DP, ALL_SLOTS), BF16),
            pltpu.VMEM((ALL_SLOTS, 128), I32),
        ],
        compiler_params=params(),
        cost_estimate=cost(4 * DP * OWNED * ALL_SLOTS, 10 << 20),
        name="update",
    )(want, msgs, table_t, accum_t)


def share_kernel(msg_ref, out_ref):
    def one(dev, total):
        coded = msg_ref[dev].astype(I32).astype(F32)
        return total + decode_share(coded[32 - SHARE_ROWS :])

    total = lax.fori_loop(0, DEVS, one, jnp.zeros((SHARE_ROWS, 128), F32), unroll=4)
    coded = code_share(total).astype(I32).astype(jnp.int16)
    for dev in range(DEVS):
        out_ref[dev] = coded


def sum_shares(msgs):
    return pl.pallas_call(
        share_kernel,
        grid=(1,),
        in_specs=[pl.BlockSpec((DEVS, 32, 128), lambda i: (0, MSG_ROWS // 32 - 1, 0))],
        out_specs=pl.BlockSpec((DEVS, SHARE_ROWS, 128), lambda i: (0, 0, 0)),
        out_shape=jax.ShapeDtypeStruct((DEVS, SHARE_ROWS, 128), jnp.int16),
        compiler_params=params(),
        cost_estimate=cost(1 << 20, 2 << 20),
        name="sum_shares",
    )(msgs)


def spread_kernel(sum_ref, rel_ref, kernel_ref, conv_ref, fc_ref, flat_ref):
    for dev in range(DEVS):
        value = decode_share(sum_ref[dev].astype(I32).astype(F32))
        flat_ref[dev * SHARE : dev * SHARE + SHARE, :] = value[:SHARE]
    for i in range(D // 8):
        for j in range(11):
            tile = flat_ref[8 * (11 * i + j) : 8 * (11 * i + j) + 8, :]
            last = min(128, NREL - 128 * j)
            rel_ref[8 * i : 8 * i + 8, 128 * j : 128 * j + last] = tile[:, :last]
    small = flat_ref[SMALL_DEV * SHARE : SMALL_DEV * SHARE + 8, :]
    for k in range(10):
        at = CH * (k % 4)
        row = small[k // 4 : k // 4 + 1]
        row = (row if at == 0 else pltpu.roll(row, 128 - at, 1))[:, :CH]
        if k < 9:
            kernel_ref[k : k + 1, :] = row
        else:
            conv_ref[...] = row
    fc_ref[...] = jnp.concatenate([small[3:4], small[4:5]], axis=1)[:, :D]


def spread_sums(sums):
    return pl.pallas_call(
        spread_kernel,
        out_shape=(
            jax.ShapeDtypeStruct((D, NREL), F32),
            jax.ShapeDtypeStruct((9, CH), F32),
            jax.ShapeDtypeStruct((1, CH), F32),
            jax.ShapeDtypeStruct((1, D), F32),
        ),
        scratch_shapes=[pltpu.VMEM((DEVS * SHARE, 128), F32)],
        compiler_params=params(),
        cost_estimate=cost(1 << 20, 2 << 20),
        name="spread_sums",
    )(sums)


def transpose_kernel(weight_ref, out_ref):
    wide = jnp.concatenate(
        [weight_ref[...].astype(F32), jnp.zeros((256 - D, BAND), F32)], axis=0
    ).T
    out_ref[...] = wide[:, :D].astype(BF16)


def transpose_weight(weight_t):
    return pl.pallas_call(
        transpose_kernel,
        grid=(BANDS,),
        in_specs=[pl.BlockSpec((D, BAND), lambda i: (0, i))],
        out_specs=pl.BlockSpec((BAND, D), lambda i: (i, 0)),
        out_shape=jax.ShapeDtypeStruct((FEAT, D), BF16),
        compiler_params=params(),
        cost_estimate=cost(1 << 20, 9 << 20),
        name="transpose_weight",
    )(weight_t)


def relations_kernel(ids_ref, rel_ref, out_ref):
    rel = rel_ref[...]
    high = rel.astype(BF16).astype(F32)
    both = jnp.concatenate([high, rel - high], axis=0).astype(BF16)
    for e in range(0, N_EMB, 2):
        cols = slice(128 * e, 128 * e + 256)
        row = lax.broadcasted_iota(I32, (RELP, 256), 0)
        hot = jnp.where(row == ids_ref[:, cols], 1.0, 0.0).astype(BF16)
        out_ref[:, cols] = dot(both, hot).astype(BF16)


def group_relations(ids, relations_t):
    return pl.pallas_call(
        relations_kernel,
        out_shape=jax.ShapeDtypeStruct((2 * D, N_EMB * TRIPS), BF16),
        compiler_params=params(),
        cost_estimate=cost(4 * D * RELP * N_EMB * TRIPS, 3 << 20),
        name="group_relations",
    )(ids, relations_t)


def projection_kernel(start_ref, group_ref, rel_ref, taps_ref, out_ref, high_ref, low_ref):
    start = pl.multiple_of(start_ref[0] * STEP, 8)
    blank = jnp.zeros((24, 256), F32)
    total = jnp.zeros((CHUNK, DP), F32)
    for e in range(0, N_EMB, 2):
        cols = slice(128 * e, 128 * e + 256)
        group = jnp.concatenate([group_ref[e], group_ref[e + 1]], axis=1)
        head = group[:DP].astype(F32)
        rel = rel_ref[:, cols].astype(F32)
        high_ref[...] = jnp.concatenate([head[:D], rel[:D], blank], axis=0)
        low_ref[...] = jnp.concatenate([jnp.zeros((D, 256), F32), rel[D:], blank], axis=0)
        high = high_ref[pl.ds(start, CHUNK_WIN), :]
        low = low_ref[pl.ds(start, CHUNK_WIN), :]
        rest = (128 - CHUNK_WIN, 256)
        ones, none = jnp.ones(rest, F32), jnp.zeros(rest, F32)
        stack = jnp.concatenate([high, ones, low, none, high, none], axis=0).astype(BF16)
        conv = dot(taps_ref[...], stack)
        feat = (conv * sigmoid(conv)).astype(BF16)
        total = total + dot_nt(feat, group[DP:])
    for s in range(N_SCORE):
        out_ref[s] = total[OWN_FEAT * s : OWN_FEAT * s + OWN_FEAT, :D]


def projection(start, groups, rels, taps):
    vmem = pl.BlockSpec(memory_space=pltpu.VMEM)
    return pl.pallas_call(
        projection_kernel,
        in_specs=[pl.BlockSpec(memory_space=pltpu.SMEM), vmem, vmem, vmem],
        out_specs=vmem,
        out_shape=jax.ShapeDtypeStruct((N_SCORE, OWN_FEAT, D), F32),
        scratch_shapes=[pltpu.VMEM((2 * D + 24, 256), F32), pltpu.VMEM((2 * D + 24, 256), F32)],
        compiler_params=params(),
        cost_estimate=cost(2 * FEAT * TRIPS * 640, 4 << 20),
        name="projection",
    )(start, groups, rels, taps)


def exchange(x, axes):
    return lax.all_to_all(x, axes, split_axis=0, concat_axis=0, tiled=True)


def high_part(x):
    return x.astype(BF16).astype(F32)


def taps_kernel(place_ref, small_ref, offset_ref, taps_ref, spread_ref, chunk_ref, twice_ref, all_ref):
    columns = small_ref[...].T
    twice_ref[0:CH, :] = columns[:CH]
    twice_ref[CH : 2 * CH, :] = columns[:CH]
    columns = columns[:CH]

    def one_of(codes, columns):
        value = jnp.zeros(codes.shape, F32)
        for k, offset in enumerate(OFFSETS):
            value = jnp.where(codes == offset, columns[:, k : k + 1], value)
        return value

    def bias_parts(columns):
        bias = columns[:, 9:10]
        first = high_part(bias)
        second = high_part(bias - first)
        return first, second, bias - first - second

    for g in range(BAND // CH):
        at = slice(CH * g, CH * g + CH)
        codes = offset_ref[at]
        low = codes >= LOW - 1
        value = one_of(jnp.where(low, codes - LOW, codes), columns)
        value = jnp.where(low, value - high_part(value), value)
        for part, column in enumerate(bias_parts(columns)):
            value = jnp.where(codes == BIAS_MARK + part, column, value)
        all_ref[at, :] = value
    whole = all_ref[...]
    taps_ref[...] = whole.astype(BF16)
    high = whole[:, :128].T[:WIN]
    low = pltpu.roll(whole, 256 - 2 * WIN, 1)[:, :128].T[:WIN]
    spread_ref[...] = jnp.concatenate([high, low], axis=0).astype(BF16)

    first = place_ref[0] * CHUNK
    base = place_ref[1] * STEP
    columns = twice_ref[pl.ds(pl.multiple_of((place_ref[0] % 4) * 8, 8), CH), :]
    parts = bias_parts(columns)
    lane = lax.broadcasted_iota(I32, (CH, 128), 1)
    for g in range(CHUNK // CH + 1):
        size = min(CH, CHUNK - CH * g)
        feature = lax.broadcasted_iota(I32, (CH, 128), 0) + (first + CH * g)
        place = feature >> 5
        row = ((place.astype(F32) + 0.5) * (1.0 / OUT_W)).astype(I32)
        origin = row * IMG_W + (place - row * OUT_W) - base
        value = jnp.where(lane < CHUNK_WIN, one_of(lane - origin, columns), 0.0)
        high = high_part(value)
        biased = high
        for part in range(3):
            biased = jnp.where(lane == CHUNK_WIN + part, parts[part], biased)
        whole = jnp.concatenate([biased, high, value - high], axis=1).astype(BF16)
        chunk_ref[CH * g : CH * g + size, :] = whole[:size]


def build_taps(place, small, offsets):
    vmem = pl.BlockSpec(memory_space=pltpu.VMEM)
    return pl.pallas_call(
        taps_kernel,
        in_specs=[pl.BlockSpec(memory_space=pltpu.SMEM), vmem, vmem],
        out_specs=(vmem,) * 3,
        out_shape=(
            jax.ShapeDtypeStruct((BAND, 256), BF16),
            jax.ShapeDtypeStruct((2 * WIN, BAND), BF16),
            jax.ShapeDtypeStruct((CHUNK, 384), BF16),
        ),
        scratch_shapes=[pltpu.VMEM((2 * CH, 128), F32), pltpu.VMEM((BAND, 256), F32)],
        compiler_params=params(),
        cost_estimate=cost(1 << 20, 3 << 20),
        name="build_taps",
    )(place, small, offsets)


def shards(
    table,
    accum,
    request,
    head_slot,
    rel_ids,
    tail_slot,
    relations,
    kernel,
    conv_bias,
    fc_weight,
    fc_bias,
):
    table_t = table.T
    asked = jnp.concatenate(
        [
            request[0],
            jnp.zeros((DEVS, SLOTS), I32),
            jnp.broadcast_to(rel_ids[None], (DEVS, TRIPS)),
        ],
        axis=1,
    )
    asked = exchange(asked, AXES)
    want = asked[:, :SLOTS].reshape(1, ALL_SLOTS)
    group = asked[:, 128:].reshape(N_EMB, N_SCORE, TRIPS)
    group = lax.dynamic_index_in_dim(group, lax.axis_index("score"), 1, keepdims=False)
    outgoing = gather_rows(want, table_t)
    incoming = exchange(outgoing, AXES)

    tails = jnp.pad(tail_slot, ((0, 0), (0, 128 - CAND)), constant_values=-1)
    counts = count_tails(tails)
    hot = (jnp.arange(NREL, dtype=I32)[:, None] == rel_ids[None, :]).astype(F32)
    rel_t = jnp.dot(relations.T, hot, precision=lax.Precision.HIGHEST)
    emb = lax.axis_index("emb")
    start = emb * CHUNK // (OUT_W * CH) // 2
    small = jnp.concatenate([kernel, conv_bias[None]], axis=0)
    small = jnp.pad(small, ((0, 118), (0, 128 - CH)))
    offsets = jnp.asarray(offset_map())
    taps, spread, chunk_taps = build_taps(jnp.stack([emb, start]), small, offsets)
    weight = transpose_weight(fc_weight.T)
    rels = group_relations(
        group.reshape(1, N_EMB * TRIPS), jnp.pad(relations.T, ((0, 0), (0, RELP - NREL)))
    )
    true_row = tail_slot[:, :1].T
    head_row = head_slot[None, :]
    ready = (counts, rel_t, taps, spread, chunk_taps, weight, rels, true_row)
    incoming, ready = lax.optimization_barrier((incoming, ready))
    counts, rel_t, taps, spread, chunk_taps, weight, rels, true_row = ready

    rows_t, head = unpack_heads(incoming, head_row)
    image, pre = forward(head, rel_t, taps, fc_weight.T)
    part, send, dpre, bias_grad, query = score(
        rows_t, counts, true_row, pre, fc_bias[None, :], head
    )
    groups = exchange(send, "emb")
    dhead, shares = backward(
        image, taps, spread, weight, dpre, offsets, rel_ids[None, :], bias_grad
    )
    returned = exchange(slot_grads(query, part, dhead, head_row, shares), AXES)

    left = projection(start.reshape(1), groups, rels, chunk_taps)
    here = lax.axis_index("score")
    for bit in range(3):
        side = (here >> bit) & 1
        halves = left.reshape(-1, 2, OWN_FEAT, D)
        kept = lax.dynamic_index_in_dim(halves, side, 1, keepdims=False)
        sent = lax.dynamic_index_in_dim(halves, 1 - side, 1, keepdims=False)
        pairs = [(i, i ^ (1 << bit)) for i in range(N_SCORE)]
        left = kept + lax.ppermute(sent, "score", pairs)
    fc_grad = left[0]

    sums = exchange(sum_shares(returned), AXES)
    new_table, new_accum = update(want, returned, table_t, accum.T)
    rel_sum, kernel_sum, conv_sum, fc_sum = spread_sums(sums)
    return (
        new_table.T,
        new_accum.T,
        fc_grad,
        kernel_sum,
        conv_sum[0],
        fc_sum[0],
        rel_sum.T,
    )


def solution(mesh):
    rows = P(AXES, None)
    in_specs = (rows, rows, P(AXES, None, None), P(AXES), P(AXES), rows) + (P(),) * 5
    out_specs = (rows, rows, rows) + (P(),) * 4
    return jax.shard_map(shards, mesh=mesh, in_specs=in_specs, out_specs=out_specs, check_vma=False)
```

```python
import jax
import jax.numpy as jnp
import numpy as np
from jax import lax
from jax.experimental import pallas as pl
from jax.experimental.pallas import tpu as pltpu
from jax.sharding import PartitionSpec as P

AXES = ("emb", "score")
DEVS = 128
N_EMB = 16
N_SCORE = 8
SLOTS = 64
ALL_SLOTS = DEVS * SLOTS
OWNED = 2048
D = 200
DP = 208
HALF = DP // 2
TRIPS = 128
CAND = 65
IMG_W = 20
OUT_W = 18
CH = 32
FEAT = 10368
BAND = 1152
BANDS = 9
WIN = 80
STEP = 40
NREL = 1345
RELP = 1408
REL_ROWS = 200 * 11
SHARE = 18
SHARE_ROWS = 24
SMALL_DEV = 124
MSG_ROWS = HALF + SHARE_ROWS
CHUNK = FEAT // N_EMB
OWN_FEAT = FEAT // DEVS
CHUNK_WIN = 104
LEARN = 0.1
EPS = 1e-10
F32 = jnp.float32
BF16 = jnp.bfloat16
I32 = jnp.int32
NT = (((1,), (1,)), ((), ()))
FILL = 0.9999

OFFSETS = [20 * a + b for a in range(3) for b in range(3)]
BIAS_MARK = 500
LOW = 1000


def offset_map():
    feature = np.arange(BAND)
    place = feature // CH
    origin = (place // OUT_W) * IMG_W + place % OUT_W
    lane = np.arange(256)
    offset = lane[None, :] % WIN - origin[:, None]
    offset = np.where((offset >= 0) & (offset < 43), offset, -1)
    offset = np.where(lane[None, :] < 2 * WIN, offset, offset + LOW)
    for part in range(16):
        offset[:, 3 * WIN + part] = BIAS_MARK + part
    return offset.astype(np.int32)


def params(mib=40):
    return pltpu.CompilerParams(vmem_limit_bytes=mib << 20)


def cost(flops, moved):
    return pl.CostEstimate(flops=flops, bytes_accessed=moved, transcendentals=0)


def dot(a, b):
    return jnp.dot(a, b, preferred_element_type=F32)


def dot_nt(a, b):
    return lax.dot_general(a, b, NT, preferred_element_type=F32)


def split(x):
    high = x.astype(BF16)
    low = (x - high.astype(F32)).astype(BF16)
    return high, low


def sigmoid(value):
    return 0.5 * jnp.tanh(0.5 * value) + 0.5


def silu_slope(value):
    sig = sigmoid(value)
    return sig * (1.0 + value * (1.0 - sig))


def as_column(row):
    return jnp.broadcast_to(row, (128, row.shape[1])).T


def to_messages(x):
    top, bottom = x[:HALF], x[HALF:]
    left = lax.broadcasted_iota(I32, (HALF, 128), 1) < SLOTS
    first = jnp.where(left, top, pltpu.roll(bottom, SLOTS, 1))
    second = jnp.where(left, pltpu.roll(top, SLOTS, 1), bottom)
    return first, second


def from_messages(first, second):
    left = lax.broadcasted_iota(I32, (HALF, 128), 1) < SLOTS
    top = jnp.where(left, first, pltpu.roll(second, SLOTS, 1))
    bottom = jnp.where(left, pltpu.roll(first, SLOTS, 1), second)
    return jnp.concatenate([top, bottom], axis=0)


def code_share(x):
    most = jnp.max(jnp.abs(x), axis=0, keepdims=True)
    power = jnp.clip(jnp.ceil(jnp.log2(jnp.maximum(most, 1e-30))), -90.0, 90.0)
    scaled = x * (jnp.exp2(15.0 - power) * FILL)
    fixed = jnp.floor(scaled + 0.5)
    rest = jnp.floor((scaled - fixed) * 16384.0 + 0.5)
    row = lax.broadcasted_iota(I32, (SHARE_ROWS, 128), 0)
    tail = jnp.where(row == SHARE, power, pltpu.roll(rest, SHARE + 1, 0))
    return jnp.where(row < SHARE, fixed, tail)


def decode_share(coded):
    row = lax.broadcasted_iota(I32, (SHARE_ROWS, 128), 0)
    rest = pltpu.roll(coded, SHARE_ROWS - SHARE - 1, 0) * (1.0 / 16384.0)
    first = SHARE_ROWS - SHARE - 1
    value = coded + jnp.where(row < first, rest, 0.0)
    return jnp.where(row < SHARE, value, 0.0) * (jnp.exp2(coded[SHARE : SHARE + 1] - 15.0) * (1.0 / FILL))


def gather_kernel(want_ref, table_ref, out_ref, rows_ref):
    @pl.when(pl.program_id(0) == 0)
    def _():
        rows_ref[...] = jnp.concatenate(
            [table_ref[...], jnp.zeros((DP - D, OWNED), F32)], axis=0
        ).astype(BF16)

    for q in range(8):
        want = want_ref[:, 256 * q : 256 * q + 256]
        total = jnp.zeros((DP, 256), F32)
        for kb in range(OWNED // 256):
            row = lax.broadcasted_iota(I32, (256, 256), 0) + 256 * kb
            hot = jnp.where(row == want, 1.0, 0.0).astype(BF16)
            total = total + dot(rows_ref[:, 256 * kb : 256 * kb + 256], hot)
        for half in range(2):
            first, second = to_messages(total[:, 128 * half : 128 * half + 128])
            out_ref[4 * q + 2 * half] = first.astype(BF16)
            out_ref[4 * q + 2 * half + 1] = second.astype(BF16)


def gather_rows(want, table_t):
    return pl.pallas_call(
        gather_kernel,
        grid=(4,),
        in_specs=[
            pl.BlockSpec((1, 2048), lambda i: (0, i)),
            pl.BlockSpec((D, OWNED), lambda i: (0, 0)),
        ],
        out_specs=pl.BlockSpec((32, HALF, 128), lambda i: (i, 0, 0)),
        out_shape=jax.ShapeDtypeStruct((DEVS, HALF, 128), BF16),
        scratch_shapes=[pltpu.VMEM((DP, OWNED), BF16)],
        compiler_params=params(),
        cost_estimate=cost(2 * DP * OWNED * ALL_SLOTS, 6 << 20),
        name="gather_rows",
    )(want, table_t)


def counts_kernel(tail_ref, out_ref, buf_ref):
    high_row = lax.broadcasted_iota(I32, (64, 128), 0)
    low_row = lax.broadcasted_iota(I32, (128, 128), 0)

    def one(t, carry):
        slot = tail_ref[pl.ds(t, 1), :]
        high = jnp.where(high_row == (slot >> 7), 1.0, 0.0).astype(BF16)
        low = jnp.where(low_row == (slot & 127), 1.0, 0.0).astype(BF16)
        buf_ref[pl.ds(pl.multiple_of(t * 64, 64), 64), :] = dot_nt(high, low)
        return carry

    lax.fori_loop(0, TRIPS, one, 0, unroll=8)
    for high in range(64):
        out_ref[:, 128 * high : 128 * high + 128] = buf_ref[
            pl.ds(high, TRIPS, stride=64), :
        ].astype(BF16)


def count_tails(tails):
    return pl.pallas_call(
        counts_kernel,
        out_shape=jax.ShapeDtypeStruct((TRIPS, ALL_SLOTS), BF16),
        scratch_shapes=[pltpu.VMEM((ALL_SLOTS, 128), F32)],
        compiler_params=params(),
        cost_estimate=cost(TRIPS * 2 * 64 * 128 * 128, 2 << 20),
        name="count_tails",
    )(tails)


def window_parts(image_ref, p):
    win = image_ref[pl.ds(pl.multiple_of(p * STEP, 8), WIN), :]
    high = win.astype(BF16).astype(F32)
    ones = jnp.ones((256 - 3 * WIN, TRIPS), F32)
    return high, win - high, ones


def front_kernel(
    msg_ref, head_ref, rel_ref, taps_ref, weight_ref, count_ref, true_ref, bias_ref,
    part_ref, send_ref, dpre_ref, bias_grad_ref, query_ref, image_ref,
    msgs, weights, counts, parts, rows_t, sems,
):
    def msg_copy(i):
        at = pl.ds(i * 32, 32)
        return pltpu.make_async_copy(msg_ref.at[at], msgs.at[at], sems.at[i])

    def part_copy(i):
        cols = pl.ds(pl.multiple_of(i * 2048, 2048), 2048)
        return pltpu.make_async_copy(parts.at[:, cols], part_ref.at[:, cols], sems.at[6 + i])

    weight_copy = pltpu.make_async_copy(weight_ref, weights, sems.at[4])
    count_copy = pltpu.make_async_copy(count_ref, counts, sems.at[5])
    for i in range(4):
        msg_copy(i).start()
    weight_copy.start()
    count_copy.start()

    def unpack(i, head):
        msg_copy(i).wait()
        for k in range(8):
            both = []
            for pair in (16 * i + 2 * k, 16 * i + 2 * k + 1):
                first = msgs[2 * pair].astype(F32)
                second = msgs[2 * pair + 1].astype(F32)
                both.append(from_messages(first, second))
            both = jnp.concatenate(both, axis=1).astype(BF16)
            base = pl.multiple_of(i * 2048 + k * 256, 256)
            rows_t[:, pl.ds(base, 256)] = both
            slot = lax.broadcasted_iota(I32, (256, TRIPS), 0) + base
            hot = jnp.where(slot == head_ref[...], 1.0, 0.0).astype(BF16)
            head = head + dot(both, hot)
        return head

    head = lax.fori_loop(0, 4, unpack, jnp.zeros((DP, TRIPS), F32))
    image_ref[0:D, :] = head[:D]
    image_ref[D : 2 * D, :] = rel_ref[...]

    weight_copy.wait()
    pre = jnp.zeros((D, TRIPS), F32)
    for p in range(BANDS):
        high, low, ones = window_parts(image_ref, p)
        stack = jnp.concatenate([high, low, high, ones], axis=0).astype(BF16)
        conv = dot(taps_ref[...], stack)
        feat = (conv * sigmoid(conv)).astype(BF16)
        pre = pre + dot(weights[:, p * BAND : p * BAND + BAND], feat)

    bias = jnp.concatenate([bias_ref[...], jnp.zeros((1, 256 - D), F32)], axis=1)
    pre = pre + as_column(bias)[:D]
    true = as_column(true_ref[...])
    true = jnp.concatenate([true, true], axis=1)
    query = pre * sigmoid(pre)
    pad = jnp.zeros((DP - D, TRIPS), F32)
    query = jnp.concatenate([query, pad], axis=0)
    query_ref[...] = query
    wide = jnp.concatenate([query, jnp.zeros((256 - DP, TRIPS), F32)], axis=0).T[:, :DP]
    high = wide.astype(BF16).astype(F32)
    both = jnp.concatenate([high, wide - high], axis=0).astype(BF16)
    count_copy.wait()

    def block(i, total):
        for k in range(8):
            base = pl.multiple_of(i * 2048 + k * 256, 256)
            cols = pl.ds(base, 256)
            rows = rows_t[:, cols]
            scores = dot(both, rows)
            scores = scores[:TRIPS] + scores[TRIPS:]
            lane = lax.broadcasted_iota(I32, (TRIPS, 256), 1) + base
            label = jnp.where(lane == true, 1.0, 0.0)
            grad = counts[:, cols].astype(F32) * sigmoid(scores) - label
            part = jnp.concatenate(split(grad), axis=0)
            parts[:, cols] = part
            total = total + dot_nt(rows, part)
        part_copy(i).start()
        return total

    total = lax.fori_loop(0, 4, block, jnp.zeros((DP, 256), F32))
    dquery = (total[:D, :TRIPS] + total[:D, TRIPS:]) * (1.0 / CAND)
    dpre = dquery * silu_slope(pre)
    bias_grad_ref[...] = jnp.sum(dpre, axis=1, keepdims=True)
    dpre_ref[...] = dpre.astype(BF16)
    dpre = jnp.concatenate([dpre, pad], axis=0).astype(BF16)
    own = head.astype(BF16)
    for e in range(N_EMB):
        send_ref[e, 0:DP] = own
        send_ref[e, DP:] = dpre
    for i in range(4):
        part_copy(i).wait()


def front(msgs, head_row, rel_t, taps, weight_t, counts, true_row, bias_row):
    vmem = pl.BlockSpec(memory_space=pltpu.VMEM)
    away = pl.BlockSpec(memory_space=pl.ANY)
    return pl.pallas_call(
        front_kernel,
        in_specs=[away, vmem, vmem, vmem, away, away, vmem, vmem],
        out_specs=(away,) + (vmem,) * 5,
        out_shape=(
            jax.ShapeDtypeStruct((2 * TRIPS, ALL_SLOTS), BF16),
            jax.ShapeDtypeStruct((N_EMB, 2 * DP, TRIPS), BF16),
            jax.ShapeDtypeStruct((D, TRIPS), BF16),
            jax.ShapeDtypeStruct((D, 1), F32),
            jax.ShapeDtypeStruct((DP, TRIPS), F32),
            jax.ShapeDtypeStruct((2 * D, TRIPS), F32),
        ),
        scratch_shapes=[
            pltpu.VMEM((DEVS, HALF, 128), BF16),
            pltpu.VMEM((D, FEAT), BF16),
            pltpu.VMEM((TRIPS, ALL_SLOTS), BF16),
            pltpu.VMEM((2 * TRIPS, ALL_SLOTS), BF16),
            pltpu.VMEM((DP, ALL_SLOTS), BF16),
            pltpu.SemaphoreType.DMA((10,)),
        ],
        compiler_params=params(),
        cost_estimate=cost(8 * 256 * DP * ALL_SLOTS, 20 << 20),
        name="front",
    )(msgs, head_row, rel_t, taps, weight_t, counts, true_row, bias_row)


def backward_kernel(
    image_ref,
    taps_ref,
    spread_ref,
    weight_ref,
    dpre_ref,
    offset_ref,
    rel_ref,
    bias_grad_ref,
    dhead_ref,
    share_ref,
    dimage_ref,
    grad_ref,
    flat_ref,
    weights,
    sems,
):
    def weight_copy(i):
        at = pl.ds(pl.multiple_of(i * 3 * BAND, BAND), 3 * BAND)
        return pltpu.make_async_copy(weight_ref.at[at], weights.at[at], sems.at[i])

    for i in range(3):
        weight_copy(i).start()
    dimage_ref[...] = jnp.zeros_like(dimage_ref)
    grad_ref[...] = jnp.zeros_like(grad_ref)

    def bands(i, carry):
        weight_copy(i).wait()
        for k in range(3):
            p = 3 * i + k
            high, low, ones = window_parts(image_ref, p)
            stack = jnp.concatenate([high, low, high, ones], axis=0).astype(BF16)
            none = jnp.zeros_like(low)
            stack_high = jnp.concatenate([high, none, high, ones], axis=0).astype(BF16)
            conv = dot(taps_ref[...], stack)
            weight = weights[pl.ds(pl.multiple_of(p * BAND, BAND), BAND), :]
            dfeat = dot(weight, dpre_ref[...])
            dconv = jnp.concatenate(split(dfeat * silu_slope(conv)), axis=1)
            grad_ref[...] += dot_nt(dconv, jnp.concatenate([stack, stack_high], axis=1))
            spread = dot(spread_ref[...], dconv)
            spread = spread[:WIN] + spread[WIN:]
            spread = spread[:, :TRIPS] + spread[:, TRIPS:]
            dimage_ref[pl.ds(pl.multiple_of(p * STEP, 8), WIN), :] += spread
        return carry

    lax.fori_loop(0, 3, bands, 0)
    dhead_ref[...] = dimage_ref[0:D, :]

    drel = dimage_ref[D : 2 * D, :]
    high = drel.astype(BF16).astype(F32)
    both = jnp.concatenate([high, drel - high], axis=0).astype(BF16)
    rel = as_column(rel_ref[...])
    for j in range(RELP // 128):
        lane = lax.broadcasted_iota(I32, (TRIPS, 128), 1) + 128 * j
        hot = jnp.where(lane == rel, 1.0, 0.0).astype(BF16)
        part = dot(both, hot)
        part = part[:D] + part[D:]
        for i in range(D // 8):
            tile = 11 * i + j
            flat_ref[8 * tile : 8 * tile + 8, :] = part[8 * i : 8 * i + 8]

    lane = lax.broadcasted_iota(I32, (CH, 128), 1)
    totals = [jnp.zeros((CH, 128), F32) for _ in range(10)]
    for g in range(BAND // CH):
        at = slice(CH * g, CH * g + CH)
        whole = grad_ref[at]
        both = whole[:, :128] + pltpu.roll(whole, 256 - WIN, 1)[:, :128]
        mark = offset_ref[at, 0:128]
        for k, offset in enumerate(OFFSETS):
            here = (mark == offset) & (lane < WIN)
            totals[k] = totals[k] + jnp.where(here, both, 0.0)
        totals[9] = totals[9] + jnp.where(lane == 3 * WIN - 128, whole[:, 128:], 0.0)
    small = jnp.zeros((CH, 128), F32)
    for k in range(10):
        small = jnp.where(lane == k, jnp.sum(totals[k], axis=1, keepdims=True), small)
    small = jnp.concatenate([small, jnp.zeros((128 - CH, 128), F32)], axis=0).T[:16]
    bias = jnp.concatenate([bias_grad_ref[...], jnp.zeros((256 - D, 1), F32)], axis=0)
    bias = jnp.broadcast_to(bias, (256, 128)).T[:8]
    row = lax.broadcasted_iota(I32, (8, 128), 0)
    lane = lax.broadcasted_iota(I32, (8, 128), 1)
    tail = jnp.zeros((8, 128), F32)
    for k in range(10):
        at = CH * (k % 4)
        moved = small[k : k + 1] if at == 0 else pltpu.roll(small[k : k + 1], at, 1)
        here = (row == k // 4) & (lane >= at) & (lane < at + CH)
        tail = jnp.where(here, moved, tail)
    tail = jnp.where(row == 3, bias[0:1, :128], tail)
    tail = jnp.where(row == 4, bias[0:1, 128:], tail)

    flat_ref[REL_ROWS:, :] = jnp.zeros((DEVS * SHARE - REL_ROWS, 128), F32)
    flat_ref[SMALL_DEV * SHARE : SMALL_DEV * SHARE + 8, :] = tail
    blank = jnp.zeros((SHARE_ROWS - SHARE, 128), F32)
    for dev in range(DEVS):
        mine = flat_ref[dev * SHARE : dev * SHARE + SHARE, :]
        share_ref[dev] = jnp.concatenate([mine, blank], axis=0)


def backward(image, taps, spread, weight, dpre, offsets, rel_col, bias_grad):
    vmem = pl.BlockSpec(memory_space=pltpu.VMEM)
    away = pl.BlockSpec(memory_space=pl.ANY)
    return pl.pallas_call(
        backward_kernel,
        in_specs=[vmem, vmem, vmem, away, vmem, vmem, vmem, vmem],
        out_specs=(vmem, vmem),
        out_shape=(
            jax.ShapeDtypeStruct((D, TRIPS), F32),
            jax.ShapeDtypeStruct((DEVS, SHARE_ROWS, 128), F32),
        ),
        scratch_shapes=[
            pltpu.VMEM((2 * D, TRIPS), F32),
            pltpu.VMEM((BAND, 256), F32),
            pltpu.VMEM((DEVS * SHARE, 128), F32),
            pltpu.VMEM((FEAT, D), BF16),
            pltpu.SemaphoreType.DMA((3,)),
        ],
        compiler_params=params(),
        cost_estimate=cost(8 * 256 * FEAT * TRIPS, 14 << 20),
        name="backward",
    )(image, taps, spread, weight, dpre, offsets, rel_col, bias_grad)


def slots_kernel(query_ref, part_ref, dhead_ref, head_ref, share_ref, out_ref):
    owner = as_column(head_ref[...])
    owner = jnp.concatenate([owner, owner], axis=1)
    q_high, q_low = split(query_ref[...] * (1.0 / CAND))
    dhead = jnp.concatenate([dhead_ref[...], jnp.zeros((DP - D, TRIPS), F32)], axis=0)
    left = jnp.concatenate([q_high, q_low, q_high, *split(dhead)], axis=1)

    def block(nb, carry):
        cols = pl.ds(pl.multiple_of(nb * 256, 256), 256)
        high = part_ref[0:TRIPS, cols]
        low = part_ref[TRIPS:, cols]
        lane = lax.broadcasted_iota(I32, (TRIPS, 256), 1) + nb * 256
        hot = jnp.where(lane == owner, 1.0, 0.0).astype(BF16)
        grad = dot(left, jnp.concatenate([high, high, low, hot, hot], axis=0))
        most = jnp.max(jnp.abs(grad), axis=0, keepdims=True)
        power = jnp.clip(jnp.ceil(jnp.log2(jnp.maximum(most, 1e-30))), -90.0, 90.0)
        fixed = jnp.floor(grad * (jnp.exp2(15.0 - power) * FILL) + 0.5)
        row = lax.broadcasted_iota(I32, (DP, 256), 0)
        fixed = jnp.where(row == D, power, fixed)
        for half in range(2):
            pair = to_messages(fixed[:, 128 * half : 128 * half + 128])
            for k in range(2):
                dev = 4 * nb + 2 * half + k
                whole = jnp.concatenate([pair[k], code_share(share_ref[dev])], axis=0)
                out_ref[dev] = whole.astype(I32).astype(jnp.int16)
        return carry

    lax.fori_loop(0, ALL_SLOTS // 256, block, 0, unroll=8)


def slot_grads(query, part, dhead, head_col, shares):
    return pl.pallas_call(
        slots_kernel,
        out_shape=jax.ShapeDtypeStruct((DEVS, MSG_ROWS, 128), jnp.int16),
        compiler_params=params(),
        cost_estimate=cost(2 * DP * 640 * ALL_SLOTS, 8 << 20),
        name="slot_grads",
    )(query, part, dhead, head_col, shares)


def update_kernel(
    want_ref, msg_ref, table_ref, accum_ref, table_out, accum_out, part_ref, column_ref
):
    nb = pl.program_id(0)

    @pl.when(nb == 0)
    def _():
        def unpack(pair, carry):
            cols = pl.ds(pl.multiple_of(pair * 128, 128), 128)
            fixed = from_messages(
                msg_ref[2 * pair].astype(I32).astype(F32)[:HALF],
                msg_ref[2 * pair + 1].astype(I32).astype(F32)[:HALF],
            )
            grad = fixed * (jnp.exp2(fixed[D : D + 1] - 15.0) * (1.0 / FILL))
            high = grad[:D].astype(BF16).astype(F32)
            both = jnp.concatenate([high, grad[:D] - high], axis=0)
            part_ref[:, cols] = both.astype(BF16)
            column_ref[cols, :] = as_column(want_ref[:, cols])
            return carry

        lax.fori_loop(0, DEVS // 2, unpack, 0, unroll=4)

    def block(kb, total):
        slots = pl.ds(pl.multiple_of(kb * 2048, 2048), 2048)
        lane = lax.broadcasted_iota(I32, (2048, 128), 1) + nb * 512
        column = column_ref[slots, :]
        hot = [jnp.where(column == lane + 128 * k, 1.0, 0.0).astype(BF16) for k in range(4)]
        hot = jnp.concatenate(hot, axis=1)
        return total + dot(part_ref[:, slots], hot)

    total = lax.fori_loop(0, ALL_SLOTS // 2048, block, jnp.zeros((2 * D, 512), F32), unroll=True)
    grad = total[:D] + total[D:]
    accum = accum_ref[...] + grad * grad
    accum_out[...] = accum
    table_out[...] = table_ref[...] - LEARN * grad / (jnp.sqrt(accum) + EPS)


def update(want, msgs, table_t, accum_t):
    rows = pl.BlockSpec((D, 512), lambda i: (0, i))
    return pl.pallas_call(
        update_kernel,
        grid=(OWNED // 512,),
        in_specs=[
            pl.BlockSpec((1, ALL_SLOTS), lambda i: (0, 0)),
            pl.BlockSpec((DEVS, MSG_ROWS, 128), lambda i: (0, 0, 0)),
            rows,
            rows,
        ],
        out_specs=(rows, rows),
        out_shape=(
            jax.ShapeDtypeStruct((D, OWNED), F32),
            jax.ShapeDtypeStruct((D, OWNED), F32),
        ),
        scratch_shapes=[
            pltpu.VMEM((2 * D, ALL_SLOTS), BF16),
            pltpu.VMEM((ALL_SLOTS, 128), I32),
        ],
        compiler_params=params(),
        cost_estimate=cost(4 * DP * OWNED * ALL_SLOTS, 10 << 20),
        name="update",
    )(want, msgs, table_t, accum_t)


def share_kernel(msg_ref, out_ref):
    def one(dev, total):
        coded = msg_ref[dev].astype(I32).astype(F32)
        return total + decode_share(coded[32 - SHARE_ROWS :])

    total = lax.fori_loop(0, DEVS, one, jnp.zeros((SHARE_ROWS, 128), F32), unroll=4)
    coded = code_share(total).astype(I32).astype(jnp.int16)
    for dev in range(DEVS):
        out_ref[dev] = coded


def sum_shares(msgs):
    return pl.pallas_call(
        share_kernel,
        grid=(1,),
        in_specs=[pl.BlockSpec((DEVS, 32, 128), lambda i: (0, MSG_ROWS // 32 - 1, 0))],
        out_specs=pl.BlockSpec((DEVS, SHARE_ROWS, 128), lambda i: (0, 0, 0)),
        out_shape=jax.ShapeDtypeStruct((DEVS, SHARE_ROWS, 128), jnp.int16),
        compiler_params=params(),
        cost_estimate=cost(1 << 20, 2 << 20),
        name="sum_shares",
    )(msgs)


def spread_kernel(sum_ref, rel_ref, kernel_ref, conv_ref, fc_ref, flat_ref):
    for dev in range(DEVS):
        value = decode_share(sum_ref[dev].astype(I32).astype(F32))
        flat_ref[dev * SHARE : dev * SHARE + SHARE, :] = value[:SHARE]
    for i in range(D // 8):
        for j in range(11):
            tile = flat_ref[8 * (11 * i + j) : 8 * (11 * i + j) + 8, :]
            last = min(128, NREL - 128 * j)
            rel_ref[8 * i : 8 * i + 8, 128 * j : 128 * j + last] = tile[:, :last]
    small = flat_ref[SMALL_DEV * SHARE : SMALL_DEV * SHARE + 8, :]
    for k in range(10):
        at = CH * (k % 4)
        row = small[k // 4 : k // 4 + 1]
        row = (row if at == 0 else pltpu.roll(row, 128 - at, 1))[:, :CH]
        if k < 9:
            kernel_ref[k : k + 1, :] = row
        else:
            conv_ref[...] = row
    fc_ref[...] = jnp.concatenate([small[3:4], small[4:5]], axis=1)[:, :D]


def spread_sums(sums):
    return pl.pallas_call(
        spread_kernel,
        out_shape=(
            jax.ShapeDtypeStruct((D, NREL), F32),
            jax.ShapeDtypeStruct((9, CH), F32),
            jax.ShapeDtypeStruct((1, CH), F32),
            jax.ShapeDtypeStruct((1, D), F32),
        ),
        scratch_shapes=[pltpu.VMEM((DEVS * SHARE, 128), F32)],
        compiler_params=params(),
        cost_estimate=cost(1 << 20, 2 << 20),
        name="spread_sums",
    )(sums)


def transpose_kernel(weight_ref, out_ref):
    wide = jnp.concatenate(
        [weight_ref[...].astype(F32), jnp.zeros((256 - D, BAND), F32)], axis=0
    ).T
    out_ref[...] = wide[:, :D].astype(BF16)


def transpose_weight(weight_t):
    return pl.pallas_call(
        transpose_kernel,
        grid=(BANDS,),
        in_specs=[pl.BlockSpec((D, BAND), lambda i: (0, i))],
        out_specs=pl.BlockSpec((BAND, D), lambda i: (i, 0)),
        out_shape=jax.ShapeDtypeStruct((FEAT, D), BF16),
        compiler_params=params(),
        cost_estimate=cost(1 << 20, 9 << 20),
        name="transpose_weight",
    )(weight_t)


def relations_kernel(ids_ref, rel_ref, out_ref):
    rel = rel_ref[...]
    high = rel.astype(BF16).astype(F32)
    both = jnp.concatenate([high, rel - high], axis=0).astype(BF16)
    for e in range(0, N_EMB, 2):
        cols = slice(128 * e, 128 * e + 256)
        row = lax.broadcasted_iota(I32, (RELP, 256), 0)
        hot = jnp.where(row == ids_ref[:, cols], 1.0, 0.0).astype(BF16)
        out_ref[:, cols] = dot(both, hot).astype(BF16)


def group_relations(ids, relations_t):
    return pl.pallas_call(
        relations_kernel,
        out_shape=jax.ShapeDtypeStruct((2 * D, N_EMB * TRIPS), BF16),
        compiler_params=params(),
        cost_estimate=cost(4 * D * RELP * N_EMB * TRIPS, 3 << 20),
        name="group_relations",
    )(ids, relations_t)


def projection_kernel(start_ref, group_ref, rel_ref, taps_ref, out_ref, high_ref, low_ref):
    start = pl.multiple_of(start_ref[0] * STEP, 8)
    blank = jnp.zeros((24, 256), F32)
    total = jnp.zeros((CHUNK, DP), F32)
    for e in range(0, N_EMB, 2):
        cols = slice(128 * e, 128 * e + 256)
        group = jnp.concatenate([group_ref[e], group_ref[e + 1]], axis=1)
        head = group[:DP].astype(F32)
        rel = rel_ref[:, cols].astype(F32)
        high_ref[...] = jnp.concatenate([head[:D], rel[:D], blank], axis=0)
        low_ref[...] = jnp.concatenate([jnp.zeros((D, 256), F32), rel[D:], blank], axis=0)
        high = high_ref[pl.ds(start, CHUNK_WIN), :]
        low = low_ref[pl.ds(start, CHUNK_WIN), :]
        rest = (128 - CHUNK_WIN, 256)
        ones, none = jnp.ones(rest, F32), jnp.zeros(rest, F32)
        stack = jnp.concatenate([high, ones, low, none, high, none], axis=0).astype(BF16)
        conv = dot(taps_ref[...], stack)
        feat = (conv * sigmoid(conv)).astype(BF16)
        total = total + dot_nt(feat, group[DP:])
    for s in range(N_SCORE):
        out_ref[s] = total[OWN_FEAT * s : OWN_FEAT * s + OWN_FEAT, :D]


def projection(start, groups, rels, taps):
    vmem = pl.BlockSpec(memory_space=pltpu.VMEM)
    return pl.pallas_call(
        projection_kernel,
        in_specs=[pl.BlockSpec(memory_space=pltpu.SMEM), vmem, vmem, vmem],
        out_specs=vmem,
        out_shape=jax.ShapeDtypeStruct((N_SCORE, OWN_FEAT, D), F32),
        scratch_shapes=[pltpu.VMEM((2 * D + 24, 256), F32), pltpu.VMEM((2 * D + 24, 256), F32)],
        compiler_params=params(),
        cost_estimate=cost(2 * FEAT * TRIPS * 640, 4 << 20),
        name="projection",
    )(start, groups, rels, taps)


def exchange(x, axes):
    return lax.all_to_all(x, axes, split_axis=0, concat_axis=0, tiled=True)


def high_part(x):
    return x.astype(BF16).astype(F32)


def taps_kernel(place_ref, small_ref, offset_ref, taps_ref, spread_ref, chunk_ref, twice_ref, all_ref):
    columns = small_ref[...].T
    twice_ref[0:CH, :] = columns[:CH]
    twice_ref[CH : 2 * CH, :] = columns[:CH]
    columns = columns[:CH]

    def one_of(codes, columns):
        value = jnp.zeros(codes.shape, F32)
        for k, offset in enumerate(OFFSETS):
            value = jnp.where(codes == offset, columns[:, k : k + 1], value)
        return value

    def bias_parts(columns):
        bias = columns[:, 9:10]
        first = high_part(bias)
        second = high_part(bias - first)
        return first, second, bias - first - second

    for g in range(BAND // CH):
        at = slice(CH * g, CH * g + CH)
        codes = offset_ref[at]
        low = codes >= LOW - 1
        value = one_of(jnp.where(low, codes - LOW, codes), columns)
        value = jnp.where(low, value - high_part(value), value)
        for part, column in enumerate(bias_parts(columns)):
            value = jnp.where(codes == BIAS_MARK + part, column, value)
        all_ref[at, :] = value
    whole = all_ref[...]
    taps_ref[...] = whole.astype(BF16)
    high = whole[:, :128].T[:WIN]
    low = pltpu.roll(whole, 256 - 2 * WIN, 1)[:, :128].T[:WIN]
    spread_ref[...] = jnp.concatenate([high, low], axis=0).astype(BF16)

    first = place_ref[0] * CHUNK
    base = place_ref[1] * STEP
    columns = twice_ref[pl.ds(pl.multiple_of((place_ref[0] % 4) * 8, 8), CH), :]
    parts = bias_parts(columns)
    lane = lax.broadcasted_iota(I32, (CH, 128), 1)
    for g in range(CHUNK // CH + 1):
        size = min(CH, CHUNK - CH * g)
        feature = lax.broadcasted_iota(I32, (CH, 128), 0) + (first + CH * g)
        place = feature >> 5
        row = ((place.astype(F32) + 0.5) * (1.0 / OUT_W)).astype(I32)
        origin = row * IMG_W + (place - row * OUT_W) - base
        value = jnp.where(lane < CHUNK_WIN, one_of(lane - origin, columns), 0.0)
        high = high_part(value)
        biased = high
        for part in range(3):
            biased = jnp.where(lane == CHUNK_WIN + part, parts[part], biased)
        whole = jnp.concatenate([biased, high, value - high], axis=1).astype(BF16)
        chunk_ref[CH * g : CH * g + size, :] = whole[:size]


def build_taps(place, small, offsets):
    vmem = pl.BlockSpec(memory_space=pltpu.VMEM)
    return pl.pallas_call(
        taps_kernel,
        in_specs=[pl.BlockSpec(memory_space=pltpu.SMEM), vmem, vmem],
        out_specs=(vmem,) * 3,
        out_shape=(
            jax.ShapeDtypeStruct((BAND, 256), BF16),
            jax.ShapeDtypeStruct((2 * WIN, BAND), BF16),
            jax.ShapeDtypeStruct((CHUNK, 384), BF16),
        ),
        scratch_shapes=[pltpu.VMEM((2 * CH, 128), F32), pltpu.VMEM((BAND, 256), F32)],
        compiler_params=params(),
        cost_estimate=cost(1 << 20, 3 << 20),
        name="build_taps",
    )(place, small, offsets)


def shards(
    table,
    accum,
    request,
    head_slot,
    rel_ids,
    tail_slot,
    relations,
    kernel,
    conv_bias,
    fc_weight,
    fc_bias,
):
    table_t = table.T
    asked = jnp.concatenate(
        [
            request[0],
            jnp.zeros((DEVS, SLOTS), I32),
            jnp.broadcast_to(rel_ids[None], (DEVS, TRIPS)),
        ],
        axis=1,
    )
    asked = exchange(asked, AXES)
    want = asked[:, :SLOTS].reshape(1, ALL_SLOTS)
    group = asked[:, 128:].reshape(N_EMB, N_SCORE, TRIPS)
    group = lax.dynamic_index_in_dim(group, lax.axis_index("score"), 1, keepdims=False)
    outgoing = gather_rows(want, table_t)
    incoming = exchange(outgoing, AXES)

    tails = jnp.pad(tail_slot, ((0, 0), (0, 128 - CAND)), constant_values=-1)
    counts = count_tails(tails)
    hot = (jnp.arange(NREL, dtype=I32)[:, None] == rel_ids[None, :]).astype(F32)
    rel_t = jnp.dot(relations.T, hot, precision=lax.Precision.HIGHEST)
    emb = lax.axis_index("emb")
    start = emb * CHUNK // (OUT_W * CH) // 2
    small = jnp.concatenate([kernel, conv_bias[None]], axis=0)
    small = jnp.pad(small, ((0, 118), (0, 128 - CH)))
    offsets = jnp.asarray(offset_map())
    taps, spread, chunk_taps = build_taps(jnp.stack([emb, start]), small, offsets)
    weight = transpose_weight(fc_weight.T)
    rels = group_relations(
        group.reshape(1, N_EMB * TRIPS), jnp.pad(relations.T, ((0, 0), (0, RELP - NREL)))
    )
    true_row = tail_slot[:, :1].T
    head_row = head_slot[None, :]
    ready = (counts, rel_t, taps, spread, chunk_taps, weight, rels, true_row)
    incoming, ready = lax.optimization_barrier((incoming, ready))
    counts, rel_t, taps, spread, chunk_taps, weight, rels, true_row = ready

    part, send, dpre, bias_grad, query, image = front(
        incoming, head_row, rel_t, taps, fc_weight.T, counts, true_row, fc_bias[None, :]
    )
    groups = exchange(send, "emb")
    dhead, shares = backward(
        image, taps, spread, weight, dpre, offsets, rel_ids[None, :], bias_grad
    )
    returned = exchange(slot_grads(query, part, dhead, head_row, shares), AXES)

    halves = projection(start.reshape(1), groups, rels, chunk_taps)
    halves = halves.reshape(N_SCORE // 2, 2, OWN_FEAT, D)
    here = lax.axis_index("score")
    side = here & 1
    kept = lax.dynamic_index_in_dim(halves, side, 1, keepdims=False)
    sent = lax.dynamic_index_in_dim(halves, 1 - side, 1, keepdims=False)
    left = kept + lax.ppermute(sent, "score", [(i, i ^ 1) for i in range(N_SCORE)])
    fc_grad = lax.dynamic_index_in_dim(left, here >> 1, 0, keepdims=False)
    for step in range(1, 4):
        sent = lax.dynamic_index_in_dim(left, (here >> 1) ^ step, 0, keepdims=False)
        pairs = [(i, i ^ (2 * step)) for i in range(N_SCORE)]
        fc_grad = fc_grad + lax.ppermute(sent, "score", pairs)

    sums = exchange(sum_shares(returned), AXES)
    new_table, new_accum = update(want, returned, table_t, accum.T)
    rel_sum, kernel_sum, conv_sum, fc_sum = spread_sums(sums)
    return (
        new_table.T,
        new_accum.T,
        fc_grad,
        kernel_sum,
        conv_sum[0],
        fc_sum[0],
        rel_sum.T,
    )


def solution(mesh):
    rows = P(AXES, None)
    in_specs = (rows, rows, P(AXES, None, None), P(AXES), P(AXES), rows) + (P(),) * 5
    out_specs = (rows, rows, rows) + (P(),) * 4
    return jax.shard_map(shards, mesh=mesh, in_specs=in_specs, out_specs=out_specs, check_vma=False)
```

```python
import jax
import jax.numpy as jnp
import numpy as np
from jax import lax
from jax.experimental import pallas as pl
from jax.experimental.pallas import tpu as pltpu
from jax.sharding import PartitionSpec as P

AXES = ("emb", "score")
DEVS = 128
N_EMB = 16
N_SCORE = 8
SLOTS = 64
ALL_SLOTS = DEVS * SLOTS
OWNED = 2048
D = 200
DP = 208
HALF = DP // 2
TRIPS = 128
CAND = 65
IMG_W = 20
OUT_W = 18
CH = 32
FEAT = 10368
BAND = 1152
BANDS = 9
WIN = 80
STEP = 40
NREL = 1345
RELP = 1408
REL_ROWS = 200 * 11
SHARE = 18
SHARE_ROWS = 24
SMALL_DEV = 124
MSG_ROWS = HALF + SHARE_ROWS
CHUNK = FEAT // N_EMB
OWN_FEAT = FEAT // DEVS
CHUNK_WIN = 104
LEARN = 0.1
EPS = 1e-10
F32 = jnp.float32
BF16 = jnp.bfloat16
I32 = jnp.int32
NT = (((1,), (1,)), ((), ()))
FILL = 0.9999

OFFSETS = [20 * a + b for a in range(3) for b in range(3)]
BIAS_MARK = 500
LOW = 1000


def offset_map():
    feature = np.arange(BAND)
    place = feature // CH
    origin = (place // OUT_W) * IMG_W + place % OUT_W
    lane = np.arange(256)
    offset = lane[None, :] % WIN - origin[:, None]
    offset = np.where((offset >= 0) & (offset < 43), offset, -1)
    offset = np.where(lane[None, :] < 2 * WIN, offset, offset + LOW)
    for part in range(16):
        offset[:, 3 * WIN + part] = BIAS_MARK + part
    return offset.astype(np.int32)


def params(mib=40):
    return pltpu.CompilerParams(vmem_limit_bytes=mib << 20)


VMEM_SPEC = pl.BlockSpec()
HBM_SPEC = pl.BlockSpec(memory_space=pltpu.HBM)
ANY_SPEC = pl.BlockSpec(memory_space=pl.ANY)
AT_QUERY = 2 * D
AT_BIAS = AT_QUERY + DP
AT_DPRE = AT_BIAS + 16
STATE = AT_DPRE + D


def cost(flops, moved):
    return pl.CostEstimate(flops=flops, bytes_accessed=moved, transcendentals=0)


def dot(a, b):
    return jnp.dot(a, b, preferred_element_type=F32)


def dot_nt(a, b):
    return lax.dot_general(a, b, NT, preferred_element_type=F32)


def split(x):
    high = x.astype(BF16)
    low = (x - high.astype(F32)).astype(BF16)
    return high, low


def sigmoid(value):
    return 0.5 * jnp.tanh(0.5 * value) + 0.5


def silu_slope(value):
    sig = sigmoid(value)
    return sig * (1.0 + value * (1.0 - sig))


def as_column(row):
    return jnp.broadcast_to(row, (128, row.shape[1])).T


def to_messages(x):
    top, bottom = x[:HALF], x[HALF:]
    left = lax.broadcasted_iota(I32, (HALF, 128), 1) < SLOTS
    first = jnp.where(left, top, pltpu.roll(bottom, SLOTS, 1))
    second = jnp.where(left, pltpu.roll(top, SLOTS, 1), bottom)
    return first, second


def from_messages(first, second):
    left = lax.broadcasted_iota(I32, (HALF, 128), 1) < SLOTS
    top = jnp.where(left, first, pltpu.roll(second, SLOTS, 1))
    bottom = jnp.where(left, pltpu.roll(first, SLOTS, 1), second)
    return jnp.concatenate([top, bottom], axis=0)


def code_share(x):
    most = jnp.max(jnp.abs(x), axis=0, keepdims=True)
    power = jnp.clip(jnp.ceil(jnp.log2(jnp.maximum(most, 1e-30))), -90.0, 90.0)
    scaled = x * (jnp.exp2(15.0 - power) * FILL)
    fixed = jnp.floor(scaled + 0.5)
    rest = jnp.floor((scaled - fixed) * 16384.0 + 0.5)
    row = lax.broadcasted_iota(I32, (SHARE_ROWS, 128), 0)
    tail = jnp.where(row == SHARE, power, pltpu.roll(rest, SHARE + 1, 0))
    return jnp.where(row < SHARE, fixed, tail)


def decode_share(coded):
    row = lax.broadcasted_iota(I32, (SHARE_ROWS, 128), 0)
    rest = pltpu.roll(coded, SHARE_ROWS - SHARE - 1, 0) * (1.0 / 16384.0)
    first = SHARE_ROWS - SHARE - 1
    value = coded + jnp.where(row < first, rest, 0.0)
    return jnp.where(row < SHARE, value, 0.0) * (jnp.exp2(coded[SHARE : SHARE + 1] - 15.0) * (1.0 / FILL))


def gather_kernel(want_ref, table_ref, out_ref, table, rows, outs, sems):
    table_copy = pltpu.make_async_copy(table_ref, table, sems.at[4])
    table_copy.start()
    table_copy.wait()
    rows[...] = jnp.concatenate([table[...], jnp.zeros((DP - D, OWNED), F32)], axis=0).astype(BF16)

    def out_copy(i):
        at = pl.ds(i * 32, 32)
        return pltpu.make_async_copy(outs.at[at], out_ref.at[at], sems.at[i])

    def block(i, carry):
        for q in range(8):
            want = want_ref[:, pl.ds(pl.multiple_of(i * 2048 + 256 * q, 256), 256)]
            total = jnp.zeros((DP, 256), F32)
            for kb in range(OWNED // 256):
                row = lax.broadcasted_iota(I32, (256, 256), 0) + 256 * kb
                hot = jnp.where(row == want, 1.0, 0.0).astype(BF16)
                total = total + dot(rows[:, 256 * kb : 256 * kb + 256], hot)
            for half in range(2):
                first, second = to_messages(total[:, 128 * half : 128 * half + 128])
                outs[32 * i + 4 * q + 2 * half] = first.astype(BF16)
                outs[32 * i + 4 * q + 2 * half + 1] = second.astype(BF16)
        out_copy(i).start()
        return carry

    lax.fori_loop(0, 4, block, 0)
    for i in range(4):
        out_copy(i).wait()


def gather_rows(want, table_t):
    return pl.pallas_call(
        gather_kernel,
        in_specs=[VMEM_SPEC, HBM_SPEC],
        out_specs=HBM_SPEC,
        out_shape=jax.ShapeDtypeStruct((DEVS, HALF, 128), BF16),
        scratch_shapes=[
            pltpu.VMEM((D, OWNED), F32),
            pltpu.VMEM((DP, OWNED), BF16),
            pltpu.VMEM((DEVS, HALF, 128), BF16),
            pltpu.SemaphoreType.DMA((5,)),
        ],
        compiler_params=params(),
        cost_estimate=cost(2 * DP * OWNED * ALL_SLOTS, 6 << 20),
        name="gather_rows",
    )(want, table_t)


def counts_kernel(tail_ref, out_ref, buf_ref):
    high_row = lax.broadcasted_iota(I32, (64, 128), 0)
    low_row = lax.broadcasted_iota(I32, (128, 128), 0)

    def one(t, carry):
        slot = tail_ref[pl.ds(t, 1), :]
        high = jnp.where(high_row == (slot >> 7), 1.0, 0.0).astype(BF16)
        low = jnp.where(low_row == (slot & 127), 1.0, 0.0).astype(BF16)
        buf_ref[pl.ds(pl.multiple_of(t * 64, 64), 64), :] = dot_nt(high, low)
        return carry

    lax.fori_loop(0, TRIPS, one, 0, unroll=8)
    for high in range(64):
        out_ref[:, 128 * high : 128 * high + 128] = buf_ref[
            pl.ds(high, TRIPS, stride=64), :
        ].astype(BF16)


def count_tails(tails):
    return pl.pallas_call(
        counts_kernel,
        out_shape=jax.ShapeDtypeStruct((TRIPS, ALL_SLOTS), BF16),
        scratch_shapes=[pltpu.VMEM((ALL_SLOTS, 128), F32)],
        compiler_params=params(),
        cost_estimate=cost(TRIPS * 2 * 64 * 128 * 128, 2 << 20),
        name="count_tails",
    )(tails)


def window_parts(image_ref, p):
    win = image_ref[pl.ds(pl.multiple_of(p * STEP, 8), WIN), :]
    high = win.astype(BF16).astype(F32)
    ones = jnp.ones((256 - 3 * WIN, TRIPS), F32)
    return high, win - high, ones


def front_kernel(
    msg_ref, head_ref, rel_ref, taps_ref, weight_ref, count_ref, true_ref, bias_ref,
    part_ref, send_ref, state_ref,
    msgs, heads, taps, weights, counts, trues, biases, parts, rows_t, own, state, sems,
):
    def msg_copy(i):
        at = pl.ds(i * 32, 32)
        return pltpu.make_async_copy(msg_ref.at[at], msgs.at[at], sems.at[i])

    def part_copy(i):
        cols = pl.ds(pl.multiple_of(i * 2048, 2048), 2048)
        return pltpu.make_async_copy(parts.at[:, cols], part_ref.at[:, cols], sems.at[4 + i])

    rel_at = state.at[pl.ds(D, D)]
    pairs = [(head_ref, heads), (rel_ref, rel_at), (taps_ref, taps), (weight_ref, weights)]
    pairs += [(bias_ref, biases), (true_ref, trues), (count_ref, counts)]
    loads = [pltpu.make_async_copy(a, b, sems.at[8 + k]) for k, (a, b) in enumerate(pairs)]
    loads[0].start()
    for i in range(4):
        msg_copy(i).start()
    for load in loads[1:]:
        load.start()
    loads[0].wait()

    def unpack(i, head):
        msg_copy(i).wait()
        for k in range(8):
            both = []
            for pair in (16 * i + 2 * k, 16 * i + 2 * k + 1):
                first = msgs[2 * pair].astype(F32)
                second = msgs[2 * pair + 1].astype(F32)
                both.append(from_messages(first, second))
            both = jnp.concatenate(both, axis=1).astype(BF16)
            base = pl.multiple_of(i * 2048 + k * 256, 256)
            rows_t[:, pl.ds(base, 256)] = both
            slot = lax.broadcasted_iota(I32, (256, TRIPS), 0) + base
            hot = jnp.where(slot == heads[...], 1.0, 0.0).astype(BF16)
            head = head + dot(both, hot)
        return head

    head = lax.fori_loop(0, 4, unpack, jnp.zeros((DP, TRIPS), F32))
    state[0:D, :] = head[:D]

    for load in loads[1:4]:
        load.wait()
    pre = jnp.zeros((D, TRIPS), F32)
    for p in range(BANDS):
        high, low, ones = window_parts(state, p)
        stack = jnp.concatenate([high, low, high, ones], axis=0).astype(BF16)
        conv = dot(taps[...], stack)
        feat = (conv * sigmoid(conv)).astype(BF16)
        pre = pre + dot(weights[:, p * BAND : p * BAND + BAND], feat)

    for load in loads[4:]:
        load.wait()
    bias = jnp.concatenate([biases[...], jnp.zeros((1, 256 - D), F32)], axis=1)
    pre = pre + as_column(bias)[:D]
    true = as_column(trues[...])
    true = jnp.concatenate([true, true], axis=1)
    query = pre * sigmoid(pre)
    pad = jnp.zeros((DP - D, TRIPS), F32)
    query = jnp.concatenate([query, pad], axis=0)
    state[AT_QUERY:AT_BIAS, :] = query
    wide = jnp.concatenate([query, jnp.zeros((256 - DP, TRIPS), F32)], axis=0).T[:, :DP]
    high = wide.astype(BF16).astype(F32)
    both = jnp.concatenate([high, wide - high], axis=0).astype(BF16)

    def block(i, total):
        for k in range(8):
            base = pl.multiple_of(i * 2048 + k * 256, 256)
            cols = pl.ds(base, 256)
            rows = rows_t[:, cols]
            scores = dot(both, rows)
            scores = scores[:TRIPS] + scores[TRIPS:]
            lane = lax.broadcasted_iota(I32, (TRIPS, 256), 1) + base
            label = jnp.where(lane == true, 1.0, 0.0)
            grad = counts[:, cols].astype(F32) * sigmoid(scores) - label
            part = jnp.concatenate(split(grad), axis=0)
            parts[:, cols] = part
            total = total + dot_nt(rows, part)
        part_copy(i).start()
        return total

    total = lax.fori_loop(0, 4, block, jnp.zeros((DP, 256), F32))
    dquery = (total[:D, :TRIPS] + total[:D, TRIPS:]) * (1.0 / CAND)
    dpre = dquery * silu_slope(pre)
    total = jnp.concatenate(
        [jnp.sum(dpre, axis=1, keepdims=True), jnp.zeros((256 - D, 1), F32)], axis=0
    )
    total = jnp.broadcast_to(total, (256, 128)).T[:8]
    state[AT_BIAS:AT_DPRE, :] = jnp.concatenate([total[:, :128], total[:, 128:]], axis=0)
    state[AT_DPRE:, :] = dpre
    own[...] = jnp.concatenate([head, dpre, pad], axis=0).astype(BF16)
    sends = [pltpu.make_async_copy(own, send_ref.at[e], sems.at[15 + e]) for e in range(N_EMB)]
    sends.append(pltpu.make_async_copy(state, state_ref, sems.at[15 + N_EMB]))
    for send in sends:
        send.start()
    for send in sends:
        send.wait()
    for i in range(4):
        part_copy(i).wait()


def front(msgs, head_row, rel_t, taps, weight_t, counts, true_row, bias_row):
    return pl.pallas_call(
        front_kernel,
        in_specs=[ANY_SPEC] + [HBM_SPEC] * 7,
        out_specs=(HBM_SPEC,) * 3,
        out_shape=(
            jax.ShapeDtypeStruct((2 * TRIPS, ALL_SLOTS), BF16),
            jax.ShapeDtypeStruct((N_EMB, 2 * DP, TRIPS), BF16),
            jax.ShapeDtypeStruct((STATE, TRIPS), F32),
        ),
        scratch_shapes=[
            pltpu.VMEM((DEVS, HALF, 128), BF16),
            pltpu.VMEM((1, TRIPS), I32),
            pltpu.VMEM((BAND, 256), BF16),
            pltpu.VMEM((D, FEAT), BF16),
            pltpu.VMEM((TRIPS, ALL_SLOTS), BF16),
            pltpu.VMEM((1, TRIPS), I32),
            pltpu.VMEM((1, D), F32),
            pltpu.VMEM((2 * TRIPS, ALL_SLOTS), BF16),
            pltpu.VMEM((DP, ALL_SLOTS), BF16),
            pltpu.VMEM((2 * DP, TRIPS), BF16),
            pltpu.VMEM((STATE, TRIPS), F32),
            pltpu.SemaphoreType.DMA((16 + N_EMB,)),
        ],
        compiler_params=params(),
        cost_estimate=cost(8 * 256 * DP * ALL_SLOTS, 20 << 20),
        name="front",
    )(msgs, head_row, rel_t, taps, weight_t, counts, true_row, bias_row)


def back_kernel(
    state_ref, taps_ref, spread_ref, weight_ref, offset_ref, part_ref, rel_ref, head_ref,
    out_ref,
    state, taps, spreads, weights, offsets, parts, outs, shares, dimage_ref, grad_ref, flat_ref,
    sems,
):
    def weight_copy(i):
        at = pl.ds(pl.multiple_of(i * 3 * BAND, BAND), 3 * BAND)
        return pltpu.make_async_copy(weight_ref.at[at], weights.at[at], sems.at[i])

    def out_copy(i):
        at = pl.ds(i * 32, 32)
        return pltpu.make_async_copy(outs.at[at], out_ref.at[at], sems.at[3 + i])

    pairs = [(state_ref, state), (taps_ref, taps), (spread_ref, spreads)]
    pairs += [(offset_ref, offsets), (part_ref, parts)]
    loads = [pltpu.make_async_copy(a, b, sems.at[7 + k]) for k, (a, b) in enumerate(pairs)]
    for load in loads[:2]:
        load.start()
    weight_copy(0).start()
    loads[2].start()
    for i in range(1, 3):
        weight_copy(i).start()
    for load in loads[3:]:
        load.start()
    for load in loads[:3]:
        load.wait()

    dimage_ref[...] = jnp.zeros_like(dimage_ref)
    grad_ref[...] = jnp.zeros_like(grad_ref)
    dpre = state[AT_DPRE:, :].astype(BF16)

    def bands(i, carry):
        weight_copy(i).wait()
        for k in range(3):
            p = 3 * i + k
            high, low, ones = window_parts(state, p)
            stack = jnp.concatenate([high, low, high, ones], axis=0).astype(BF16)
            none = jnp.zeros_like(low)
            stack_high = jnp.concatenate([high, none, high, ones], axis=0).astype(BF16)
            conv = dot(taps[...], stack)
            weight = weights[pl.ds(pl.multiple_of(p * BAND, BAND), BAND), :]
            dfeat = dot(weight, dpre)
            dconv = jnp.concatenate(split(dfeat * silu_slope(conv)), axis=1)
            grad_ref[...] += dot_nt(dconv, jnp.concatenate([stack, stack_high], axis=1))
            spread = dot(spreads[...], dconv)
            spread = spread[:WIN] + spread[WIN:]
            spread = spread[:, :TRIPS] + spread[:, TRIPS:]
            dimage_ref[pl.ds(pl.multiple_of(p * STEP, 8), WIN), :] += spread
        return carry

    lax.fori_loop(0, 3, bands, 0)
    for load in loads[3:]:
        load.wait()

    drel = dimage_ref[D : 2 * D, :]
    high = drel.astype(BF16).astype(F32)
    both = jnp.concatenate([high, drel - high], axis=0).astype(BF16)
    rel = as_column(rel_ref[...])
    for j in range(RELP // 128):
        lane = lax.broadcasted_iota(I32, (TRIPS, 128), 1) + 128 * j
        hot = jnp.where(lane == rel, 1.0, 0.0).astype(BF16)
        part = dot(both, hot)
        part = part[:D] + part[D:]
        for i in range(D // 8):
            tile = 11 * i + j
            flat_ref[8 * tile : 8 * tile + 8, :] = part[8 * i : 8 * i + 8]

    lane = lax.broadcasted_iota(I32, (CH, 128), 1)
    totals = [jnp.zeros((CH, 128), F32) for _ in range(10)]
    for g in range(BAND // CH):
        at = slice(CH * g, CH * g + CH)
        whole = grad_ref[at]
        both = whole[:, :128] + pltpu.roll(whole, 256 - WIN, 1)[:, :128]
        mark = offsets[at, 0:128]
        for k, offset in enumerate(OFFSETS):
            here = (mark == offset) & (lane < WIN)
            totals[k] = totals[k] + jnp.where(here, both, 0.0)
        totals[9] = totals[9] + jnp.where(lane == 3 * WIN - 128, whole[:, 128:], 0.0)
    small = jnp.zeros((CH, 128), F32)
    for k in range(10):
        small = jnp.where(lane == k, jnp.sum(totals[k], axis=1, keepdims=True), small)
    small = jnp.concatenate([small, jnp.zeros((128 - CH, 128), F32)], axis=0).T[:16]
    row = lax.broadcasted_iota(I32, (8, 128), 0)
    lane = lax.broadcasted_iota(I32, (8, 128), 1)
    tail = jnp.zeros((8, 128), F32)
    for k in range(10):
        at = CH * (k % 4)
        moved = small[k : k + 1] if at == 0 else pltpu.roll(small[k : k + 1], at, 1)
        here = (row == k // 4) & (lane >= at) & (lane < at + CH)
        tail = jnp.where(here, moved, tail)
    tail = jnp.where(row == 3, state[AT_BIAS : AT_BIAS + 1, :], tail)
    tail = jnp.where(row == 4, state[AT_BIAS + 8 : AT_BIAS + 9, :], tail)

    flat_ref[REL_ROWS:, :] = jnp.zeros((DEVS * SHARE - REL_ROWS, 128), F32)
    flat_ref[SMALL_DEV * SHARE : SMALL_DEV * SHARE + 8, :] = tail
    blank = jnp.zeros((SHARE_ROWS - SHARE, 128), F32)
    for dev in range(DEVS):
        mine = flat_ref[dev * SHARE : dev * SHARE + SHARE, :]
        shares[dev] = jnp.concatenate([mine, blank], axis=0)

    owner = as_column(head_ref[...])
    owner = jnp.concatenate([owner, owner], axis=1)
    q_high, q_low = split(state[AT_QUERY:AT_BIAS, :] * (1.0 / CAND))
    dhead = jnp.concatenate([dimage_ref[0:D, :], jnp.zeros((DP - D, TRIPS), F32)], axis=0)
    left = jnp.concatenate([q_high, q_low, q_high, *split(dhead)], axis=1)

    def slots(nb):
        base = pl.multiple_of(nb * 256, 256)
        cols = pl.ds(base, 256)
        high = parts[0:TRIPS, cols]
        low = parts[TRIPS:, cols]
        lane = lax.broadcasted_iota(I32, (TRIPS, 256), 1) + base
        hot = jnp.where(lane == owner, 1.0, 0.0).astype(BF16)
        grad = dot(left, jnp.concatenate([high, high, low, hot, hot], axis=0))
        most = jnp.max(jnp.abs(grad), axis=0, keepdims=True)
        power = jnp.clip(jnp.ceil(jnp.log2(jnp.maximum(most, 1e-30))), -90.0, 90.0)
        fixed = jnp.floor(grad * (jnp.exp2(15.0 - power) * FILL) + 0.5)
        row = lax.broadcasted_iota(I32, (DP, 256), 0)
        fixed = jnp.where(row == D, power, fixed)
        for half in range(2):
            pair = to_messages(fixed[:, 128 * half : 128 * half + 128])
            for k in range(2):
                dev = 4 * nb + 2 * half + k
                whole = jnp.concatenate([pair[k], code_share(shares[dev])], axis=0)
                outs[dev] = whole.astype(I32).astype(jnp.int16)

    def chunk(i, carry):
        for k in range(8):
            slots(8 * i + k)
        out_copy(i).start()
        return carry

    lax.fori_loop(0, 4, chunk, 0)
    for i in range(4):
        out_copy(i).wait()


def back(state, taps, spread, weight, offsets, part, rel_row, head_row):
    return pl.pallas_call(
        back_kernel,
        in_specs=[HBM_SPEC] * 6 + [VMEM_SPEC] * 2,
        out_specs=HBM_SPEC,
        out_shape=jax.ShapeDtypeStruct((DEVS, MSG_ROWS, 128), jnp.int16),
        scratch_shapes=[
            pltpu.VMEM((STATE, TRIPS), F32),
            pltpu.VMEM((BAND, 256), BF16),
            pltpu.VMEM((2 * WIN, BAND), BF16),
            pltpu.VMEM((FEAT, D), BF16),
            pltpu.VMEM((BAND, 256), I32),
            pltpu.VMEM((2 * TRIPS, ALL_SLOTS), BF16),
            pltpu.VMEM((DEVS, MSG_ROWS, 128), jnp.int16),
            pltpu.VMEM((DEVS, SHARE_ROWS, 128), F32),
            pltpu.VMEM((2 * D, TRIPS), F32),
            pltpu.VMEM((BAND, 256), F32),
            pltpu.VMEM((DEVS * SHARE, 128), F32),
            pltpu.SemaphoreType.DMA((12,)),
        ],
        compiler_params=params(),
        cost_estimate=cost(8 * 256 * FEAT * TRIPS, 20 << 20),
        name="back",
    )(state, taps, spread, weight, offsets, part, rel_row, head_row)


def update_kernel(
    want_ref, msg_ref, table_ref, accum_ref, table_out, accum_out, part_ref, column_ref
):
    nb = pl.program_id(0)

    @pl.when(nb == 0)
    def _():
        def unpack(pair, carry):
            cols = pl.ds(pl.multiple_of(pair * 128, 128), 128)
            fixed = from_messages(
                msg_ref[2 * pair].astype(I32).astype(F32)[:HALF],
                msg_ref[2 * pair + 1].astype(I32).astype(F32)[:HALF],
            )
            grad = fixed * (jnp.exp2(fixed[D : D + 1] - 15.0) * (1.0 / FILL))
            high = grad[:D].astype(BF16).astype(F32)
            both = jnp.concatenate([high, grad[:D] - high], axis=0)
            part_ref[:, cols] = both.astype(BF16)
            column_ref[cols, :] = as_column(want_ref[:, cols])
            return carry

        lax.fori_loop(0, DEVS // 2, unpack, 0, unroll=4)

    def block(kb, total):
        slots = pl.ds(pl.multiple_of(kb * 2048, 2048), 2048)
        lane = lax.broadcasted_iota(I32, (2048, 128), 1) + nb * 512
        column = column_ref[slots, :]
        hot = [jnp.where(column == lane + 128 * k, 1.0, 0.0).astype(BF16) for k in range(4)]
        hot = jnp.concatenate(hot, axis=1)
        return total + dot(part_ref[:, slots], hot)

    total = lax.fori_loop(0, ALL_SLOTS // 2048, block, jnp.zeros((2 * D, 512), F32), unroll=True)
    grad = total[:D] + total[D:]
    accum = accum_ref[...] + grad * grad
    accum_out[...] = accum
    table_out[...] = table_ref[...] - LEARN * grad / (jnp.sqrt(accum) + EPS)


def update(want, msgs, table_t, accum_t):
    rows = pl.BlockSpec((D, 512), lambda i: (0, i))
    return pl.pallas_call(
        update_kernel,
        grid=(OWNED // 512,),
        in_specs=[
            pl.BlockSpec((1, ALL_SLOTS), lambda i: (0, 0)),
            pl.BlockSpec((DEVS, MSG_ROWS, 128), lambda i: (0, 0, 0)),
            rows,
            rows,
        ],
        out_specs=(rows, rows),
        out_shape=(
            jax.ShapeDtypeStruct((D, OWNED), F32),
            jax.ShapeDtypeStruct((D, OWNED), F32),
        ),
        scratch_shapes=[
            pltpu.VMEM((2 * D, ALL_SLOTS), BF16),
            pltpu.VMEM((ALL_SLOTS, 128), I32),
        ],
        compiler_params=params(56),
        cost_estimate=cost(4 * DP * OWNED * ALL_SLOTS, 10 << 20),
        name="update",
    )(want, msgs, table_t, accum_t)


def share_kernel(msg_ref, out_ref):
    def one(dev, total):
        coded = msg_ref[dev].astype(I32).astype(F32)
        return total + decode_share(coded[32 - SHARE_ROWS :])

    total = lax.fori_loop(0, DEVS, one, jnp.zeros((SHARE_ROWS, 128), F32), unroll=16)
    coded = code_share(total).astype(I32).astype(jnp.int16)
    for dev in range(DEVS):
        out_ref[dev] = coded


def sum_shares(msgs):
    return pl.pallas_call(
        share_kernel,
        grid=(1,),
        in_specs=[pl.BlockSpec((DEVS, 32, 128), lambda i: (0, MSG_ROWS // 32 - 1, 0))],
        out_specs=pl.BlockSpec((DEVS, SHARE_ROWS, 128), lambda i: (0, 0, 0)),
        out_shape=jax.ShapeDtypeStruct((DEVS, SHARE_ROWS, 128), jnp.int16),
        compiler_params=params(),
        cost_estimate=cost(1 << 20, 2 << 20),
        name="sum_shares",
    )(msgs)


def spread_kernel(sum_ref, rel_ref, kernel_ref, conv_ref, fc_ref, flat_ref):
    for dev in range(DEVS):
        value = decode_share(sum_ref[dev].astype(I32).astype(F32))
        flat_ref[dev * SHARE : dev * SHARE + SHARE, :] = value[:SHARE]
    for i in range(D // 8):
        for j in range(11):
            tile = flat_ref[8 * (11 * i + j) : 8 * (11 * i + j) + 8, :]
            last = min(128, NREL - 128 * j)
            rel_ref[8 * i : 8 * i + 8, 128 * j : 128 * j + last] = tile[:, :last]
    small = flat_ref[SMALL_DEV * SHARE : SMALL_DEV * SHARE + 8, :]
    for k in range(10):
        at = CH * (k % 4)
        row = small[k // 4 : k // 4 + 1]
        row = (row if at == 0 else pltpu.roll(row, 128 - at, 1))[:, :CH]
        if k < 9:
            kernel_ref[k : k + 1, :] = row
        else:
            conv_ref[...] = row
    fc_ref[...] = jnp.concatenate([small[3:4], small[4:5]], axis=1)[:, :D]


def spread_sums(sums):
    return pl.pallas_call(
        spread_kernel,
        out_shape=(
            jax.ShapeDtypeStruct((D, NREL), F32),
            jax.ShapeDtypeStruct((9, CH), F32),
            jax.ShapeDtypeStruct((1, CH), F32),
            jax.ShapeDtypeStruct((1, D), F32),
        ),
        scratch_shapes=[pltpu.VMEM((DEVS * SHARE, 128), F32)],
        compiler_params=params(),
        cost_estimate=cost(1 << 20, 2 << 20),
        name="spread_sums",
    )(sums)


def transpose_kernel(weight_ref, out_ref):
    wide = jnp.concatenate(
        [weight_ref[...].astype(F32), jnp.zeros((256 - D, BAND), F32)], axis=0
    ).T
    out_ref[...] = wide[:, :D].astype(BF16)


def transpose_weight(weight_t):
    return pl.pallas_call(
        transpose_kernel,
        grid=(BANDS,),
        in_specs=[pl.BlockSpec((D, BAND), lambda i: (0, i))],
        out_specs=pl.BlockSpec((BAND, D), lambda i: (i, 0)),
        out_shape=jax.ShapeDtypeStruct((FEAT, D), BF16),
        compiler_params=params(),
        cost_estimate=cost(1 << 20, 9 << 20),
        name="transpose_weight",
    )(weight_t)


def relations_kernel(ids_ref, rel_ref, out_ref):
    rel = rel_ref[...]
    high = rel.astype(BF16).astype(F32)
    both = jnp.concatenate([high, rel - high], axis=0).astype(BF16)
    for e in range(0, N_EMB, 2):
        cols = slice(128 * e, 128 * e + 256)
        row = lax.broadcasted_iota(I32, (RELP, 256), 0)
        hot = jnp.where(row == ids_ref[:, cols], 1.0, 0.0).astype(BF16)
        out_ref[:, cols] = dot(both, hot).astype(BF16)


def group_relations(ids, relations_t):
    return pl.pallas_call(
        relations_kernel,
        out_shape=jax.ShapeDtypeStruct((2 * D, N_EMB * TRIPS), BF16),
        compiler_params=params(),
        cost_estimate=cost(4 * D * RELP * N_EMB * TRIPS, 3 << 20),
        name="group_relations",
    )(ids, relations_t)


def projection_kernel(start_ref, group_ref, rel_ref, taps_ref, out_ref, high_ref, low_ref):
    start = pl.multiple_of(start_ref[0] * STEP, 8)
    blank = jnp.zeros((24, 256), F32)
    total = jnp.zeros((CHUNK, DP), F32)
    for e in range(0, N_EMB, 2):
        cols = slice(128 * e, 128 * e + 256)
        group = jnp.concatenate([group_ref[e], group_ref[e + 1]], axis=1)
        head = group[:DP].astype(F32)
        rel = rel_ref[:, cols].astype(F32)
        high_ref[...] = jnp.concatenate([head[:D], rel[:D], blank], axis=0)
        low_ref[...] = jnp.concatenate([jnp.zeros((D, 256), F32), rel[D:], blank], axis=0)
        high = high_ref[pl.ds(start, CHUNK_WIN), :]
        low = low_ref[pl.ds(start, CHUNK_WIN), :]
        rest = (128 - CHUNK_WIN, 256)
        ones, none = jnp.ones(rest, F32), jnp.zeros(rest, F32)
        stack = jnp.concatenate([high, ones, low, none, high, none], axis=0).astype(BF16)
        conv = dot(taps_ref[...], stack)
        feat = (conv * sigmoid(conv)).astype(BF16)
        total = total + dot_nt(feat, group[DP:])
    for s in range(N_SCORE):
        out_ref[s] = total[OWN_FEAT * s : OWN_FEAT * s + OWN_FEAT, :D]


def projection(start, groups, rels, taps):
    vmem = pl.BlockSpec(memory_space=pltpu.VMEM)
    return pl.pallas_call(
        projection_kernel,
        in_specs=[pl.BlockSpec(memory_space=pltpu.SMEM), vmem, vmem, vmem],
        out_specs=vmem,
        out_shape=jax.ShapeDtypeStruct((N_SCORE, OWN_FEAT, D), F32),
        scratch_shapes=[pltpu.VMEM((2 * D + 24, 256), F32), pltpu.VMEM((2 * D + 24, 256), F32)],
        compiler_params=params(),
        cost_estimate=cost(2 * FEAT * TRIPS * 640, 4 << 20),
        name="projection",
    )(start, groups, rels, taps)


def exchange(x, axes):
    return lax.all_to_all(x, axes, split_axis=0, concat_axis=0, tiled=True)


def high_part(x):
    return x.astype(BF16).astype(F32)


def taps_kernel(place_ref, small_ref, offset_ref, taps_ref, spread_ref, chunk_ref, twice_ref, all_ref):
    columns = small_ref[...].T
    twice_ref[0:CH, :] = columns[:CH]
    twice_ref[CH : 2 * CH, :] = columns[:CH]
    columns = columns[:CH]

    def one_of(codes, columns):
        value = jnp.zeros(codes.shape, F32)
        for k, offset in enumerate(OFFSETS):
            value = jnp.where(codes == offset, columns[:, k : k + 1], value)
        return value

    def bias_parts(columns):
        bias = columns[:, 9:10]
        first = high_part(bias)
        second = high_part(bias - first)
        return first, second, bias - first - second

    for g in range(BAND // CH):
        at = slice(CH * g, CH * g + CH)
        codes = offset_ref[at]
        low = codes >= LOW - 1
        value = one_of(jnp.where(low, codes - LOW, codes), columns)
        value = jnp.where(low, value - high_part(value), value)
        for part, column in enumerate(bias_parts(columns)):
            value = jnp.where(codes == BIAS_MARK + part, column, value)
        all_ref[at, :] = value
    whole = all_ref[...]
    taps_ref[...] = whole.astype(BF16)
    high = whole[:, :128].T[:WIN]
    low = pltpu.roll(whole, 256 - 2 * WIN, 1)[:, :128].T[:WIN]
    spread_ref[...] = jnp.concatenate([high, low], axis=0).astype(BF16)

    first = place_ref[0] * CHUNK
    base = place_ref[1] * STEP
    columns = twice_ref[pl.ds(pl.multiple_of((place_ref[0] % 4) * 8, 8), CH), :]
    parts = bias_parts(columns)
    lane = lax.broadcasted_iota(I32, (CH, 128), 1)
    for g in range(CHUNK // CH + 1):
        size = min(CH, CHUNK - CH * g)
        feature = lax.broadcasted_iota(I32, (CH, 128), 0) + (first + CH * g)
        place = feature >> 5
        row = ((place.astype(F32) + 0.5) * (1.0 / OUT_W)).astype(I32)
        origin = row * IMG_W + (place - row * OUT_W) - base
        value = jnp.where(lane < CHUNK_WIN, one_of(lane - origin, columns), 0.0)
        high = high_part(value)
        biased = high
        for part in range(3):
            biased = jnp.where(lane == CHUNK_WIN + part, parts[part], biased)
        whole = jnp.concatenate([biased, high, value - high], axis=1).astype(BF16)
        chunk_ref[CH * g : CH * g + size, :] = whole[:size]


def build_taps(place, small, offsets):
    vmem = pl.BlockSpec(memory_space=pltpu.VMEM)
    return pl.pallas_call(
        taps_kernel,
        in_specs=[pl.BlockSpec(memory_space=pltpu.SMEM), vmem, vmem],
        out_specs=(vmem,) * 3,
        out_shape=(
            jax.ShapeDtypeStruct((BAND, 256), BF16),
            jax.ShapeDtypeStruct((2 * WIN, BAND), BF16),
            jax.ShapeDtypeStruct((CHUNK, 384), BF16),
        ),
        scratch_shapes=[pltpu.VMEM((2 * CH, 128), F32), pltpu.VMEM((BAND, 256), F32)],
        compiler_params=params(),
        cost_estimate=cost(1 << 20, 3 << 20),
        name="build_taps",
    )(place, small, offsets)


def shards(
    table,
    accum,
    request,
    head_slot,
    rel_ids,
    tail_slot,
    relations,
    kernel,
    conv_bias,
    fc_weight,
    fc_bias,
):
    table_t = table.T
    asked = jnp.concatenate(
        [
            request[0],
            jnp.zeros((DEVS, SLOTS), I32),
            jnp.broadcast_to(rel_ids[None], (DEVS, TRIPS)),
        ],
        axis=1,
    )
    asked = exchange(asked, AXES)
    want = asked[:, :SLOTS].reshape(1, ALL_SLOTS)
    group = asked[:, 128:].reshape(N_EMB, N_SCORE, TRIPS)
    group = lax.dynamic_index_in_dim(group, lax.axis_index("score"), 1, keepdims=False)
    outgoing = gather_rows(want, table_t)
    incoming = exchange(outgoing, AXES)

    tails = jnp.pad(tail_slot, ((0, 0), (0, 128 - CAND)), constant_values=-1)
    counts = count_tails(tails)
    hot = (jnp.arange(NREL, dtype=I32)[:, None] == rel_ids[None, :]).astype(F32)
    rel_t = jnp.dot(relations.T, hot, precision=lax.Precision.HIGHEST)
    emb = lax.axis_index("emb")
    start = emb * CHUNK // (OUT_W * CH) // 2
    small = jnp.concatenate([kernel, conv_bias[None]], axis=0)
    small = jnp.pad(small, ((0, 118), (0, 128 - CH)))
    offsets = jnp.asarray(offset_map())
    taps, spread, chunk_taps = build_taps(jnp.stack([emb, start]), small, offsets)
    weight = transpose_weight(fc_weight.T)
    rels = group_relations(
        group.reshape(1, N_EMB * TRIPS), jnp.pad(relations.T, ((0, 0), (0, RELP - NREL)))
    )
    true_row = tail_slot[:, :1].T
    head_row = head_slot[None, :]
    ready = (counts, rel_t, taps, spread, chunk_taps, weight, rels, true_row)
    incoming, ready = lax.optimization_barrier((incoming, ready))
    counts, rel_t, taps, spread, chunk_taps, weight, rels, true_row = ready

    part, send, state = front(
        incoming, head_row, rel_t, taps, fc_weight.T, counts, true_row, fc_bias[None, :]
    )
    groups = exchange(send, "emb")
    returned = exchange(
        back(state, taps, spread, weight, offsets, part, rel_ids[None, :], head_row), AXES
    )

    halves = projection(start.reshape(1), groups, rels, chunk_taps)
    halves = halves.reshape(N_SCORE // 2, 2, OWN_FEAT, D)
    here = lax.axis_index("score")
    side = here & 1
    kept = lax.dynamic_index_in_dim(halves, side, 1, keepdims=False)
    sent = lax.dynamic_index_in_dim(halves, 1 - side, 1, keepdims=False)
    left = kept + lax.ppermute(sent, "score", [(i, i ^ 1) for i in range(N_SCORE)])
    fc_grad = lax.dynamic_index_in_dim(left, here >> 1, 0, keepdims=False)
    for step in range(1, 4):
        sent = lax.dynamic_index_in_dim(left, (here >> 1) ^ step, 0, keepdims=False)
        pairs = [(i, i ^ (2 * step)) for i in range(N_SCORE)]
        fc_grad = fc_grad + lax.ppermute(sent, "score", pairs)

    sums = exchange(sum_shares(returned), AXES)
    new_table, new_accum = update(want, returned, table_t, accum.T)
    rel_sum, kernel_sum, conv_sum, fc_sum = spread_sums(sums)
    return (
        new_table.T,
        new_accum.T,
        fc_grad,
        kernel_sum,
        conv_sum[0],
        fc_sum[0],
        rel_sum.T,
    )


def solution(mesh):
    rows = P(AXES, None)
    in_specs = (rows, rows, P(AXES, None, None), P(AXES), P(AXES), rows) + (P(),) * 5
    out_specs = (rows, rows, rows) + (P(),) * 4
    return jax.shard_map(shards, mesh=mesh, in_specs=in_specs, out_specs=out_specs, check_vma=False)
```

```python
import jax
import jax.numpy as jnp
import numpy as np
from jax import lax
from jax.experimental import pallas as pl
from jax.experimental.pallas import tpu as pltpu
from jax.sharding import PartitionSpec as P

AXES = ("emb", "score")
DEVS = 128
N_EMB = 16
N_SCORE = 8
SLOTS = 64
ALL_SLOTS = DEVS * SLOTS
OWNED = 2048
D = 200
DP = 208
HALF = DP // 2
TRIPS = 128
CAND = 65
IMG_W = 20
OUT_W = 18
CH = 32
FEAT = 10368
BAND = 1152
BANDS = 9
WIN = 80
STEP = 40
NREL = 1345
RELP = 1408
REL_ROWS = 200 * 11
SHARE = 18
SHARE_ROWS = 24
SMALL_DEV = 124
MSG_ROWS = HALF + SHARE_ROWS
CHUNK = FEAT // N_EMB
OWN_FEAT = FEAT // DEVS
CHUNK_WIN = 104
LEARN = 0.1
EPS = 1e-10
F32 = jnp.float32
BF16 = jnp.bfloat16
I32 = jnp.int32
NT = (((1,), (1,)), ((), ()))
FILL = 0.9999

OFFSETS = [20 * a + b for a in range(3) for b in range(3)]
BIAS_MARK = 500
LOW = 1000


def offset_map():
    feature = np.arange(BAND)
    place = feature // CH
    origin = (place // OUT_W) * IMG_W + place % OUT_W
    lane = np.arange(256)
    offset = lane[None, :] % WIN - origin[:, None]
    offset = np.where((offset >= 0) & (offset < 43), offset, -1)
    offset = np.where(lane[None, :] < 2 * WIN, offset, offset + LOW)
    for part in range(16):
        offset[:, 3 * WIN + part] = BIAS_MARK + part
    return offset.astype(np.int32)


def window_start(emb):
    return emb * CHUNK // (OUT_W * CH) // 2


def params(mib=40):
    return pltpu.CompilerParams(vmem_limit_bytes=mib << 20)


VMEM_SPEC = pl.BlockSpec()
HBM_SPEC = pl.BlockSpec(memory_space=pltpu.HBM)
ANY_SPEC = pl.BlockSpec(memory_space=pl.ANY)
AT_QUERY = 2 * D
AT_BIAS = AT_QUERY + DP
AT_DPRE = AT_BIAS + 16
STATE = AT_DPRE + D
GROUP = CHUNK_WIN + D


def cost(flops, moved):
    return pl.CostEstimate(flops=flops, bytes_accessed=moved, transcendentals=0)


def dot(a, b):
    return jnp.dot(a, b, preferred_element_type=F32)


def dot_nt(a, b):
    return lax.dot_general(a, b, NT, preferred_element_type=F32)


def split(x):
    high = x.astype(BF16)
    low = (x - high.astype(F32)).astype(BF16)
    return high, low


def sigmoid(value):
    return 0.5 * jnp.tanh(0.5 * value) + 0.5


def silu_slope(value):
    sig = sigmoid(value)
    return sig * (1.0 + value * (1.0 - sig))


def as_column(row):
    return jnp.broadcast_to(row, (128, row.shape[1])).T


def to_messages(x):
    top, bottom = x[:HALF], x[HALF:]
    left = lax.broadcasted_iota(I32, (HALF, 128), 1) < SLOTS
    first = jnp.where(left, top, pltpu.roll(bottom, SLOTS, 1))
    second = jnp.where(left, pltpu.roll(top, SLOTS, 1), bottom)
    return first, second


def from_messages(first, second):
    left = lax.broadcasted_iota(I32, (HALF, 128), 1) < SLOTS
    top = jnp.where(left, first, pltpu.roll(second, SLOTS, 1))
    bottom = jnp.where(left, pltpu.roll(first, SLOTS, 1), second)
    return jnp.concatenate([top, bottom], axis=0)


def code_share(x):
    most = jnp.max(jnp.abs(x), axis=0, keepdims=True)
    power = jnp.clip(jnp.ceil(jnp.log2(jnp.maximum(most, 1e-30))), -90.0, 90.0)
    scaled = x * (jnp.exp2(15.0 - power) * FILL)
    fixed = jnp.floor(scaled + 0.5)
    rest = jnp.floor((scaled - fixed) * 16384.0 + 0.5)
    row = lax.broadcasted_iota(I32, (SHARE_ROWS, 128), 0)
    tail = jnp.where(row == SHARE, power, pltpu.roll(rest, SHARE + 1, 0))
    return jnp.where(row < SHARE, fixed, tail)


def decode_share(coded):
    row = lax.broadcasted_iota(I32, (SHARE_ROWS, 128), 0)
    rest = pltpu.roll(coded, SHARE_ROWS - SHARE - 1, 0) * (1.0 / 16384.0)
    first = SHARE_ROWS - SHARE - 1
    value = coded + jnp.where(row < first, rest, 0.0)
    return jnp.where(row < SHARE, value, 0.0) * (jnp.exp2(coded[SHARE : SHARE + 1] - 15.0) * (1.0 / FILL))


def gather_kernel(want_ref, table_ref, out_ref, table, rows, outs, sems):
    table_copy = pltpu.make_async_copy(table_ref, table, sems.at[4])
    table_copy.start()
    table_copy.wait()
    rows[...] = jnp.concatenate([table[...], jnp.zeros((DP - D, OWNED), F32)], axis=0).astype(BF16)

    def out_copy(i):
        at = pl.ds(i * 32, 32)
        return pltpu.make_async_copy(outs.at[at], out_ref.at[at], sems.at[i])

    def block(i, carry):
        for q in range(8):
            want = want_ref[:, pl.ds(pl.multiple_of(i * 2048 + 256 * q, 256), 256)]
            total = jnp.zeros((DP, 256), F32)
            for kb in range(OWNED // 256):
                row = lax.broadcasted_iota(I32, (256, 256), 0) + 256 * kb
                hot = jnp.where(row == want, 1.0, 0.0).astype(BF16)
                total = total + dot(rows[:, 256 * kb : 256 * kb + 256], hot)
            for half in range(2):
                first, second = to_messages(total[:, 128 * half : 128 * half + 128])
                outs[32 * i + 4 * q + 2 * half] = first.astype(BF16)
                outs[32 * i + 4 * q + 2 * half + 1] = second.astype(BF16)
        out_copy(i).start()
        return carry

    lax.fori_loop(0, 4, block, 0)
    for i in range(4):
        out_copy(i).wait()


def gather_rows(want, table_t):
    return pl.pallas_call(
        gather_kernel,
        in_specs=[VMEM_SPEC, HBM_SPEC],
        out_specs=HBM_SPEC,
        out_shape=jax.ShapeDtypeStruct((DEVS, HALF, 128), BF16),
        scratch_shapes=[
            pltpu.VMEM((D, OWNED), F32),
            pltpu.VMEM((DP, OWNED), BF16),
            pltpu.VMEM((DEVS, HALF, 128), BF16),
            pltpu.SemaphoreType.DMA((5,)),
        ],
        compiler_params=params(60),
        cost_estimate=cost(2 * DP * OWNED * ALL_SLOTS, 6 << 20),
        name="gather_rows",
    )(want, table_t)


def counts_kernel(tail_ref, out_ref, buf_ref):
    high_row = lax.broadcasted_iota(I32, (64, 128), 0)
    low_row = lax.broadcasted_iota(I32, (128, 128), 0)

    def one(t, carry):
        slot = tail_ref[pl.ds(t, 1), :]
        high = jnp.where(high_row == (slot >> 7), 1.0, 0.0).astype(BF16)
        low = jnp.where(low_row == (slot & 127), 1.0, 0.0).astype(BF16)
        buf_ref[pl.ds(pl.multiple_of(t * 64, 64), 64), :] = dot_nt(high, low)
        return carry

    lax.fori_loop(0, TRIPS, one, 0, unroll=8)
    for high in range(64):
        out_ref[:, 128 * high : 128 * high + 128] = buf_ref[
            pl.ds(high, TRIPS, stride=64), :
        ].astype(BF16)


def count_tails(tails):
    return pl.pallas_call(
        counts_kernel,
        out_shape=jax.ShapeDtypeStruct((TRIPS, ALL_SLOTS), BF16),
        scratch_shapes=[pltpu.VMEM((ALL_SLOTS, 128), F32)],
        compiler_params=params(),
        cost_estimate=cost(TRIPS * 2 * 64 * 128 * 128, 2 << 20),
        name="count_tails",
    )(tails)


def window_parts(image_ref, p):
    win = image_ref[pl.ds(pl.multiple_of(p * STEP, 8), WIN), :]
    high = win.astype(BF16).astype(F32)
    ones = jnp.ones((256 - 3 * WIN, TRIPS), F32)
    return high, win - high, ones


def front_kernel(
    msg_ref, head_ref, rel_ref, taps_ref, weight_ref, count_ref, true_ref, bias_ref,
    part_ref, send_ref, state_ref,
    msgs, heads, taps, weights, counts, trues, biases, parts, rows_t, own, state, sems,
):
    def msg_copy(i):
        at = pl.ds(i * 32, 32)
        return pltpu.make_async_copy(msg_ref.at[at], msgs.at[at], sems.at[i])

    def part_copy(i):
        cols = pl.ds(pl.multiple_of(i * 2048, 2048), 2048)
        return pltpu.make_async_copy(parts.at[:, cols], part_ref.at[:, cols], sems.at[4 + i])

    rel_at = state.at[pl.ds(D, D)]
    pairs = [(head_ref, heads), (rel_ref, rel_at), (taps_ref, taps), (weight_ref, weights)]
    pairs += [(bias_ref, biases), (true_ref, trues), (count_ref, counts)]
    loads = [pltpu.make_async_copy(a, b, sems.at[8 + k]) for k, (a, b) in enumerate(pairs)]
    loads[0].start()
    for i in range(4):
        msg_copy(i).start()
    for load in loads[1:]:
        load.start()
    loads[0].wait()

    def unpack(i, head):
        msg_copy(i).wait()
        for k in range(8):
            both = []
            for pair in (16 * i + 2 * k, 16 * i + 2 * k + 1):
                first = msgs[2 * pair].astype(F32)
                second = msgs[2 * pair + 1].astype(F32)
                both.append(from_messages(first, second))
            both = jnp.concatenate(both, axis=1).astype(BF16)
            base = pl.multiple_of(i * 2048 + k * 256, 256)
            rows_t[:, pl.ds(base, 256)] = both
            slot = lax.broadcasted_iota(I32, (256, TRIPS), 0) + base
            hot = jnp.where(slot == heads[...], 1.0, 0.0).astype(BF16)
            head = head + dot(both, hot)
        return head

    head = lax.fori_loop(0, 4, unpack, jnp.zeros((DP, TRIPS), F32))
    state[0:D, :] = head[:D]

    for load in loads[1:4]:
        load.wait()
    pre = jnp.zeros((D, TRIPS), F32)
    for p in range(BANDS):
        high, low, ones = window_parts(state, p)
        stack = jnp.concatenate([high, low, high, ones], axis=0).astype(BF16)
        conv = dot(taps[...], stack)
        feat = (conv * sigmoid(conv)).astype(BF16)
        pre = pre + dot(weights[:, p * BAND : p * BAND + BAND], feat)

    for load in loads[4:]:
        load.wait()
    bias = jnp.concatenate([biases[...], jnp.zeros((1, 256 - D), F32)], axis=1)
    pre = pre + as_column(bias)[:D]
    true = as_column(trues[...])
    true = jnp.concatenate([true, true], axis=1)
    query = pre * sigmoid(pre)
    pad = jnp.zeros((DP - D, TRIPS), F32)
    query = jnp.concatenate([query, pad], axis=0)
    state[AT_QUERY:AT_BIAS, :] = query
    wide = jnp.concatenate([query, jnp.zeros((256 - DP, TRIPS), F32)], axis=0).T[:, :DP]
    high = wide.astype(BF16).astype(F32)
    both = jnp.concatenate([high, wide - high], axis=0).astype(BF16)

    def block(i, total):
        for k in range(8):
            base = pl.multiple_of(i * 2048 + k * 256, 256)
            cols = pl.ds(base, 256)
            rows = rows_t[:, cols]
            scores = dot(both, rows)
            scores = scores[:TRIPS] + scores[TRIPS:]
            lane = lax.broadcasted_iota(I32, (TRIPS, 256), 1) + base
            label = jnp.where(lane == true, 1.0, 0.0)
            grad = counts[:, cols].astype(F32) * sigmoid(scores) - label
            part = jnp.concatenate(split(grad), axis=0)
            parts[:, cols] = part
            total = total + dot_nt(rows, part)
        part_copy(i).start()
        return total

    total = lax.fori_loop(0, 4, block, jnp.zeros((DP, 256), F32))
    dquery = (total[:D, :TRIPS] + total[:D, TRIPS:]) * (1.0 / CAND)
    dpre = dquery * silu_slope(pre)
    total = jnp.concatenate(
        [jnp.sum(dpre, axis=1, keepdims=True), jnp.zeros((256 - D, 1), F32)], axis=0
    )
    total = jnp.broadcast_to(total, (256, 128)).T[:8]
    state[AT_BIAS:AT_DPRE, :] = jnp.concatenate([total[:, :128], total[:, 128:]], axis=0)
    state[AT_DPRE:, :] = dpre
    head = jnp.concatenate([head[:D], jnp.zeros((D + 32, TRIPS), F32)], axis=0)
    for e in range(N_EMB):
        at = window_start(e) * STEP
        own[e] = jnp.concatenate([head[at : at + CHUNK_WIN], dpre], axis=0).astype(BF16)
    sends = [pltpu.make_async_copy(own, send_ref, sems.at[15])]
    sends.append(pltpu.make_async_copy(state, state_ref, sems.at[16]))
    for send in sends:
        send.start()
    for send in sends:
        send.wait()
    for i in range(4):
        part_copy(i).wait()


def front(msgs, head_row, rel_t, taps, weight_t, counts, true_row, bias_row):
    return pl.pallas_call(
        front_kernel,
        in_specs=[ANY_SPEC] + [HBM_SPEC] * 7,
        out_specs=(HBM_SPEC,) * 3,
        out_shape=(
            jax.ShapeDtypeStruct((2 * TRIPS, ALL_SLOTS), BF16),
            jax.ShapeDtypeStruct((N_EMB, GROUP, TRIPS), BF16),
            jax.ShapeDtypeStruct((STATE, TRIPS), F32),
        ),
        scratch_shapes=[
            pltpu.VMEM((DEVS, HALF, 128), BF16),
            pltpu.VMEM((1, TRIPS), I32),
            pltpu.VMEM((BAND, 256), BF16),
            pltpu.VMEM((D, FEAT), BF16),
            pltpu.VMEM((TRIPS, ALL_SLOTS), BF16),
            pltpu.VMEM((1, TRIPS), I32),
            pltpu.VMEM((1, D), F32),
            pltpu.VMEM((2 * TRIPS, ALL_SLOTS), BF16),
            pltpu.VMEM((DP, ALL_SLOTS), BF16),
            pltpu.VMEM((N_EMB, GROUP, TRIPS), BF16),
            pltpu.VMEM((STATE, TRIPS), F32),
            pltpu.SemaphoreType.DMA((17,)),
        ],
        compiler_params=params(57),
        cost_estimate=cost(8 * 256 * DP * ALL_SLOTS, 20 << 20),
        name="front",
    )(msgs, head_row, rel_t, taps, weight_t, counts, true_row, bias_row)


def back_kernel(
    state_ref, taps_ref, spread_ref, weight_ref, offset_ref, part_ref, rel_ref, head_ref,
    out_ref,
    state, taps, spreads, weights, offsets, parts, outs, shares, dimage_ref, grad_ref, flat_ref,
    sems,
):
    def weight_copy(i):
        at = pl.ds(pl.multiple_of(i * 3 * BAND, BAND), 3 * BAND)
        return pltpu.make_async_copy(weight_ref.at[at], weights.at[at], sems.at[i])

    def out_copy(i):
        at = pl.ds(i * 32, 32)
        return pltpu.make_async_copy(outs.at[at], out_ref.at[at], sems.at[3 + i])

    pairs = [(state_ref, state), (taps_ref, taps), (spread_ref, spreads)]
    pairs += [(offset_ref, offsets), (part_ref, parts)]
    loads = [pltpu.make_async_copy(a, b, sems.at[7 + k]) for k, (a, b) in enumerate(pairs)]
    for load in loads[:2]:
        load.start()
    weight_copy(0).start()
    loads[2].start()
    for i in range(1, 3):
        weight_copy(i).start()
    for load in loads[3:]:
        load.start()
    for load in loads[:3]:
        load.wait()

    dimage_ref[...] = jnp.zeros_like(dimage_ref)
    grad_ref[...] = jnp.zeros_like(grad_ref)
    dpre = state[AT_DPRE:, :].astype(BF16)

    def bands(i, carry):
        weight_copy(i).wait()
        for k in range(3):
            p = 3 * i + k
            high, low, ones = window_parts(state, p)
            stack = jnp.concatenate([high, low, high, ones], axis=0).astype(BF16)
            none = jnp.zeros_like(low)
            stack_high = jnp.concatenate([high, none, high, ones], axis=0).astype(BF16)
            conv = dot(taps[...], stack)
            weight = weights[pl.ds(pl.multiple_of(p * BAND, BAND), BAND), :]
            dfeat = dot(weight, dpre)
            dconv = jnp.concatenate(split(dfeat * silu_slope(conv)), axis=1)
            grad_ref[...] += dot_nt(dconv, jnp.concatenate([stack, stack_high], axis=1))
            spread = dot(spreads[...], dconv)
            spread = spread[:WIN] + spread[WIN:]
            spread = spread[:, :TRIPS] + spread[:, TRIPS:]
            dimage_ref[pl.ds(pl.multiple_of(p * STEP, 8), WIN), :] += spread
        return carry

    lax.fori_loop(0, 3, bands, 0)
    for load in loads[3:]:
        load.wait()

    drel = dimage_ref[D : 2 * D, :]
    high = drel.astype(BF16).astype(F32)
    both = jnp.concatenate([high, drel - high], axis=0).astype(BF16)
    rel = as_column(rel_ref[...])
    for j in range(RELP // 128):
        lane = lax.broadcasted_iota(I32, (TRIPS, 128), 1) + 128 * j
        hot = jnp.where(lane == rel, 1.0, 0.0).astype(BF16)
        part = dot(both, hot)
        part = part[:D] + part[D:]
        for i in range(D // 8):
            tile = 11 * i + j
            flat_ref[8 * tile : 8 * tile + 8, :] = part[8 * i : 8 * i + 8]

    lane = lax.broadcasted_iota(I32, (CH, 128), 1)
    totals = [jnp.zeros((CH, 128), F32) for _ in range(10)]
    for g in range(BAND // CH):
        at = slice(CH * g, CH * g + CH)
        whole = grad_ref[at]
        both = whole[:, :128] + pltpu.roll(whole, 256 - WIN, 1)[:, :128]
        mark = offsets[at, 0:128]
        for k, offset in enumerate(OFFSETS):
            here = (mark == offset) & (lane < WIN)
            totals[k] = totals[k] + jnp.where(here, both, 0.0)
        totals[9] = totals[9] + jnp.where(lane == 3 * WIN - 128, whole[:, 128:], 0.0)
    small = jnp.zeros((CH, 128), F32)
    for k in range(10):
        small = jnp.where(lane == k, jnp.sum(totals[k], axis=1, keepdims=True), small)
    small = jnp.concatenate([small, jnp.zeros((128 - CH, 128), F32)], axis=0).T[:16]
    row = lax.broadcasted_iota(I32, (8, 128), 0)
    lane = lax.broadcasted_iota(I32, (8, 128), 1)
    tail = jnp.zeros((8, 128), F32)
    for k in range(10):
        at = CH * (k % 4)
        moved = small[k : k + 1] if at == 0 else pltpu.roll(small[k : k + 1], at, 1)
        here = (row == k // 4) & (lane >= at) & (lane < at + CH)
        tail = jnp.where(here, moved, tail)
    tail = jnp.where(row == 3, state[AT_BIAS : AT_BIAS + 1, :], tail)
    tail = jnp.where(row == 4, state[AT_BIAS + 8 : AT_BIAS + 9, :], tail)

    flat_ref[REL_ROWS:, :] = jnp.zeros((DEVS * SHARE - REL_ROWS, 128), F32)
    flat_ref[SMALL_DEV * SHARE : SMALL_DEV * SHARE + 8, :] = tail
    blank = jnp.zeros((SHARE_ROWS - SHARE, 128), F32)
    for dev in range(DEVS):
        mine = flat_ref[dev * SHARE : dev * SHARE + SHARE, :]
        shares[dev] = jnp.concatenate([mine, blank], axis=0)

    owner = as_column(head_ref[...])
    owner = jnp.concatenate([owner, owner], axis=1)
    q_high, q_low = split(state[AT_QUERY:AT_BIAS, :] * (1.0 / CAND))
    dhead = jnp.concatenate([dimage_ref[0:D, :], jnp.zeros((DP - D, TRIPS), F32)], axis=0)
    left = jnp.concatenate([q_high, q_low, q_high, *split(dhead)], axis=1)

    def slots(nb):
        base = pl.multiple_of(nb * 256, 256)
        cols = pl.ds(base, 256)
        high = parts[0:TRIPS, cols]
        low = parts[TRIPS:, cols]
        lane = lax.broadcasted_iota(I32, (TRIPS, 256), 1) + base
        hot = jnp.where(lane == owner, 1.0, 0.0).astype(BF16)
        grad = dot(left, jnp.concatenate([high, high, low, hot, hot], axis=0))
        most = jnp.max(jnp.abs(grad), axis=0, keepdims=True)
        power = jnp.clip(jnp.ceil(jnp.log2(jnp.maximum(most, 1e-30))), -90.0, 90.0)
        fixed = jnp.floor(grad * (jnp.exp2(15.0 - power) * FILL) + 0.5)
        row = lax.broadcasted_iota(I32, (DP, 256), 0)
        fixed = jnp.where(row == D, power, fixed)
        for half in range(2):
            pair = to_messages(fixed[:, 128 * half : 128 * half + 128])
            for k in range(2):
                dev = 4 * nb + 2 * half + k
                whole = jnp.concatenate([pair[k], code_share(shares[dev])], axis=0)
                outs[dev] = whole.astype(I32).astype(jnp.int16)

    def chunk(i, carry):
        for k in range(8):
            slots(8 * i + k)
        out_copy(i).start()
        return carry

    lax.fori_loop(0, 4, chunk, 0)
    for i in range(4):
        out_copy(i).wait()


def back(state, taps, spread, weight, offsets, part, rel_row, head_row):
    return pl.pallas_call(
        back_kernel,
        in_specs=[HBM_SPEC] * 6 + [VMEM_SPEC] * 2,
        out_specs=HBM_SPEC,
        out_shape=jax.ShapeDtypeStruct((DEVS, MSG_ROWS, 128), jnp.int16),
        scratch_shapes=[
            pltpu.VMEM((STATE, TRIPS), F32),
            pltpu.VMEM((BAND, 256), BF16),
            pltpu.VMEM((2 * WIN, BAND), BF16),
            pltpu.VMEM((FEAT, D), BF16),
            pltpu.VMEM((BAND, 256), I32),
            pltpu.VMEM((2 * TRIPS, ALL_SLOTS), BF16),
            pltpu.VMEM((DEVS, MSG_ROWS, 128), jnp.int16),
            pltpu.VMEM((DEVS, SHARE_ROWS, 128), F32),
            pltpu.VMEM((2 * D, TRIPS), F32),
            pltpu.VMEM((BAND, 256), F32),
            pltpu.VMEM((DEVS * SHARE, 128), F32),
            pltpu.SemaphoreType.DMA((12,)),
        ],
        compiler_params=params(60),
        cost_estimate=cost(8 * 256 * FEAT * TRIPS, 20 << 20),
        name="back",
    )(state, taps, spread, weight, offsets, part, rel_row, head_row)


def update_kernel(
    want_ref, msg_ref, table_ref, accum_ref, table_out, accum_out, part_ref, column_ref, total_ref
):
    nb = pl.program_id(0)

    def unpack(pair):
        cols = slice(pair * 128, pair * 128 + 128)
        fixed = from_messages(
            msg_ref[2 * pair].astype(I32).astype(F32)[:HALF],
            msg_ref[2 * pair + 1].astype(I32).astype(F32)[:HALF],
        )
        grad = fixed * (jnp.exp2(fixed[D : D + 1] - 15.0) * (1.0 / FILL))
        high = high_part(grad[:D])
        part_ref[:, cols] = jnp.concatenate([high, grad[:D] - high], axis=0).astype(BF16)
        column_ref[cols, :] = as_column(want_ref[:, cols])

    def block(kb):
        slots = slice(kb * 2048, kb * 2048 + 2048)
        lane = lax.broadcasted_iota(I32, (2048, 128), 1) + nb * 512
        column = column_ref[slots, :]
        hot = [jnp.where(column == lane + 128 * k, 1.0, 0.0).astype(BF16) for k in range(4)]
        return dot(part_ref[:, slots], jnp.concatenate(hot, axis=1))

    @pl.when(nb == 0)
    def _():
        total = jnp.zeros((2 * D, 512), F32)
        for kb in range(4):
            for pair in range(16):
                unpack(16 * kb + pair)
            total = total + block(kb)
        total_ref[...] = total

    @pl.when(nb > 0)
    def _():
        total = jnp.zeros((2 * D, 512), F32)
        for kb in range(4):
            total = total + block(kb)
        total_ref[...] = total

    grad = total_ref[:D] + total_ref[D:]
    accum = accum_ref[...] + grad * grad
    accum_out[...] = accum
    table_out[...] = table_ref[...] - LEARN * grad / (jnp.sqrt(accum) + EPS)


def update(want, msgs, table_t, accum_t):
    rows = pl.BlockSpec((D, 512), lambda i: (0, i))
    return pl.pallas_call(
        update_kernel,
        grid=(OWNED // 512,),
        in_specs=[
            pl.BlockSpec((1, ALL_SLOTS), lambda i: (0, 0)),
            pl.BlockSpec((DEVS, MSG_ROWS, 128), lambda i: (0, 0, 0)),
            rows,
            rows,
        ],
        out_specs=(rows, rows),
        out_shape=(
            jax.ShapeDtypeStruct((D, OWNED), F32),
            jax.ShapeDtypeStruct((D, OWNED), F32),
        ),
        scratch_shapes=[
            pltpu.VMEM((2 * D, ALL_SLOTS), BF16),
            pltpu.VMEM((ALL_SLOTS, 128), I32),
            pltpu.VMEM((2 * D, 512), F32),
        ],
        compiler_params=params(60),
        cost_estimate=cost(4 * DP * OWNED * ALL_SLOTS, 10 << 20),
        name="update",
    )(want, msgs, table_t, accum_t)


def share_kernel(msg_ref, out_ref):
    def one(dev, total):
        coded = msg_ref[dev].astype(I32).astype(F32)
        return total + decode_share(coded[32 - SHARE_ROWS :])

    total = lax.fori_loop(0, DEVS, one, jnp.zeros((SHARE_ROWS, 128), F32), unroll=16)
    coded = code_share(total).astype(I32).astype(jnp.int16)
    for dev in range(DEVS):
        out_ref[dev] = coded


def sum_shares(msgs):
    return pl.pallas_call(
        share_kernel,
        grid=(1,),
        in_specs=[pl.BlockSpec((DEVS, 32, 128), lambda i: (0, MSG_ROWS // 32 - 1, 0))],
        out_specs=pl.BlockSpec((DEVS, SHARE_ROWS, 128), lambda i: (0, 0, 0)),
        out_shape=jax.ShapeDtypeStruct((DEVS, SHARE_ROWS, 128), jnp.int16),
        compiler_params=params(),
        cost_estimate=cost(1 << 20, 2 << 20),
        name="sum_shares",
    )(msgs)


def spread_kernel(sum_ref, rel_ref, kernel_ref, conv_ref, fc_ref, flat_ref):
    for dev in range(DEVS):
        value = decode_share(sum_ref[dev].astype(I32).astype(F32))
        flat_ref[dev * SHARE : dev * SHARE + SHARE, :] = value[:SHARE]
    for i in range(D // 8):
        for j in range(11):
            tile = flat_ref[8 * (11 * i + j) : 8 * (11 * i + j) + 8, :]
            last = min(128, NREL - 128 * j)
            rel_ref[8 * i : 8 * i + 8, 128 * j : 128 * j + last] = tile[:, :last]
    small = flat_ref[SMALL_DEV * SHARE : SMALL_DEV * SHARE + 8, :]
    for k in range(10):
        at = CH * (k % 4)
        row = small[k // 4 : k // 4 + 1]
        row = (row if at == 0 else pltpu.roll(row, 128 - at, 1))[:, :CH]
        if k < 9:
            kernel_ref[k : k + 1, :] = row
        else:
            conv_ref[...] = row
    fc_ref[...] = jnp.concatenate([small[3:4], small[4:5]], axis=1)[:, :D]


def spread_sums(sums):
    return pl.pallas_call(
        spread_kernel,
        out_shape=(
            jax.ShapeDtypeStruct((D, NREL), F32),
            jax.ShapeDtypeStruct((9, CH), F32),
            jax.ShapeDtypeStruct((1, CH), F32),
            jax.ShapeDtypeStruct((1, D), F32),
        ),
        scratch_shapes=[pltpu.VMEM((DEVS * SHARE, 128), F32)],
        compiler_params=params(),
        cost_estimate=cost(1 << 20, 2 << 20),
        name="spread_sums",
    )(sums)


def transpose_kernel(weight_ref, out_ref):
    wide = jnp.concatenate(
        [weight_ref[...].astype(F32), jnp.zeros((256 - D, BAND), F32)], axis=0
    ).T
    out_ref[...] = wide[:, :D].astype(BF16)


def transpose_weight(weight_t):
    return pl.pallas_call(
        transpose_kernel,
        grid=(BANDS,),
        in_specs=[pl.BlockSpec((D, BAND), lambda i: (0, i))],
        out_specs=pl.BlockSpec((BAND, D), lambda i: (i, 0)),
        out_shape=jax.ShapeDtypeStruct((FEAT, D), BF16),
        compiler_params=params(),
        cost_estimate=cost(1 << 20, 9 << 20),
        name="transpose_weight",
    )(weight_t)


def relations_kernel(ids_ref, rel_ref, out_ref):
    rel = rel_ref[...]
    high = rel.astype(BF16).astype(F32)
    both = jnp.concatenate([high, rel - high], axis=0).astype(BF16)
    for e in range(0, N_EMB, 2):
        cols = slice(128 * e, 128 * e + 256)
        row = lax.broadcasted_iota(I32, (RELP, 256), 0)
        hot = jnp.where(row == ids_ref[:, cols], 1.0, 0.0).astype(BF16)
        out_ref[:, cols] = dot(both, hot).astype(BF16)


def group_relations(ids, relations_t):
    return pl.pallas_call(
        relations_kernel,
        out_shape=jax.ShapeDtypeStruct((2 * D, N_EMB * TRIPS), BF16),
        compiler_params=params(),
        cost_estimate=cost(4 * D * RELP * N_EMB * TRIPS, 3 << 20),
        name="group_relations",
    )(ids, relations_t)


def projection_kernel(start_ref, group_ref, rel_ref, taps_ref, out_ref, high_ref, low_ref):
    start = pl.multiple_of(start_ref[0] * STEP, 8)
    blank = jnp.zeros((24, 256), F32)
    total = jnp.zeros((CHUNK, D), F32)
    for e in range(0, N_EMB, 2):
        cols = slice(128 * e, 128 * e + 256)
        group = jnp.concatenate([group_ref[e], group_ref[e + 1]], axis=1).astype(F32)
        head = group[:CHUNK_WIN]
        rel = rel_ref[:, cols].astype(F32)
        high_ref[...] = jnp.concatenate([jnp.zeros((D, 256), F32), rel[:D], blank], axis=0)
        low_ref[...] = jnp.concatenate([jnp.zeros((D, 256), F32), rel[D:], blank], axis=0)
        high = head + high_ref[pl.ds(start, CHUNK_WIN), :]
        low = low_ref[pl.ds(start, CHUNK_WIN), :]
        rest = (128 - CHUNK_WIN, 256)
        ones, none = jnp.ones(rest, F32), jnp.zeros(rest, F32)
        stack = jnp.concatenate([high, ones, low, none, high, none], axis=0).astype(BF16)
        conv = dot(taps_ref[...], stack)
        feat = (conv * sigmoid(conv)).astype(BF16)
        total = total + dot_nt(feat, group[CHUNK_WIN:].astype(BF16))
    for s in range(N_SCORE):
        out_ref[s] = total[OWN_FEAT * s : OWN_FEAT * s + OWN_FEAT]


def projection(start, groups, rels, taps):
    vmem = pl.BlockSpec(memory_space=pltpu.VMEM)
    return pl.pallas_call(
        projection_kernel,
        in_specs=[pl.BlockSpec(memory_space=pltpu.SMEM), vmem, vmem, vmem],
        out_specs=vmem,
        out_shape=jax.ShapeDtypeStruct((N_SCORE, OWN_FEAT, D), F32),
        scratch_shapes=[pltpu.VMEM((2 * D + 24, 256), F32), pltpu.VMEM((2 * D + 24, 256), F32)],
        compiler_params=params(),
        cost_estimate=cost(2 * FEAT * TRIPS * 640, 4 << 20),
        name="projection",
    )(start, groups, rels, taps)


def exchange(x, axes):
    return lax.all_to_all(x, axes, split_axis=0, concat_axis=0, tiled=True)


def high_part(x):
    return x.astype(BF16).astype(F32)


def taps_kernel(place_ref, small_ref, offset_ref, taps_ref, spread_ref, chunk_ref, twice_ref, all_ref):
    columns = small_ref[...].T
    twice_ref[0:CH, :] = columns[:CH]
    twice_ref[CH : 2 * CH, :] = columns[:CH]
    columns = columns[:CH]

    def one_of(codes, columns):
        value = jnp.zeros(codes.shape, F32)
        for k, offset in enumerate(OFFSETS):
            value = jnp.where(codes == offset, columns[:, k : k + 1], value)
        return value

    def bias_parts(columns):
        bias = columns[:, 9:10]
        first = high_part(bias)
        second = high_part(bias - first)
        return first, second, bias - first - second

    for g in range(BAND // CH):
        at = slice(CH * g, CH * g + CH)
        codes = offset_ref[at]
        low = codes >= LOW - 1
        value = one_of(jnp.where(low, codes - LOW, codes), columns)
        value = jnp.where(low, value - high_part(value), value)
        for part, column in enumerate(bias_parts(columns)):
            value = jnp.where(codes == BIAS_MARK + part, column, value)
        all_ref[at, :] = value
    whole = all_ref[...]
    taps_ref[...] = whole.astype(BF16)
    high = whole[:, :128].T[:WIN]
    low = pltpu.roll(whole, 256 - 2 * WIN, 1)[:, :128].T[:WIN]
    spread_ref[...] = jnp.concatenate([high, low], axis=0).astype(BF16)

    first = place_ref[0] * CHUNK
    base = place_ref[1] * STEP
    columns = twice_ref[pl.ds(pl.multiple_of((place_ref[0] % 4) * 8, 8), CH), :]
    parts = bias_parts(columns)
    lane = lax.broadcasted_iota(I32, (CH, 128), 1)
    for g in range(CHUNK // CH + 1):
        size = min(CH, CHUNK - CH * g)
        feature = lax.broadcasted_iota(I32, (CH, 128), 0) + (first + CH * g)
        place = feature >> 5
        row = ((place.astype(F32) + 0.5) * (1.0 / OUT_W)).astype(I32)
        origin = row * IMG_W + (place - row * OUT_W) - base
        value = jnp.where(lane < CHUNK_WIN, one_of(lane - origin, columns), 0.0)
        high = high_part(value)
        biased = high
        for part in range(3):
            biased = jnp.where(lane == CHUNK_WIN + part, parts[part], biased)
        whole = jnp.concatenate([biased, high, value - high], axis=1).astype(BF16)
        chunk_ref[CH * g : CH * g + size, :] = whole[:size]


def build_taps(place, small, offsets):
    vmem = pl.BlockSpec(memory_space=pltpu.VMEM)
    return pl.pallas_call(
        taps_kernel,
        in_specs=[pl.BlockSpec(memory_space=pltpu.SMEM), vmem, vmem],
        out_specs=(vmem,) * 3,
        out_shape=(
            jax.ShapeDtypeStruct((BAND, 256), BF16),
            jax.ShapeDtypeStruct((2 * WIN, BAND), BF16),
            jax.ShapeDtypeStruct((CHUNK, 384), BF16),
        ),
        scratch_shapes=[pltpu.VMEM((2 * CH, 128), F32), pltpu.VMEM((BAND, 256), F32)],
        compiler_params=params(),
        cost_estimate=cost(1 << 20, 3 << 20),
        name="build_taps",
    )(place, small, offsets)


def shards(
    table,
    accum,
    request,
    head_slot,
    rel_ids,
    tail_slot,
    relations,
    kernel,
    conv_bias,
    fc_weight,
    fc_bias,
):
    table_t = table.T
    asked = jnp.concatenate(
        [
            request[0],
            jnp.zeros((DEVS, SLOTS), I32),
            jnp.broadcast_to(rel_ids[None], (DEVS, TRIPS)),
        ],
        axis=1,
    )
    asked = exchange(asked, AXES)
    want = asked[:, :SLOTS].reshape(1, ALL_SLOTS)
    group = asked[:, 128:].reshape(N_EMB, N_SCORE, TRIPS)
    group = lax.dynamic_index_in_dim(group, lax.axis_index("score"), 1, keepdims=False)
    outgoing = gather_rows(want, table_t)
    incoming = exchange(outgoing, AXES)

    tails = jnp.pad(tail_slot, ((0, 0), (0, 128 - CAND)), constant_values=-1)
    counts = count_tails(tails)
    hot = (jnp.arange(NREL, dtype=I32)[:, None] == rel_ids[None, :]).astype(F32)
    rel_t = jnp.dot(relations.T, hot, precision=lax.Precision.HIGHEST)
    emb = lax.axis_index("emb")
    start = window_start(emb)
    small = jnp.concatenate([kernel, conv_bias[None]], axis=0)
    small = jnp.pad(small, ((0, 118), (0, 128 - CH)))
    offsets = jnp.asarray(offset_map())
    taps, spread, chunk_taps = build_taps(jnp.stack([emb, start]), small, offsets)
    weight = transpose_weight(fc_weight.T)
    rels = group_relations(
        group.reshape(1, N_EMB * TRIPS), jnp.pad(relations.T, ((0, 0), (0, RELP - NREL)))
    )
    true_row = tail_slot[:, :1].T
    head_row = head_slot[None, :]
    ready = (counts, rel_t, taps, spread, chunk_taps, weight, rels, true_row)
    incoming, ready = lax.optimization_barrier((incoming, ready))
    counts, rel_t, taps, spread, chunk_taps, weight, rels, true_row = ready

    part, send, state = front(
        incoming, head_row, rel_t, taps, fc_weight.T, counts, true_row, fc_bias[None, :]
    )
    groups = exchange(send, "emb")
    returned = exchange(
        back(state, taps, spread, weight, offsets, part, rel_ids[None, :], head_row), AXES
    )

    halves = projection(start.reshape(1), groups, rels, chunk_taps)
    halves = halves.reshape(N_SCORE // 2, 2, OWN_FEAT, D)
    here = lax.axis_index("score")
    side = here & 1
    kept = lax.dynamic_index_in_dim(halves, side, 1, keepdims=False)
    sent = lax.dynamic_index_in_dim(halves, 1 - side, 1, keepdims=False)
    left = kept + lax.ppermute(sent, "score", [(i, i ^ 1) for i in range(N_SCORE)])
    fc_grad = lax.dynamic_index_in_dim(left, here >> 1, 0, keepdims=False)
    for step in range(1, 4):
        sent = lax.dynamic_index_in_dim(left, (here >> 1) ^ step, 0, keepdims=False)
        pairs = [(i, i ^ (2 * step)) for i in range(N_SCORE)]
        fc_grad = fc_grad + lax.ppermute(sent, "score", pairs)

    sums = exchange(sum_shares(returned), AXES)
    new_table, new_accum = update(want, returned, table_t, accum.T)
    rel_sum, kernel_sum, conv_sum, fc_sum = spread_sums(sums)
    return (
        new_table.T,
        new_accum.T,
        fc_grad,
        kernel_sum,
        conv_sum[0],
        fc_sum[0],
        rel_sum.T,
    )


def solution(mesh):
    rows = P(AXES, None)
    in_specs = (rows, rows, P(AXES, None, None), P(AXES), P(AXES), rows) + (P(),) * 5
    out_specs = (rows, rows, rows) + (P(),) * 4
    return jax.shard_map(shards, mesh=mesh, in_specs=in_specs, out_specs=out_specs, check_vma=False)
```

```python
import jax
import jax.numpy as jnp
import numpy as np
from jax import lax
from jax.experimental import pallas as pl
from jax.experimental.pallas import tpu as pltpu
from jax.sharding import PartitionSpec as P

AXES = ("emb", "score")
DEVS = 128
N_EMB = 16
N_SCORE = 8
SLOTS = 64
ALL_SLOTS = DEVS * SLOTS
OWNED = 2048
D = 200
DP = 208
HALF = DP // 2
TRIPS = 128
CAND = 65
IMG_W = 20
OUT_W = 18
CH = 32
FEAT = 10368
BAND = 1152
BANDS = 9
WIN = 80
STEP = 40
NREL = 1345
RELP = 1408
REL_ROWS = 200 * 11
SHARE = 18
SHARE_ROWS = 24
SMALL_DEV = 124
MSG_ROWS = HALF + SHARE_ROWS
CHUNK = FEAT // N_EMB
OWN_FEAT = FEAT // DEVS
CHUNK_WIN = 80
LEARN = 0.1
EPS = 1e-10
F32 = jnp.float32
BF16 = jnp.bfloat16
I32 = jnp.int32
NT = (((1,), (1,)), ((), ()))
FILL = 0.9999

OFFSETS = [20 * a + b for a in range(3) for b in range(3)]
BIAS_MARK = 500
LOW = 1000


def offset_map():
    feature = np.arange(BAND)
    place = feature // CH
    origin = (place // OUT_W) * IMG_W + place % OUT_W
    lane = np.arange(256)
    offset = lane[None, :] % WIN - origin[:, None]
    offset = np.where((offset >= 0) & (offset < 43), offset, -1)
    offset = np.where(lane[None, :] < 2 * WIN, offset, offset + LOW)
    for part in range(16):
        offset[:, 3 * WIN + part] = BIAS_MARK + part
    return offset.astype(np.int32)


def window_start(emb):
    return emb * CHUNK // (OUT_W * CH)


def params(mib=40):
    return pltpu.CompilerParams(vmem_limit_bytes=mib << 20)


VMEM_SPEC = pl.BlockSpec()
HBM_SPEC = pl.BlockSpec(memory_space=pltpu.HBM)
ANY_SPEC = pl.BlockSpec(memory_space=pl.ANY)
AT_QUERY = 2 * D
AT_BIAS = AT_QUERY + DP
AT_DPRE = AT_BIAS + 16
STATE = AT_DPRE + D
GROUP = CHUNK_WIN + D


def cost(flops, moved):
    return pl.CostEstimate(flops=flops, bytes_accessed=moved, transcendentals=0)


def dot(a, b):
    return jnp.dot(a, b, preferred_element_type=F32)


def dot_nt(a, b):
    return lax.dot_general(a, b, NT, preferred_element_type=F32)


def split(x):
    high = x.astype(BF16)
    low = (x - high.astype(F32)).astype(BF16)
    return high, low


def sigmoid(value):
    return 0.5 * jnp.tanh(0.5 * value) + 0.5


def silu_slope(value):
    sig = sigmoid(value)
    return sig * (1.0 + value * (1.0 - sig))


def as_column(row):
    return jnp.broadcast_to(row, (128, row.shape[1])).T


def to_messages(x):
    top, bottom = x[:HALF], x[HALF:]
    left = lax.broadcasted_iota(I32, (HALF, 128), 1) < SLOTS
    first = jnp.where(left, top, pltpu.roll(bottom, SLOTS, 1))
    second = jnp.where(left, pltpu.roll(top, SLOTS, 1), bottom)
    return first, second


def from_messages(first, second):
    left = lax.broadcasted_iota(I32, (HALF, 128), 1) < SLOTS
    top = jnp.where(left, first, pltpu.roll(second, SLOTS, 1))
    bottom = jnp.where(left, pltpu.roll(first, SLOTS, 1), second)
    return jnp.concatenate([top, bottom], axis=0)


def code_share(x):
    most = jnp.max(jnp.abs(x), axis=0, keepdims=True)
    power = jnp.clip(jnp.ceil(jnp.log2(jnp.maximum(most, 1e-30))), -90.0, 90.0)
    scaled = x * (jnp.exp2(15.0 - power) * FILL)
    fixed = jnp.floor(scaled + 0.5)
    rest = jnp.floor((scaled - fixed) * 16384.0 + 0.5)
    row = lax.broadcasted_iota(I32, (SHARE_ROWS, 128), 0)
    tail = jnp.where(row == SHARE, power, pltpu.roll(rest, SHARE + 1, 0))
    return jnp.where(row < SHARE, fixed, tail)


def decode_share(coded):
    row = lax.broadcasted_iota(I32, (SHARE_ROWS, 128), 0)
    rest = pltpu.roll(coded, SHARE_ROWS - SHARE - 1, 0) * (1.0 / 16384.0)
    first = SHARE_ROWS - SHARE - 1
    value = coded + jnp.where(row < first, rest, 0.0)
    return jnp.where(row < SHARE, value, 0.0) * (jnp.exp2(coded[SHARE : SHARE + 1] - 15.0) * (1.0 / FILL))


def rounded_kernel(table_ref, out_ref):
    out_ref[...] = jnp.concatenate(
        [table_ref[...], jnp.zeros((DP - D, 512), F32)], axis=0
    ).astype(BF16)


def round_table(table_t):
    return pl.pallas_call(
        rounded_kernel,
        grid=(4,),
        in_specs=[pl.BlockSpec((D, 512), lambda i: (0, i))],
        out_specs=pl.BlockSpec((DP, 512), lambda i: (0, i)),
        out_shape=jax.ShapeDtypeStruct((DP, OWNED), BF16),
        compiler_params=params(60),
        cost_estimate=cost(1 << 20, 3 << 20),
        name="round_table",
    )(table_t)


def gather_kernel(want_ref, table_ref, out_ref, rows, outs, sems):
    table_copy = pltpu.make_async_copy(table_ref, rows, sems.at[4])
    table_copy.start()
    table_copy.wait()

    def out_copy(i):
        at = pl.ds(i * 32, 32)
        return pltpu.make_async_copy(outs.at[at], out_ref.at[at], sems.at[i])

    def block(i, carry):
        for q in range(8):
            want = want_ref[:, pl.ds(pl.multiple_of(i * 2048 + 256 * q, 256), 256)]
            total = jnp.zeros((DP, 256), F32)
            for kb in range(OWNED // 256):
                row = lax.broadcasted_iota(I32, (256, 256), 0) + 256 * kb
                hot = jnp.where(row == want, 1.0, 0.0).astype(BF16)
                total = total + dot(rows[:, 256 * kb : 256 * kb + 256], hot)
            for half in range(2):
                first, second = to_messages(total[:, 128 * half : 128 * half + 128])
                outs[32 * i + 4 * q + 2 * half] = first.astype(BF16)
                outs[32 * i + 4 * q + 2 * half + 1] = second.astype(BF16)
        out_copy(i).start()
        return carry

    lax.fori_loop(0, 4, block, 0, unroll=True)
    for i in range(4):
        out_copy(i).wait()


def gather_rows(want, table_t):
    return pl.pallas_call(
        gather_kernel,
        in_specs=[VMEM_SPEC, HBM_SPEC],
        out_specs=HBM_SPEC,
        out_shape=jax.ShapeDtypeStruct((DEVS, HALF, 128), BF16),
        scratch_shapes=[
            pltpu.VMEM((DP, OWNED), BF16),
            pltpu.VMEM((DEVS, HALF, 128), BF16),
            pltpu.SemaphoreType.DMA((5,)),
        ],
        compiler_params=params(60),
        cost_estimate=cost(2 * DP * OWNED * ALL_SLOTS, 6 << 20),
        name="gather_rows",
    )(want, table_t)


def counts_kernel(tail_ref, out_ref, buf_ref):
    high_row = lax.broadcasted_iota(I32, (64, 128), 0)
    low_row = lax.broadcasted_iota(I32, (128, 128), 0)

    def one(t, carry):
        slot = tail_ref[pl.ds(t, 1), :]
        high = jnp.where(high_row == (slot >> 7), 1.0, 0.0).astype(BF16)
        low = jnp.where(low_row == (slot & 127), 1.0, 0.0).astype(BF16)
        buf_ref[pl.ds(pl.multiple_of(t * 64, 64), 64), :] = dot_nt(high, low)
        return carry

    lax.fori_loop(0, TRIPS, one, 0, unroll=8)
    for high in range(64):
        out_ref[:, 128 * high : 128 * high + 128] = buf_ref[
            pl.ds(high, TRIPS, stride=64), :
        ].astype(BF16)


def count_tails(tails):
    return pl.pallas_call(
        counts_kernel,
        out_shape=jax.ShapeDtypeStruct((TRIPS, ALL_SLOTS), BF16),
        scratch_shapes=[pltpu.VMEM((ALL_SLOTS, 128), F32)],
        compiler_params=params(),
        cost_estimate=cost(TRIPS * 2 * 64 * 128 * 128, 2 << 20),
        name="count_tails",
    )(tails)


def window_parts(image_ref, p):
    win = image_ref[pl.ds(pl.multiple_of(p * STEP, 8), WIN), :]
    high = win.astype(BF16).astype(F32)
    ones = jnp.ones((256 - 3 * WIN, TRIPS), F32)
    return high, win - high, ones


def front_kernel(
    msg_ref, head_ref, rel_ref, taps_ref, weight_ref, count_ref, true_ref, bias_ref,
    part_ref, send_ref, state_ref,
    msgs, heads, taps, weights, counts, trues, biases, parts, rows_t, own, state, sems,
):
    def msg_copy(i):
        at = pl.ds(i * 32, 32)
        return pltpu.make_async_copy(msg_ref.at[at], msgs.at[at], sems.at[i])

    def part_copy(i):
        cols = pl.ds(pl.multiple_of(i * 2048, 2048), 2048)
        return pltpu.make_async_copy(parts.at[:, cols], part_ref.at[:, cols], sems.at[4 + i])

    rel_at = state.at[pl.ds(D, D)]
    pairs = [(head_ref, heads), (rel_ref, rel_at), (taps_ref, taps), (weight_ref, weights)]
    pairs += [(bias_ref, biases), (true_ref, trues), (count_ref, counts)]
    loads = [pltpu.make_async_copy(a, b, sems.at[8 + k]) for k, (a, b) in enumerate(pairs)]
    loads[0].start()
    for i in range(4):
        msg_copy(i).start()
    for load in loads[1:]:
        load.start()
    loads[0].wait()

    def unpack(i, head):
        msg_copy(i).wait()
        for k in range(8):
            both = []
            for pair in (16 * i + 2 * k, 16 * i + 2 * k + 1):
                first = msgs[2 * pair].astype(F32)
                second = msgs[2 * pair + 1].astype(F32)
                both.append(from_messages(first, second))
            both = jnp.concatenate(both, axis=1).astype(BF16)
            base = pl.multiple_of(i * 2048 + k * 256, 256)
            rows_t[:, pl.ds(base, 256)] = both
            slot = lax.broadcasted_iota(I32, (256, TRIPS), 0) + base
            hot = jnp.where(slot == heads[...], 1.0, 0.0).astype(BF16)
            head = head + dot(both, hot)
        return head

    head = lax.fori_loop(0, 4, unpack, jnp.zeros((DP, TRIPS), F32))
    state[0:D, :] = head[:D]

    for load in loads[1:4]:
        load.wait()
    pre = jnp.zeros((D, TRIPS), F32)
    for p in range(BANDS):
        high, low, ones = window_parts(state, p)
        stack = jnp.concatenate([high, low, high, ones], axis=0).astype(BF16)
        conv = dot(taps[...], stack)
        feat = (conv * sigmoid(conv)).astype(BF16)
        pre = pre + dot(weights[:, p * BAND : p * BAND + BAND], feat)

    for load in loads[4:]:
        load.wait()
    bias = jnp.concatenate([biases[...], jnp.zeros((1, 256 - D), F32)], axis=1)
    pre = pre + as_column(bias)[:D]
    true = as_column(trues[...])
    true = jnp.concatenate([true, true], axis=1)
    query = pre * sigmoid(pre)
    pad = jnp.zeros((DP - D, TRIPS), F32)
    query = jnp.concatenate([query, pad], axis=0)
    state[AT_QUERY:AT_BIAS, :] = query
    wide = jnp.concatenate([query, jnp.zeros((256 - DP, TRIPS), F32)], axis=0).T[:, :DP]
    high = wide.astype(BF16).astype(F32)
    both = jnp.concatenate([high, wide - high], axis=0).astype(BF16)

    def block(i, total):
        for k in range(8):
            base = pl.multiple_of(i * 2048 + k * 256, 256)
            cols = pl.ds(base, 256)
            rows = rows_t[:, cols]
            scores = dot(both, rows)
            scores = scores[:TRIPS] + scores[TRIPS:]
            lane = lax.broadcasted_iota(I32, (TRIPS, 256), 1) + base
            label = jnp.where(lane == true, 1.0, 0.0)
            grad = counts[:, cols].astype(F32) * sigmoid(scores) - label
            part = jnp.concatenate(split(grad), axis=0)
            parts[:, cols] = part
            total = total + dot_nt(rows, part)
        part_copy(i).start()
        return total

    total = lax.fori_loop(0, 4, block, jnp.zeros((DP, 256), F32), unroll=True)
    dquery = (total[:D, :TRIPS] + total[:D, TRIPS:]) * (1.0 / CAND)
    dpre = dquery * silu_slope(pre)
    total = jnp.concatenate(
        [jnp.sum(dpre, axis=1, keepdims=True), jnp.zeros((256 - D, 1), F32)], axis=0
    )
    total = jnp.broadcast_to(total, (256, 128)).T[:8]
    state[AT_BIAS:AT_DPRE, :] = jnp.concatenate([total[:, :128], total[:, 128:]], axis=0)
    state[AT_DPRE:, :] = dpre
    head = jnp.concatenate([head[:D], jnp.zeros((D + 32, TRIPS), F32)], axis=0)
    for e in range(N_EMB):
        at = window_start(e) * IMG_W
        own[e] = jnp.concatenate([head[at : at + CHUNK_WIN], dpre], axis=0).astype(BF16)
    sends = [pltpu.make_async_copy(own, send_ref, sems.at[15])]
    sends.append(pltpu.make_async_copy(state, state_ref, sems.at[16]))
    for send in sends:
        send.start()
    for send in sends:
        send.wait()
    for i in range(4):
        part_copy(i).wait()


def front(msgs, head_row, rel_t, taps, weight_t, counts, true_row, bias_row):
    return pl.pallas_call(
        front_kernel,
        in_specs=[ANY_SPEC] + [HBM_SPEC] * 7,
        out_specs=(HBM_SPEC,) * 3,
        out_shape=(
            jax.ShapeDtypeStruct((2 * TRIPS, ALL_SLOTS), BF16),
            jax.ShapeDtypeStruct((N_EMB, GROUP, TRIPS), BF16),
            jax.ShapeDtypeStruct((STATE, TRIPS), F32),
        ),
        scratch_shapes=[
            pltpu.VMEM((DEVS, HALF, 128), BF16),
            pltpu.VMEM((1, TRIPS), I32),
            pltpu.VMEM((BAND, 256), BF16),
            pltpu.VMEM((D, FEAT), BF16),
            pltpu.VMEM((TRIPS, ALL_SLOTS), BF16),
            pltpu.VMEM((1, TRIPS), I32),
            pltpu.VMEM((1, D), F32),
            pltpu.VMEM((2 * TRIPS, ALL_SLOTS), BF16),
            pltpu.VMEM((DP, ALL_SLOTS), BF16),
            pltpu.VMEM((N_EMB, GROUP, TRIPS), BF16),
            pltpu.VMEM((STATE, TRIPS), F32),
            pltpu.SemaphoreType.DMA((17,)),
        ],
        compiler_params=params(57),
        cost_estimate=cost(8 * 256 * DP * ALL_SLOTS, 20 << 20),
        name="front",
    )(msgs, head_row, rel_t, taps, weight_t, counts, true_row, bias_row)


def back_kernel(
    state_ref, taps_ref, spread_ref, weight_ref, offset_ref, part_ref, rel_ref, head_ref,
    out_ref,
    state, taps, spreads, weights, offsets, parts, outs, shares, dimage_ref, grad_ref, flat_ref,
    sems,
):
    def weight_copy(i):
        at = pl.ds(pl.multiple_of(i * 3 * BAND, BAND), 3 * BAND)
        return pltpu.make_async_copy(weight_ref.at[at], weights.at[at], sems.at[i])

    def out_copy(i):
        at = pl.ds(i * 32, 32)
        return pltpu.make_async_copy(outs.at[at], out_ref.at[at], sems.at[3 + i])

    pairs = [(state_ref, state), (taps_ref, taps), (spread_ref, spreads)]
    pairs += [(offset_ref, offsets), (part_ref, parts)]
    loads = [pltpu.make_async_copy(a, b, sems.at[7 + k]) for k, (a, b) in enumerate(pairs)]
    for load in loads[:2]:
        load.start()
    weight_copy(0).start()
    loads[2].start()
    for i in range(1, 3):
        weight_copy(i).start()
    for load in loads[3:]:
        load.start()
    for load in loads[:3]:
        load.wait()

    dimage_ref[...] = jnp.zeros_like(dimage_ref)
    grad_ref[...] = jnp.zeros_like(grad_ref)
    dpre = state[AT_DPRE:, :].astype(BF16)

    def bands(i, carry):
        weight_copy(i).wait()
        for k in range(3):
            p = 3 * i + k
            high, low, ones = window_parts(state, p)
            stack = jnp.concatenate([high, low, high, ones], axis=0).astype(BF16)
            none = jnp.zeros_like(low)
            stack_high = jnp.concatenate([high, none, high, ones], axis=0).astype(BF16)
            conv = dot(taps[...], stack)
            weight = weights[pl.ds(pl.multiple_of(p * BAND, BAND), BAND), :]
            dfeat = dot(weight, dpre)
            dconv = jnp.concatenate(split(dfeat * silu_slope(conv)), axis=1)
            grad_ref[...] += dot_nt(dconv, jnp.concatenate([stack, stack_high], axis=1))
            spread = dot(spreads[...], dconv)
            spread = spread[:WIN] + spread[WIN:]
            spread = spread[:, :TRIPS] + spread[:, TRIPS:]
            dimage_ref[pl.ds(pl.multiple_of(p * STEP, 8), WIN), :] += spread
        return carry

    lax.fori_loop(0, 3, bands, 0)
    for load in loads[3:]:
        load.wait()

    drel = dimage_ref[D : 2 * D, :]
    high = drel.astype(BF16).astype(F32)
    both = jnp.concatenate([high, drel - high], axis=0).astype(BF16)
    rel = as_column(rel_ref[...])
    for j in range(RELP // 128):
        lane = lax.broadcasted_iota(I32, (TRIPS, 128), 1) + 128 * j
        hot = jnp.where(lane == rel, 1.0, 0.0).astype(BF16)
        part = dot(both, hot)
        part = part[:D] + part[D:]
        for i in range(D // 8):
            tile = 11 * i + j
            flat_ref[8 * tile : 8 * tile + 8, :] = part[8 * i : 8 * i + 8]

    lane = lax.broadcasted_iota(I32, (CH, 128), 1)
    totals = [jnp.zeros((CH, 128), F32) for _ in range(10)]
    for g in range(BAND // CH):
        at = slice(CH * g, CH * g + CH)
        whole = grad_ref[at]
        both = whole[:, :128] + pltpu.roll(whole, 256 - WIN, 1)[:, :128]
        mark = offsets[at, 0:128]
        for k, offset in enumerate(OFFSETS):
            here = (mark == offset) & (lane < WIN)
            totals[k] = totals[k] + jnp.where(here, both, 0.0)
        totals[9] = totals[9] + jnp.where(lane == 3 * WIN - 128, whole[:, 128:], 0.0)
    small = jnp.zeros((CH, 128), F32)
    for k in range(10):
        small = jnp.where(lane == k, jnp.sum(totals[k], axis=1, keepdims=True), small)
    small = jnp.concatenate([small, jnp.zeros((128 - CH, 128), F32)], axis=0).T[:16]
    row = lax.broadcasted_iota(I32, (8, 128), 0)
    lane = lax.broadcasted_iota(I32, (8, 128), 1)
    tail = jnp.zeros((8, 128), F32)
    for k in range(10):
        at = CH * (k % 4)
        moved = small[k : k + 1] if at == 0 else pltpu.roll(small[k : k + 1], at, 1)
        here = (row == k // 4) & (lane >= at) & (lane < at + CH)
        tail = jnp.where(here, moved, tail)
    tail = jnp.where(row == 3, state[AT_BIAS : AT_BIAS + 1, :], tail)
    tail = jnp.where(row == 4, state[AT_BIAS + 8 : AT_BIAS + 9, :], tail)

    flat_ref[REL_ROWS:, :] = jnp.zeros((DEVS * SHARE - REL_ROWS, 128), F32)
    flat_ref[SMALL_DEV * SHARE : SMALL_DEV * SHARE + 8, :] = tail
    blank = jnp.zeros((SHARE_ROWS - SHARE, 128), F32)
    for dev in range(DEVS):
        mine = flat_ref[dev * SHARE : dev * SHARE + SHARE, :]
        shares[dev] = jnp.concatenate([mine, blank], axis=0)

    owner = as_column(head_ref[...])
    owner = jnp.concatenate([owner, owner], axis=1)
    q_high, q_low = split(state[AT_QUERY:AT_BIAS, :] * (1.0 / CAND))
    dhead = jnp.concatenate([dimage_ref[0:D, :], jnp.zeros((DP - D, TRIPS), F32)], axis=0)
    left = jnp.concatenate([q_high, q_low, q_high, *split(dhead)], axis=1)

    def slots(nb):
        base = pl.multiple_of(nb * 256, 256)
        cols = pl.ds(base, 256)
        high = parts[0:TRIPS, cols]
        low = parts[TRIPS:, cols]
        lane = lax.broadcasted_iota(I32, (TRIPS, 256), 1) + base
        hot = jnp.where(lane == owner, 1.0, 0.0).astype(BF16)
        grad = dot(left, jnp.concatenate([high, high, low, hot, hot], axis=0))
        most = jnp.max(jnp.abs(grad), axis=0, keepdims=True)
        power = jnp.clip(jnp.ceil(jnp.log2(jnp.maximum(most, 1e-30))), -90.0, 90.0)
        fixed = jnp.floor(grad * (jnp.exp2(15.0 - power) * FILL) + 0.5)
        row = lax.broadcasted_iota(I32, (DP, 256), 0)
        fixed = jnp.where(row == D, power, fixed)
        for half in range(2):
            pair = to_messages(fixed[:, 128 * half : 128 * half + 128])
            for k in range(2):
                dev = 4 * nb + 2 * half + k
                whole = jnp.concatenate([pair[k], code_share(shares[dev])], axis=0)
                outs[dev] = whole.astype(I32).astype(jnp.int16)

    def chunk(i, carry):
        for k in range(8):
            slots(8 * i + k)
        out_copy(i).start()
        return carry

    lax.fori_loop(0, 4, chunk, 0, unroll=True)
    for i in range(4):
        out_copy(i).wait()


def back(state, taps, spread, weight, offsets, part, rel_row, head_row):
    return pl.pallas_call(
        back_kernel,
        in_specs=[HBM_SPEC] * 6 + [VMEM_SPEC] * 2,
        out_specs=HBM_SPEC,
        out_shape=jax.ShapeDtypeStruct((DEVS, MSG_ROWS, 128), jnp.int16),
        scratch_shapes=[
            pltpu.VMEM((STATE, TRIPS), F32),
            pltpu.VMEM((BAND, 256), BF16),
            pltpu.VMEM((2 * WIN, BAND), BF16),
            pltpu.VMEM((FEAT, D), BF16),
            pltpu.VMEM((BAND, 256), I32),
            pltpu.VMEM((2 * TRIPS, ALL_SLOTS), BF16),
            pltpu.VMEM((DEVS, MSG_ROWS, 128), jnp.int16),
            pltpu.VMEM((DEVS, SHARE_ROWS, 128), F32),
            pltpu.VMEM((2 * D, TRIPS), F32),
            pltpu.VMEM((BAND, 256), F32),
            pltpu.VMEM((DEVS * SHARE, 128), F32),
            pltpu.SemaphoreType.DMA((12,)),
        ],
        compiler_params=params(60),
        cost_estimate=cost(8 * 256 * FEAT * TRIPS, 20 << 20),
        name="back",
    )(state, taps, spread, weight, offsets, part, rel_row, head_row)


def update_kernel(
    want_ref, msg_ref, table_ref, accum_ref, table_out, accum_out, part_ref, column_ref, total_ref
):
    nb = pl.program_id(0)

    def unpack(pair):
        cols = slice(pair * 128, pair * 128 + 128)
        fixed = from_messages(
            msg_ref[2 * pair].astype(I32).astype(F32)[:HALF],
            msg_ref[2 * pair + 1].astype(I32).astype(F32)[:HALF],
        )
        grad = fixed * (jnp.exp2(fixed[D : D + 1] - 15.0) * (1.0 / FILL))
        high = high_part(grad[:D])
        part_ref[:, cols] = jnp.concatenate([high, grad[:D] - high], axis=0).astype(BF16)
        column_ref[cols, :] = as_column(want_ref[:, cols])

    def block(kb):
        slots = slice(kb * 2048, kb * 2048 + 2048)
        lane = lax.broadcasted_iota(I32, (2048, 128), 1) + nb * 512
        column = column_ref[slots, :]
        hot = [jnp.where(column == lane + 128 * k, 1.0, 0.0).astype(BF16) for k in range(4)]
        return dot(part_ref[:, slots], jnp.concatenate(hot, axis=1))

    @pl.when(nb == 0)
    def _():
        total = jnp.zeros((2 * D, 512), F32)
        for kb in range(4):
            for pair in range(16):
                unpack(16 * kb + pair)
            total = total + block(kb)
        total_ref[...] = total

    @pl.when(nb > 0)
    def _():
        total = jnp.zeros((2 * D, 512), F32)
        for kb in range(4):
            total = total + block(kb)
        total_ref[...] = total

    grad = total_ref[:D] + total_ref[D:]
    accum = accum_ref[...] + grad * grad
    accum_out[...] = accum
    table_out[...] = table_ref[...] - LEARN * grad / (jnp.sqrt(accum) + EPS)


def update(want, msgs, table_t, accum_t):
    rows = pl.BlockSpec((D, 512), lambda i: (0, i))
    return pl.pallas_call(
        update_kernel,
        grid=(OWNED // 512,),
        in_specs=[
            pl.BlockSpec((1, ALL_SLOTS), lambda i: (0, 0)),
            pl.BlockSpec((DEVS, MSG_ROWS, 128), lambda i: (0, 0, 0)),
            rows,
            rows,
        ],
        out_specs=(rows, rows),
        out_shape=(
            jax.ShapeDtypeStruct((D, OWNED), F32),
            jax.ShapeDtypeStruct((D, OWNED), F32),
        ),
        scratch_shapes=[
            pltpu.VMEM((2 * D, ALL_SLOTS), BF16),
            pltpu.VMEM((ALL_SLOTS, 128), I32),
            pltpu.VMEM((2 * D, 512), F32),
        ],
        compiler_params=params(60),
        cost_estimate=cost(4 * DP * OWNED * ALL_SLOTS, 10 << 20),
        name="update",
    )(want, msgs, table_t, accum_t)


def share_kernel(msg_ref, out_ref):
    def one(dev, total):
        coded = msg_ref[dev].astype(I32).astype(F32)
        return total + decode_share(coded[32 - SHARE_ROWS :])

    total = lax.fori_loop(0, DEVS, one, jnp.zeros((SHARE_ROWS, 128), F32), unroll=16)
    coded = code_share(total).astype(I32).astype(jnp.int16)
    for dev in range(DEVS):
        out_ref[dev] = coded


def sum_shares(msgs):
    return pl.pallas_call(
        share_kernel,
        grid=(1,),
        in_specs=[pl.BlockSpec((DEVS, 32, 128), lambda i: (0, MSG_ROWS // 32 - 1, 0))],
        out_specs=pl.BlockSpec((DEVS, SHARE_ROWS, 128), lambda i: (0, 0, 0)),
        out_shape=jax.ShapeDtypeStruct((DEVS, SHARE_ROWS, 128), jnp.int16),
        compiler_params=params(),
        cost_estimate=cost(1 << 20, 2 << 20),
        name="sum_shares",
    )(msgs)


def spread_kernel(sum_ref, rel_ref, kernel_ref, conv_ref, fc_ref, flat_ref):
    for dev in range(DEVS):
        value = decode_share(sum_ref[dev].astype(I32).astype(F32))
        flat_ref[dev * SHARE : dev * SHARE + SHARE, :] = value[:SHARE]
    for i in range(D // 8):
        for j in range(11):
            tile = flat_ref[8 * (11 * i + j) : 8 * (11 * i + j) + 8, :]
            last = min(128, NREL - 128 * j)
            rel_ref[8 * i : 8 * i + 8, 128 * j : 128 * j + last] = tile[:, :last]
    small = flat_ref[SMALL_DEV * SHARE : SMALL_DEV * SHARE + 8, :]
    for k in range(10):
        at = CH * (k % 4)
        row = small[k // 4 : k // 4 + 1]
        row = (row if at == 0 else pltpu.roll(row, 128 - at, 1))[:, :CH]
        if k < 9:
            kernel_ref[k : k + 1, :] = row
        else:
            conv_ref[...] = row
    fc_ref[...] = jnp.concatenate([small[3:4], small[4:5]], axis=1)[:, :D]


def spread_sums(sums):
    return pl.pallas_call(
        spread_kernel,
        out_shape=(
            jax.ShapeDtypeStruct((D, NREL), F32),
            jax.ShapeDtypeStruct((9, CH), F32),
            jax.ShapeDtypeStruct((1, CH), F32),
            jax.ShapeDtypeStruct((1, D), F32),
        ),
        scratch_shapes=[pltpu.VMEM((DEVS * SHARE, 128), F32)],
        compiler_params=params(),
        cost_estimate=cost(1 << 20, 2 << 20),
        name="spread_sums",
    )(sums)


def transpose_kernel(weight_ref, out_ref):
    wide = jnp.concatenate(
        [weight_ref[...].astype(F32), jnp.zeros((256 - D, BAND), F32)], axis=0
    ).T
    out_ref[...] = wide[:, :D].astype(BF16)


def transpose_weight(weight_t):
    return pl.pallas_call(
        transpose_kernel,
        grid=(BANDS,),
        in_specs=[pl.BlockSpec((D, BAND), lambda i: (0, i))],
        out_specs=pl.BlockSpec((BAND, D), lambda i: (i, 0)),
        out_shape=jax.ShapeDtypeStruct((FEAT, D), BF16),
        compiler_params=params(),
        cost_estimate=cost(1 << 20, 9 << 20),
        name="transpose_weight",
    )(weight_t)


def relations_kernel(ids_ref, rel_ref, out_ref):
    rel = rel_ref[...]
    high = rel.astype(BF16).astype(F32)
    both = jnp.concatenate([high, rel - high], axis=0).astype(BF16)
    for e in range(0, N_EMB, 2):
        cols = slice(128 * e, 128 * e + 256)
        row = lax.broadcasted_iota(I32, (RELP, 256), 0)
        hot = jnp.where(row == ids_ref[:, cols], 1.0, 0.0).astype(BF16)
        out_ref[:, cols] = dot(both, hot).astype(BF16)


def group_relations(ids, relations_t):
    return pl.pallas_call(
        relations_kernel,
        out_shape=jax.ShapeDtypeStruct((2 * D, N_EMB * TRIPS), BF16),
        compiler_params=params(),
        cost_estimate=cost(4 * D * RELP * N_EMB * TRIPS, 3 << 20),
        name="group_relations",
    )(ids, relations_t)


def projection_kernel(start_ref, group_ref, rel_ref, taps_ref, out_ref, high_ref, low_ref):
    start = pl.multiple_of((start_ref[0] >> 1) * STEP, 8)
    odd = (start_ref[0] & 1) == 1
    blank = jnp.zeros((24, 256), F32)
    total = jnp.zeros((CHUNK, D), F32)
    for e in range(0, N_EMB, 2):
        cols = slice(128 * e, 128 * e + 256)
        group = jnp.concatenate([group_ref[e], group_ref[e + 1]], axis=1).astype(F32)
        head = group[:CHUNK_WIN]
        rel = rel_ref[:, cols].astype(F32)
        high_ref[...] = jnp.concatenate([jnp.zeros((D, 256), F32), rel[:D], blank], axis=0)
        low_ref[...] = jnp.concatenate([jnp.zeros((D, 256), F32), rel[D:], blank], axis=0)
        high = high_ref[pl.ds(start, 104), :]
        high = head + jnp.where(odd, high[IMG_W : IMG_W + CHUNK_WIN], high[:CHUNK_WIN])
        low = low_ref[pl.ds(start, 104), :]
        low = jnp.where(odd, low[IMG_W : IMG_W + CHUNK_WIN], low[:CHUNK_WIN])
        rest = (128 - CHUNK_WIN, 256)
        ones, none = jnp.ones(rest, F32), jnp.zeros(rest, F32)
        stack = jnp.concatenate([high, ones, low, none, high, none], axis=0).astype(BF16)
        conv = dot(taps_ref[...], stack)
        feat = (conv * sigmoid(conv)).astype(BF16)
        total = total + dot_nt(feat, group[CHUNK_WIN:].astype(BF16))
    for s in range(N_SCORE):
        out_ref[s] = total[OWN_FEAT * s : OWN_FEAT * s + OWN_FEAT]


def projection(start, groups, rels, taps):
    vmem = pl.BlockSpec(memory_space=pltpu.VMEM)
    return pl.pallas_call(
        projection_kernel,
        in_specs=[pl.BlockSpec(memory_space=pltpu.SMEM), vmem, vmem, vmem],
        out_specs=vmem,
        out_shape=jax.ShapeDtypeStruct((N_SCORE, OWN_FEAT, D), F32),
        scratch_shapes=[pltpu.VMEM((2 * D + 24, 256), F32), pltpu.VMEM((2 * D + 24, 256), F32)],
        compiler_params=params(),
        cost_estimate=cost(2 * FEAT * TRIPS * 640, 4 << 20),
        name="projection",
    )(start, groups, rels, taps)


def exchange(x, axes):
    return lax.all_to_all(x, axes, split_axis=0, concat_axis=0, tiled=True)


def high_part(x):
    return x.astype(BF16).astype(F32)


def taps_kernel(place_ref, small_ref, offset_ref, taps_ref, spread_ref, chunk_ref, twice_ref, all_ref):
    columns = small_ref[...].T
    twice_ref[0:CH, :] = columns[:CH]
    twice_ref[CH : 2 * CH, :] = columns[:CH]
    columns = columns[:CH]

    def one_of(codes, columns):
        value = jnp.zeros(codes.shape, F32)
        for k, offset in enumerate(OFFSETS):
            value = jnp.where(codes == offset, columns[:, k : k + 1], value)
        return value

    def bias_parts(columns):
        bias = columns[:, 9:10]
        first = high_part(bias)
        second = high_part(bias - first)
        return first, second, bias - first - second

    for g in range(BAND // CH):
        at = slice(CH * g, CH * g + CH)
        codes = offset_ref[at]
        low = codes >= LOW - 1
        value = one_of(jnp.where(low, codes - LOW, codes), columns)
        value = jnp.where(low, value - high_part(value), value)
        for part, column in enumerate(bias_parts(columns)):
            value = jnp.where(codes == BIAS_MARK + part, column, value)
        all_ref[at, :] = value
    whole = all_ref[...]
    taps_ref[...] = whole.astype(BF16)
    high = whole[:, :128].T[:WIN]
    low = pltpu.roll(whole, 256 - 2 * WIN, 1)[:, :128].T[:WIN]
    spread_ref[...] = jnp.concatenate([high, low], axis=0).astype(BF16)

    first = place_ref[0] * CHUNK
    base = place_ref[1] * IMG_W
    columns = twice_ref[pl.ds(pl.multiple_of((place_ref[0] % 4) * 8, 8), CH), :]
    parts = bias_parts(columns)
    lane = lax.broadcasted_iota(I32, (CH, 128), 1)
    for g in range(CHUNK // CH + 1):
        size = min(CH, CHUNK - CH * g)
        feature = lax.broadcasted_iota(I32, (CH, 128), 0) + (first + CH * g)
        place = feature >> 5
        row = ((place.astype(F32) + 0.5) * (1.0 / OUT_W)).astype(I32)
        origin = row * IMG_W + (place - row * OUT_W) - base
        value = jnp.where(lane < CHUNK_WIN, one_of(lane - origin, columns), 0.0)
        high = high_part(value)
        biased = high
        for part in range(3):
            biased = jnp.where(lane == CHUNK_WIN + part, parts[part], biased)
        whole = jnp.concatenate([biased, high, value - high], axis=1).astype(BF16)
        chunk_ref[CH * g : CH * g + size, :] = whole[:size]


def build_taps(place, small, offsets):
    vmem = pl.BlockSpec(memory_space=pltpu.VMEM)
    return pl.pallas_call(
        taps_kernel,
        in_specs=[pl.BlockSpec(memory_space=pltpu.SMEM), vmem, vmem],
        out_specs=(vmem,) * 3,
        out_shape=(
            jax.ShapeDtypeStruct((BAND, 256), BF16),
            jax.ShapeDtypeStruct((2 * WIN, BAND), BF16),
            jax.ShapeDtypeStruct((CHUNK, 384), BF16),
        ),
        scratch_shapes=[pltpu.VMEM((2 * CH, 128), F32), pltpu.VMEM((BAND, 256), F32)],
        compiler_params=params(),
        cost_estimate=cost(1 << 20, 3 << 20),
        name="build_taps",
    )(place, small, offsets)


def shards(
    table,
    accum,
    request,
    head_slot,
    rel_ids,
    tail_slot,
    relations,
    kernel,
    conv_bias,
    fc_weight,
    fc_bias,
):
    table_t = table.T
    asked = jnp.concatenate(
        [
            request[0],
            jnp.zeros((DEVS, SLOTS), I32),
            jnp.broadcast_to(rel_ids[None], (DEVS, TRIPS)),
        ],
        axis=1,
    )
    asked, rounded = lax.optimization_barrier((exchange(asked, AXES), round_table(table_t)))
    want = asked[:, :SLOTS].reshape(1, ALL_SLOTS)
    group = asked[:, 128:].reshape(N_EMB, N_SCORE, TRIPS)
    group = lax.dynamic_index_in_dim(group, lax.axis_index("score"), 1, keepdims=False)
    outgoing = gather_rows(want, rounded)
    incoming = exchange(outgoing, AXES)

    tails = jnp.pad(tail_slot, ((0, 0), (0, 128 - CAND)), constant_values=-1)
    counts = count_tails(tails)
    hot = (jnp.arange(NREL, dtype=I32)[:, None] == rel_ids[None, :]).astype(F32)
    rel_t = jnp.dot(relations.T, hot, precision=lax.Precision.HIGHEST)
    emb = lax.axis_index("emb")
    start = window_start(emb)
    small = jnp.concatenate([kernel, conv_bias[None]], axis=0)
    small = jnp.pad(small, ((0, 118), (0, 128 - CH)))
    offsets = jnp.asarray(offset_map())
    taps, spread, chunk_taps = build_taps(jnp.stack([emb, start]), small, offsets)
    weight = transpose_weight(fc_weight.T)
    rels = group_relations(
        group.reshape(1, N_EMB * TRIPS), jnp.pad(relations.T, ((0, 0), (0, RELP - NREL)))
    )
    true_row = tail_slot[:, :1].T
    head_row = head_slot[None, :]
    ready = (counts, rel_t, taps, spread, chunk_taps, weight, rels, true_row)
    incoming, ready = lax.optimization_barrier((incoming, ready))
    counts, rel_t, taps, spread, chunk_taps, weight, rels, true_row = ready

    part, send, state = front(
        incoming, head_row, rel_t, taps, fc_weight.T, counts, true_row, fc_bias[None, :]
    )
    groups = exchange(send, "emb")
    returned = exchange(
        back(state, taps, spread, weight, offsets, part, rel_ids[None, :], head_row), AXES
    )

    halves = projection(start.reshape(1), groups, rels, chunk_taps)
    halves = halves.reshape(N_SCORE // 2, 2, OWN_FEAT, D)
    here = lax.axis_index("score")
    side = here & 1
    kept = lax.dynamic_index_in_dim(halves, side, 1, keepdims=False)
    sent = lax.dynamic_index_in_dim(halves, 1 - side, 1, keepdims=False)
    left = kept + lax.ppermute(sent, "score", [(i, i ^ 1) for i in range(N_SCORE)])
    fc_grad = lax.dynamic_index_in_dim(left, here >> 1, 0, keepdims=False)
    for step in range(1, 4):
        sent = lax.dynamic_index_in_dim(left, (here >> 1) ^ step, 0, keepdims=False)
        pairs = [(i, i ^ (2 * step)) for i in range(N_SCORE)]
        fc_grad = fc_grad + lax.ppermute(sent, "score", pairs)

    sums = exchange(sum_shares(returned), AXES)
    new_table, new_accum = update(want, returned, table_t, accum.T)
    rel_sum, kernel_sum, conv_sum, fc_sum = spread_sums(sums)
    return (
        new_table.T,
        new_accum.T,
        fc_grad,
        kernel_sum,
        conv_sum[0],
        fc_sum[0],
        rel_sum.T,
    )


def solution(mesh):
    rows = P(AXES, None)
    in_specs = (rows, rows, P(AXES, None, None), P(AXES), P(AXES), rows) + (P(),) * 5
    out_specs = (rows, rows, rows) + (P(),) * 4
    return jax.shard_map(shards, mesh=mesh, in_specs=in_specs, out_specs=out_specs, check_vma=False)
```

```python
import jax
import jax.numpy as jnp
import numpy as np
from jax import lax
from jax.experimental import pallas as pl
from jax.experimental.pallas import tpu as pltpu
from jax.sharding import PartitionSpec as P

AXES = ("emb", "score")
DEVS = 128
N_EMB = 16
N_SCORE = 8
SLOTS = 64
ALL_SLOTS = DEVS * SLOTS
OWNED = 2048
D = 200
DP = 208
HALF = DP // 2
TRIPS = 128
CAND = 65
IMG_W = 20
OUT_W = 18
CH = 32
FEAT = 10368
BAND = 1152
BANDS = 9
WIN = 80
STEP = 40
NREL = 1345
RELP = 1408
REL_ROWS = 200 * 11
SHARE = 18
SHARE_ROWS = 24
SMALL_DEV = 124
MSG_ROWS = HALF + SHARE_ROWS
CHUNK = FEAT // N_EMB
OWN_FEAT = FEAT // DEVS
CHUNK_WIN = 80
LEARN = 0.1
EPS = 1e-10
F32 = jnp.float32
BF16 = jnp.bfloat16
I32 = jnp.int32
NT = (((1,), (1,)), ((), ()))
FILL = 0.9999

OFFSETS = [20 * a + b for a in range(3) for b in range(3)]
BIAS_MARK = 500
LOW = 1000


def offset_map():
    feature = np.arange(BAND)
    place = feature // CH
    origin = (place // OUT_W) * IMG_W + place % OUT_W
    lane = np.arange(256)
    offset = lane[None, :] % WIN - origin[:, None]
    offset = np.where((offset >= 0) & (offset < 43), offset, -1)
    offset = np.where(lane[None, :] < 2 * WIN, offset, offset + LOW)
    for part in range(16):
        offset[:, 3 * WIN + part] = BIAS_MARK + part
    return offset.astype(np.int32)


def window_start(emb):
    return emb * CHUNK // (OUT_W * CH)


def params(mib=40):
    return pltpu.CompilerParams(vmem_limit_bytes=mib << 20)


VMEM_SPEC = pl.BlockSpec()
HBM_SPEC = pl.BlockSpec(memory_space=pltpu.HBM)
ANY_SPEC = pl.BlockSpec(memory_space=pl.ANY)
AT_QUERY = 2 * D
AT_BIAS = AT_QUERY + DP
AT_DPRE = AT_BIAS + 16
STATE = AT_DPRE + D
GROUP = CHUNK_WIN + D


def cost(flops, moved):
    return pl.CostEstimate(flops=flops, bytes_accessed=moved, transcendentals=0)


def dot(a, b):
    return jnp.dot(a, b, preferred_element_type=F32)


def dot_nt(a, b):
    return lax.dot_general(a, b, NT, preferred_element_type=F32)


def split(x):
    high = x.astype(BF16)
    low = (x - high.astype(F32)).astype(BF16)
    return high, low


def sigmoid(value):
    return 0.5 * jnp.tanh(0.5 * value) + 0.5


def silu_slope(value):
    sig = sigmoid(value)
    return sig * (1.0 + value * (1.0 - sig))


def as_column(row):
    return jnp.broadcast_to(row, (128, row.shape[1])).T


def to_messages(x):
    top, bottom = x[:HALF], x[HALF:]
    left = lax.broadcasted_iota(I32, (HALF, 128), 1) < SLOTS
    first = jnp.where(left, top, pltpu.roll(bottom, SLOTS, 1))
    second = jnp.where(left, pltpu.roll(top, SLOTS, 1), bottom)
    return first, second


def from_messages(first, second):
    left = lax.broadcasted_iota(I32, (HALF, 128), 1) < SLOTS
    top = jnp.where(left, first, pltpu.roll(second, SLOTS, 1))
    bottom = jnp.where(left, pltpu.roll(first, SLOTS, 1), second)
    return jnp.concatenate([top, bottom], axis=0)


def code_share(x):
    most = jnp.max(jnp.abs(x), axis=0, keepdims=True)
    power = jnp.clip(jnp.ceil(jnp.log2(jnp.maximum(most, 1e-30))), -90.0, 90.0)
    scaled = x * (jnp.exp2(15.0 - power) * FILL)
    fixed = jnp.floor(scaled + 0.5)
    rest = jnp.floor((scaled - fixed) * 16384.0 + 0.5)
    row = lax.broadcasted_iota(I32, (SHARE_ROWS, 128), 0)
    tail = jnp.where(row == SHARE, power, pltpu.roll(rest, SHARE + 1, 0))
    return jnp.where(row < SHARE, fixed, tail)


def decode_share(coded):
    row = lax.broadcasted_iota(I32, (SHARE_ROWS, 128), 0)
    rest = pltpu.roll(coded, SHARE_ROWS - SHARE - 1, 0) * (1.0 / 16384.0)
    first = SHARE_ROWS - SHARE - 1
    value = coded + jnp.where(row < first, rest, 0.0)
    return jnp.where(row < SHARE, value, 0.0) * (jnp.exp2(coded[SHARE : SHARE + 1] - 15.0) * (1.0 / FILL))


def rounded_kernel(table_ref, out_ref):
    out_ref[...] = jnp.concatenate(
        [table_ref[...], jnp.zeros((DP - D, 512), F32)], axis=0
    ).astype(BF16)


def round_table(table_t):
    return pl.pallas_call(
        rounded_kernel,
        grid=(4,),
        in_specs=[pl.BlockSpec((D, 512), lambda i: (0, i))],
        out_specs=pl.BlockSpec((DP, 512), lambda i: (0, i)),
        out_shape=jax.ShapeDtypeStruct((DP, OWNED), BF16),
        compiler_params=params(60),
        cost_estimate=cost(1 << 20, 3 << 20),
        name="round_table",
    )(table_t)


def gather_kernel(want_ref, table_ref, out_ref, rows, outs, sems):
    table_copy = pltpu.make_async_copy(table_ref, rows, sems.at[4])
    table_copy.start()
    table_copy.wait()

    def out_copy(i):
        at = pl.ds(i * 32, 32)
        return pltpu.make_async_copy(outs.at[at], out_ref.at[at], sems.at[i])

    def block(i, carry):
        for q in range(8):
            want = want_ref[:, pl.ds(pl.multiple_of(i * 2048 + 256 * q, 256), 256)]
            total = jnp.zeros((DP, 256), F32)
            for kb in range(OWNED // 256):
                row = lax.broadcasted_iota(I32, (256, 256), 0) + 256 * kb
                hot = jnp.where(row == want, 1.0, 0.0).astype(BF16)
                total = total + dot(rows[:, 256 * kb : 256 * kb + 256], hot)
            for half in range(2):
                first, second = to_messages(total[:, 128 * half : 128 * half + 128])
                outs[32 * i + 4 * q + 2 * half] = first.astype(BF16)
                outs[32 * i + 4 * q + 2 * half + 1] = second.astype(BF16)
        out_copy(i).start()
        return carry

    lax.fori_loop(0, 4, block, 0, unroll=True)
    for i in range(4):
        out_copy(i).wait()


def gather_rows(want, table_t):
    return pl.pallas_call(
        gather_kernel,
        in_specs=[VMEM_SPEC, HBM_SPEC],
        out_specs=HBM_SPEC,
        out_shape=jax.ShapeDtypeStruct((DEVS, HALF, 128), BF16),
        scratch_shapes=[
            pltpu.VMEM((DP, OWNED), BF16),
            pltpu.VMEM((DEVS, HALF, 128), BF16),
            pltpu.SemaphoreType.DMA((5,)),
        ],
        compiler_params=params(60),
        cost_estimate=cost(2 * DP * OWNED * ALL_SLOTS, 6 << 20),
        name="gather_rows",
    )(want, table_t)


def counts_kernel(tail_ref, out_ref, buf_ref):
    high_row = lax.broadcasted_iota(I32, (64, 128), 0)
    low_row = lax.broadcasted_iota(I32, (128, 128), 0)

    def one(t, carry):
        slot = tail_ref[pl.ds(t, 1), :]
        high = jnp.where(high_row == (slot >> 7), 1.0, 0.0).astype(BF16)
        low = jnp.where(low_row == (slot & 127), 1.0, 0.0).astype(BF16)
        buf_ref[pl.ds(pl.multiple_of(t * 64, 64), 64), :] = dot_nt(high, low)
        return carry

    lax.fori_loop(0, TRIPS, one, 0, unroll=8)
    for high in range(64):
        out_ref[:, 128 * high : 128 * high + 128] = buf_ref[
            pl.ds(high, TRIPS, stride=64), :
        ].astype(BF16)


def count_tails(tails):
    return pl.pallas_call(
        counts_kernel,
        out_shape=jax.ShapeDtypeStruct((TRIPS, ALL_SLOTS), BF16),
        scratch_shapes=[pltpu.VMEM((ALL_SLOTS, 128), F32)],
        compiler_params=params(),
        cost_estimate=cost(TRIPS * 2 * 64 * 128 * 128, 2 << 20),
        name="count_tails",
    )(tails)


def window_parts(image_ref, p):
    win = image_ref[pl.ds(pl.multiple_of(p * STEP, 8), WIN), :]
    high = win.astype(BF16).astype(F32)
    ones = jnp.ones((256 - 3 * WIN, TRIPS), F32)
    return high, win - high, ones


def front_kernel(
    msg_ref, head_ref, rel_ref, taps_ref, weight_ref, count_ref, true_ref, bias_ref,
    part_ref, send_ref, state_ref,
    msgs, heads, taps, weights, counts, trues, biases, parts, rows_t, own, state, sems,
):
    def msg_copy(i):
        at = pl.ds(i * 32, 32)
        return pltpu.make_async_copy(msg_ref.at[at], msgs.at[at], sems.at[i])

    def part_copy(i):
        cols = pl.ds(pl.multiple_of(i * 2048, 2048), 2048)
        return pltpu.make_async_copy(parts.at[:, cols], part_ref.at[:, cols], sems.at[4 + i])

    rel_at = state.at[pl.ds(D, D)]
    pairs = [(head_ref, heads), (rel_ref, rel_at), (taps_ref, taps), (weight_ref, weights)]
    pairs += [(bias_ref, biases), (true_ref, trues), (count_ref, counts)]
    loads = [pltpu.make_async_copy(a, b, sems.at[8 + k]) for k, (a, b) in enumerate(pairs)]
    loads[0].start()
    for i in range(4):
        msg_copy(i).start()
    for load in loads[1:]:
        load.start()
    loads[0].wait()

    def unpack(i, head):
        msg_copy(i).wait()
        for k in range(8):
            both = []
            for pair in (16 * i + 2 * k, 16 * i + 2 * k + 1):
                first = msgs[2 * pair].astype(F32)
                second = msgs[2 * pair + 1].astype(F32)
                both.append(from_messages(first, second))
            both = jnp.concatenate(both, axis=1).astype(BF16)
            base = pl.multiple_of(i * 2048 + k * 256, 256)
            rows_t[:, pl.ds(base, 256)] = both
            slot = lax.broadcasted_iota(I32, (256, TRIPS), 0) + base
            hot = jnp.where(slot == heads[...], 1.0, 0.0).astype(BF16)
            head = head + dot(both, hot)
        return head

    head = lax.fori_loop(0, 4, unpack, jnp.zeros((DP, TRIPS), F32))
    state[0:D, :] = head[:D]

    for load in loads[1:4]:
        load.wait()
    pre = jnp.zeros((D, TRIPS), F32)
    for p in range(BANDS):
        high, low, ones = window_parts(state, p)
        stack = jnp.concatenate([high, low, high, ones], axis=0).astype(BF16)
        conv = dot(taps[...], stack)
        feat = (conv * sigmoid(conv)).astype(BF16)
        pre = pre + dot(weights[:, p * BAND : p * BAND + BAND], feat)

    for load in loads[4:]:
        load.wait()
    bias = jnp.concatenate([biases[...], jnp.zeros((1, 256 - D), F32)], axis=1)
    pre = pre + as_column(bias)[:D]
    true = as_column(trues[...])
    true = jnp.concatenate([true, true], axis=1)
    query = pre * sigmoid(pre)
    pad = jnp.zeros((DP - D, TRIPS), F32)
    query = jnp.concatenate([query, pad], axis=0)
    state[AT_QUERY:AT_BIAS, :] = query
    wide = jnp.concatenate([query, jnp.zeros((256 - DP, TRIPS), F32)], axis=0).T[:, :DP]
    high = wide.astype(BF16).astype(F32)
    both = jnp.concatenate([high, wide - high], axis=0).astype(BF16)

    def block(i, total):
        for k in range(8):
            base = pl.multiple_of(i * 2048 + k * 256, 256)
            cols = pl.ds(base, 256)
            rows = rows_t[:, cols]
            scores = dot(both, rows)
            scores = scores[:TRIPS] + scores[TRIPS:]
            lane = lax.broadcasted_iota(I32, (TRIPS, 256), 1) + base
            label = jnp.where(lane == true, 1.0, 0.0)
            grad = counts[:, cols].astype(F32) * sigmoid(scores) - label
            part = jnp.concatenate(split(grad), axis=0)
            parts[:, cols] = part
            total = total + dot_nt(rows, part)
        part_copy(i).start()
        return total

    total = lax.fori_loop(0, 4, block, jnp.zeros((DP, 256), F32), unroll=True)
    dquery = (total[:D, :TRIPS] + total[:D, TRIPS:]) * (1.0 / CAND)
    dpre = dquery * silu_slope(pre)
    total = jnp.concatenate(
        [jnp.sum(dpre, axis=1, keepdims=True), jnp.zeros((256 - D, 1), F32)], axis=0
    )
    total = jnp.broadcast_to(total, (256, 128)).T[:8]
    state[AT_BIAS:AT_DPRE, :] = jnp.concatenate([total[:, :128], total[:, 128:]], axis=0)
    state[AT_DPRE:, :] = dpre
    head = jnp.concatenate([head[:D], jnp.zeros((D + 32, TRIPS), F32)], axis=0)
    for e in range(N_EMB):
        at = window_start(e) * IMG_W
        own[e] = jnp.concatenate([head[at : at + CHUNK_WIN], dpre], axis=0).astype(BF16)
    sends = [pltpu.make_async_copy(own, send_ref, sems.at[15])]
    sends.append(pltpu.make_async_copy(state, state_ref, sems.at[16]))
    for send in sends:
        send.start()
    for send in sends:
        send.wait()
    for i in range(4):
        part_copy(i).wait()


def front(msgs, head_row, rel_t, taps, weight_t, counts, true_row, bias_row):
    return pl.pallas_call(
        front_kernel,
        in_specs=[ANY_SPEC] + [HBM_SPEC] * 7,
        out_specs=(HBM_SPEC,) * 3,
        out_shape=(
            jax.ShapeDtypeStruct((2 * TRIPS, ALL_SLOTS), BF16),
            jax.ShapeDtypeStruct((N_EMB, GROUP, TRIPS), BF16),
            jax.ShapeDtypeStruct((STATE, TRIPS), F32),
        ),
        scratch_shapes=[
            pltpu.VMEM((DEVS, HALF, 128), BF16),
            pltpu.VMEM((1, TRIPS), I32),
            pltpu.VMEM((BAND, 256), BF16),
            pltpu.VMEM((D, FEAT), BF16),
            pltpu.VMEM((TRIPS, ALL_SLOTS), BF16),
            pltpu.VMEM((1, TRIPS), I32),
            pltpu.VMEM((1, D), F32),
            pltpu.VMEM((2 * TRIPS, ALL_SLOTS), BF16),
            pltpu.VMEM((DP, ALL_SLOTS), BF16),
            pltpu.VMEM((N_EMB, GROUP, TRIPS), BF16),
            pltpu.VMEM((STATE, TRIPS), F32),
            pltpu.SemaphoreType.DMA((17,)),
        ],
        compiler_params=params(57),
        cost_estimate=cost(8 * 256 * DP * ALL_SLOTS, 20 << 20),
        name="front",
    )(msgs, head_row, rel_t, taps, weight_t, counts, true_row, bias_row)


def back_kernel(
    state_ref, taps_ref, spread_ref, weight_ref, offset_ref, part_ref, rel_ref, head_ref,
    out_ref,
    state, taps, spreads, weights, offsets, parts, outs, shares, dimage_ref, grad_ref, flat_ref,
    sems,
):
    def weight_copy(i):
        at = pl.ds(pl.multiple_of(i * 3 * BAND, BAND), 3 * BAND)
        return pltpu.make_async_copy(weight_ref.at[at], weights.at[at], sems.at[i])

    def out_copy(i):
        at = pl.ds(i * 32, 32)
        return pltpu.make_async_copy(outs.at[at], out_ref.at[at], sems.at[3 + i])

    pairs = [(state_ref, state), (taps_ref, taps), (spread_ref, spreads)]
    pairs += [(offset_ref, offsets), (part_ref, parts)]
    loads = [pltpu.make_async_copy(a, b, sems.at[7 + k]) for k, (a, b) in enumerate(pairs)]
    for load in loads[:2]:
        load.start()
    weight_copy(0).start()
    loads[2].start()
    for i in range(1, 3):
        weight_copy(i).start()
    for load in loads[3:]:
        load.start()
    for load in loads[:3]:
        load.wait()

    dimage_ref[...] = jnp.zeros_like(dimage_ref)
    grad_ref[...] = jnp.zeros_like(grad_ref)
    dpre = state[AT_DPRE:, :].astype(BF16)

    def bands(i, carry):
        weight_copy(i).wait()
        for k in range(3):
            p = 3 * i + k
            high, low, ones = window_parts(state, p)
            stack = jnp.concatenate([high, low, high, ones], axis=0).astype(BF16)
            none = jnp.zeros_like(low)
            stack_high = jnp.concatenate([high, none, high, ones], axis=0).astype(BF16)
            conv = dot(taps[...], stack)
            weight = weights[pl.ds(pl.multiple_of(p * BAND, BAND), BAND), :]
            dfeat = dot(weight, dpre)
            dconv = jnp.concatenate(split(dfeat * silu_slope(conv)), axis=1)
            grad_ref[...] += dot_nt(dconv, jnp.concatenate([stack, stack_high], axis=1))
            spread = dot(spreads[...], dconv)
            spread = spread[:WIN] + spread[WIN:]
            spread = spread[:, :TRIPS] + spread[:, TRIPS:]
            dimage_ref[pl.ds(pl.multiple_of(p * STEP, 8), WIN), :] += spread
        return carry

    lax.fori_loop(0, 3, bands, 0)
    for load in loads[3:]:
        load.wait()

    drel = dimage_ref[D : 2 * D, :]
    high = drel.astype(BF16).astype(F32)
    both = jnp.concatenate([high, drel - high], axis=0).astype(BF16)
    rel = as_column(rel_ref[...])
    for j in range(RELP // 128):
        lane = lax.broadcasted_iota(I32, (TRIPS, 128), 1) + 128 * j
        hot = jnp.where(lane == rel, 1.0, 0.0).astype(BF16)
        part = dot(both, hot)
        part = part[:D] + part[D:]
        for i in range(D // 8):
            tile = 11 * i + j
            flat_ref[8 * tile : 8 * tile + 8, :] = part[8 * i : 8 * i + 8]

    lane = lax.broadcasted_iota(I32, (CH, 128), 1)
    totals = [jnp.zeros((CH, 128), F32) for _ in range(10)]
    for g in range(BAND // CH):
        at = slice(CH * g, CH * g + CH)
        whole = grad_ref[at]
        both = whole[:, :128] + pltpu.roll(whole, 256 - WIN, 1)[:, :128]
        mark = offsets[at, 0:128]
        for k, offset in enumerate(OFFSETS):
            here = (mark == offset) & (lane < WIN)
            totals[k] = totals[k] + jnp.where(here, both, 0.0)
        totals[9] = totals[9] + jnp.where(lane == 3 * WIN - 128, whole[:, 128:], 0.0)
    small = jnp.zeros((CH, 128), F32)
    for k in range(10):
        small = jnp.where(lane == k, jnp.sum(totals[k], axis=1, keepdims=True), small)
    small = jnp.concatenate([small, jnp.zeros((128 - CH, 128), F32)], axis=0).T[:16]
    row = lax.broadcasted_iota(I32, (8, 128), 0)
    lane = lax.broadcasted_iota(I32, (8, 128), 1)
    tail = jnp.zeros((8, 128), F32)
    for k in range(10):
        at = CH * (k % 4)
        moved = small[k : k + 1] if at == 0 else pltpu.roll(small[k : k + 1], at, 1)
        here = (row == k // 4) & (lane >= at) & (lane < at + CH)
        tail = jnp.where(here, moved, tail)
    tail = jnp.where(row == 3, state[AT_BIAS : AT_BIAS + 1, :], tail)
    tail = jnp.where(row == 4, state[AT_BIAS + 8 : AT_BIAS + 9, :], tail)

    flat_ref[REL_ROWS:, :] = jnp.zeros((DEVS * SHARE - REL_ROWS, 128), F32)
    flat_ref[SMALL_DEV * SHARE : SMALL_DEV * SHARE + 8, :] = tail
    blank = jnp.zeros((SHARE_ROWS - SHARE, 128), F32)
    for dev in range(DEVS):
        mine = flat_ref[dev * SHARE : dev * SHARE + SHARE, :]
        shares[dev] = jnp.concatenate([mine, blank], axis=0)

    owner = as_column(head_ref[...])
    owner = jnp.concatenate([owner, owner], axis=1)
    q_high, q_low = split(state[AT_QUERY:AT_BIAS, :] * (1.0 / CAND))
    dhead = jnp.concatenate([dimage_ref[0:D, :], jnp.zeros((DP - D, TRIPS), F32)], axis=0)
    left = jnp.concatenate([q_high, q_low, q_high, *split(dhead)], axis=1)

    def slots(nb):
        base = pl.multiple_of(nb * 256, 256)
        cols = pl.ds(base, 256)
        high = parts[0:TRIPS, cols]
        low = parts[TRIPS:, cols]
        lane = lax.broadcasted_iota(I32, (TRIPS, 256), 1) + base
        hot = jnp.where(lane == owner, 1.0, 0.0).astype(BF16)
        grad = dot(left, jnp.concatenate([high, high, low, hot, hot], axis=0))
        most = jnp.max(jnp.abs(grad), axis=0, keepdims=True)
        power = jnp.clip(jnp.ceil(jnp.log2(jnp.maximum(most, 1e-30))), -90.0, 90.0)
        fixed = jnp.floor(grad * (jnp.exp2(15.0 - power) * FILL) + 0.5)
        row = lax.broadcasted_iota(I32, (DP, 256), 0)
        fixed = jnp.where(row == D, power, fixed)
        for half in range(2):
            pair = to_messages(fixed[:, 128 * half : 128 * half + 128])
            for k in range(2):
                dev = 4 * nb + 2 * half + k
                whole = jnp.concatenate([pair[k], code_share(shares[dev])], axis=0)
                outs[dev] = whole.astype(I32).astype(jnp.int16)

    def chunk(i, carry):
        for k in range(8):
            slots(8 * i + k)
        out_copy(i).start()
        return carry

    lax.fori_loop(0, 4, chunk, 0, unroll=True)
    for i in range(4):
        out_copy(i).wait()


def back(state, taps, spread, weight, offsets, part, rel_row, head_row):
    return pl.pallas_call(
        back_kernel,
        in_specs=[HBM_SPEC] * 6 + [VMEM_SPEC] * 2,
        out_specs=HBM_SPEC,
        out_shape=jax.ShapeDtypeStruct((DEVS, MSG_ROWS, 128), jnp.int16),
        scratch_shapes=[
            pltpu.VMEM((STATE, TRIPS), F32),
            pltpu.VMEM((BAND, 256), BF16),
            pltpu.VMEM((2 * WIN, BAND), BF16),
            pltpu.VMEM((FEAT, D), BF16),
            pltpu.VMEM((BAND, 256), I32),
            pltpu.VMEM((2 * TRIPS, ALL_SLOTS), BF16),
            pltpu.VMEM((DEVS, MSG_ROWS, 128), jnp.int16),
            pltpu.VMEM((DEVS, SHARE_ROWS, 128), F32),
            pltpu.VMEM((2 * D, TRIPS), F32),
            pltpu.VMEM((BAND, 256), F32),
            pltpu.VMEM((DEVS * SHARE, 128), F32),
            pltpu.SemaphoreType.DMA((12,)),
        ],
        compiler_params=params(60),
        cost_estimate=cost(8 * 256 * FEAT * TRIPS, 20 << 20),
        name="back",
    )(state, taps, spread, weight, offsets, part, rel_row, head_row)


def update_kernel(
    want_ref, msg_ref, table_ref, accum_ref, table_out, accum_out, part_ref, column_ref, total_ref
):
    nb = pl.program_id(0)

    def unpack(pair):
        cols = slice(pair * 128, pair * 128 + 128)
        fixed = from_messages(
            msg_ref[2 * pair].astype(I32).astype(F32)[:HALF],
            msg_ref[2 * pair + 1].astype(I32).astype(F32)[:HALF],
        )
        grad = fixed * (jnp.exp2(fixed[D : D + 1] - 15.0) * (1.0 / FILL))
        high = high_part(grad[:D])
        part_ref[:, cols] = jnp.concatenate([high, grad[:D] - high], axis=0).astype(BF16)
        column_ref[cols, :] = as_column(want_ref[:, cols])

    def block(kb):
        slots = slice(kb * 2048, kb * 2048 + 2048)
        lane = lax.broadcasted_iota(I32, (2048, 128), 1) + nb * 512
        column = column_ref[slots, :]
        hot = [jnp.where(column == lane + 128 * k, 1.0, 0.0).astype(BF16) for k in range(4)]
        return dot(part_ref[:, slots], jnp.concatenate(hot, axis=1))

    @pl.when(nb == 0)
    def _():
        total = jnp.zeros((2 * D, 512), F32)
        for kb in range(4):
            for pair in range(16):
                unpack(16 * kb + pair)
            total = total + block(kb)
        total_ref[...] = total

    @pl.when(nb > 0)
    def _():
        total = jnp.zeros((2 * D, 512), F32)
        for kb in range(4):
            total = total + block(kb)
        total_ref[...] = total

    grad = total_ref[:D] + total_ref[D:]
    accum = accum_ref[...] + grad * grad
    accum_out[...] = accum
    table_out[...] = table_ref[...] - LEARN * grad / (jnp.sqrt(accum) + EPS)


def update(want, msgs, table_t, accum_t):
    rows = pl.BlockSpec((D, 512), lambda i: (0, i))
    return pl.pallas_call(
        update_kernel,
        grid=(OWNED // 512,),
        in_specs=[
            pl.BlockSpec((1, ALL_SLOTS), lambda i: (0, 0)),
            pl.BlockSpec((DEVS, MSG_ROWS, 128), lambda i: (0, 0, 0)),
            rows,
            rows,
        ],
        out_specs=(rows, rows),
        out_shape=(
            jax.ShapeDtypeStruct((D, OWNED), F32),
            jax.ShapeDtypeStruct((D, OWNED), F32),
        ),
        scratch_shapes=[
            pltpu.VMEM((2 * D, ALL_SLOTS), BF16),
            pltpu.VMEM((ALL_SLOTS, 128), I32),
            pltpu.VMEM((2 * D, 512), F32),
        ],
        compiler_params=params(60),
        cost_estimate=cost(4 * DP * OWNED * ALL_SLOTS, 10 << 20),
        name="update",
    )(want, msgs, table_t, accum_t)


def share_kernel(msg_ref, out_ref):
    def one(dev, total):
        coded = msg_ref[dev].astype(I32).astype(F32)
        return total + decode_share(coded[32 - SHARE_ROWS :])

    total = lax.fori_loop(0, DEVS, one, jnp.zeros((SHARE_ROWS, 128), F32), unroll=16)
    coded = code_share(total).astype(I32).astype(jnp.int16)
    for dev in range(DEVS):
        out_ref[dev] = coded


def sum_shares(msgs):
    return pl.pallas_call(
        share_kernel,
        grid=(1,),
        in_specs=[pl.BlockSpec((DEVS, 32, 128), lambda i: (0, MSG_ROWS // 32 - 1, 0))],
        out_specs=pl.BlockSpec((DEVS, SHARE_ROWS, 128), lambda i: (0, 0, 0)),
        out_shape=jax.ShapeDtypeStruct((DEVS, SHARE_ROWS, 128), jnp.int16),
        compiler_params=params(),
        cost_estimate=cost(1 << 20, 2 << 20),
        name="sum_shares",
    )(msgs)


def spread_kernel(sum_ref, rel_ref, kernel_ref, conv_ref, fc_ref, flat_ref):
    for dev in range(DEVS):
        value = decode_share(sum_ref[dev].astype(I32).astype(F32))
        flat_ref[dev * SHARE : dev * SHARE + SHARE, :] = value[:SHARE]
    for i in range(D // 8):
        for j in range(11):
            tile = flat_ref[8 * (11 * i + j) : 8 * (11 * i + j) + 8, :]
            last = min(128, NREL - 128 * j)
            rel_ref[8 * i : 8 * i + 8, 128 * j : 128 * j + last] = tile[:, :last]
    small = flat_ref[SMALL_DEV * SHARE : SMALL_DEV * SHARE + 8, :]
    for k in range(10):
        at = CH * (k % 4)
        row = small[k // 4 : k // 4 + 1]
        row = (row if at == 0 else pltpu.roll(row, 128 - at, 1))[:, :CH]
        if k < 9:
            kernel_ref[k : k + 1, :] = row
        else:
            conv_ref[...] = row
    fc_ref[...] = jnp.concatenate([small[3:4], small[4:5]], axis=1)[:, :D]


def spread_sums(sums):
    return pl.pallas_call(
        spread_kernel,
        out_shape=(
            jax.ShapeDtypeStruct((D, NREL), F32),
            jax.ShapeDtypeStruct((9, CH), F32),
            jax.ShapeDtypeStruct((1, CH), F32),
            jax.ShapeDtypeStruct((1, D), F32),
        ),
        scratch_shapes=[pltpu.VMEM((DEVS * SHARE, 128), F32)],
        compiler_params=params(),
        cost_estimate=cost(1 << 20, 2 << 20),
        name="spread_sums",
    )(sums)


def transpose_kernel(weight_ref, out_ref):
    wide = jnp.concatenate(
        [weight_ref[...].astype(F32), jnp.zeros((256 - D, BAND), F32)], axis=0
    ).T
    out_ref[...] = wide[:, :D].astype(BF16)


def transpose_weight(weight_t):
    return pl.pallas_call(
        transpose_kernel,
        grid=(BANDS,),
        in_specs=[pl.BlockSpec((D, BAND), lambda i: (0, i))],
        out_specs=pl.BlockSpec((BAND, D), lambda i: (i, 0)),
        out_shape=jax.ShapeDtypeStruct((FEAT, D), BF16),
        compiler_params=params(),
        cost_estimate=cost(1 << 20, 9 << 20),
        name="transpose_weight",
    )(weight_t)


def relations_kernel(ids_ref, rel_ref, out_ref):
    rel = rel_ref[...]
    high = rel.astype(BF16).astype(F32)
    both = jnp.concatenate([high, rel - high], axis=0).astype(BF16)
    for e in range(0, N_EMB, 2):
        cols = slice(128 * e, 128 * e + 256)
        row = lax.broadcasted_iota(I32, (RELP, 256), 0)
        hot = jnp.where(row == ids_ref[:, cols], 1.0, 0.0).astype(BF16)
        out_ref[:, cols] = dot(both, hot).astype(BF16)


def group_relations(ids, relations_t):
    return pl.pallas_call(
        relations_kernel,
        out_shape=jax.ShapeDtypeStruct((2 * D, N_EMB * TRIPS), BF16),
        compiler_params=params(),
        cost_estimate=cost(4 * D * RELP * N_EMB * TRIPS, 3 << 20),
        name="group_relations",
    )(ids, relations_t)


def projection_kernel(start_ref, group_ref, rel_ref, taps_ref, out_ref, high_ref, low_ref):
    start = pl.multiple_of((start_ref[0] >> 1) * STEP, 8)
    odd = (start_ref[0] & 1) == 1
    blank = jnp.zeros((24, 256), F32)
    total = jnp.zeros((CHUNK, D), F32)
    for e in range(0, N_EMB, 2):
        cols = slice(128 * e, 128 * e + 256)
        group = jnp.concatenate([group_ref[e], group_ref[e + 1]], axis=1).astype(F32)
        head = group[:CHUNK_WIN]
        rel = rel_ref[:, cols].astype(F32)
        high_ref[...] = jnp.concatenate([jnp.zeros((D, 256), F32), rel[:D], blank], axis=0)
        low_ref[...] = jnp.concatenate([jnp.zeros((D, 256), F32), rel[D:], blank], axis=0)
        high = high_ref[pl.ds(start, 104), :]
        high = head + jnp.where(odd, high[IMG_W : IMG_W + CHUNK_WIN], high[:CHUNK_WIN])
        low = low_ref[pl.ds(start, 104), :]
        low = jnp.where(odd, low[IMG_W : IMG_W + CHUNK_WIN], low[:CHUNK_WIN])
        rest = (128 - CHUNK_WIN, 256)
        ones, none = jnp.ones(rest, F32), jnp.zeros(rest, F32)
        stack = jnp.concatenate([high, ones, low, none, high, none], axis=0).astype(BF16)
        conv = dot(taps_ref[...], stack)
        feat = (conv * sigmoid(conv)).astype(BF16)
        total = total + dot_nt(feat, group[CHUNK_WIN:].astype(BF16))
    for s in range(N_SCORE):
        out_ref[s] = total[OWN_FEAT * s : OWN_FEAT * s + OWN_FEAT]


def projection(start, groups, rels, taps):
    vmem = pl.BlockSpec(memory_space=pltpu.VMEM)
    return pl.pallas_call(
        projection_kernel,
        in_specs=[pl.BlockSpec(memory_space=pltpu.SMEM), vmem, vmem, vmem],
        out_specs=vmem,
        out_shape=jax.ShapeDtypeStruct((N_SCORE, OWN_FEAT, D), F32),
        scratch_shapes=[pltpu.VMEM((2 * D + 24, 256), F32), pltpu.VMEM((2 * D + 24, 256), F32)],
        compiler_params=params(),
        cost_estimate=cost(2 * FEAT * TRIPS * 640, 4 << 20),
        name="projection",
    )(start, groups, rels, taps)


def exchange(x, axes):
    return lax.all_to_all(x, axes, split_axis=0, concat_axis=0, tiled=True)


def high_part(x):
    return x.astype(BF16).astype(F32)


def taps_kernel(place_ref, small_ref, offset_ref, taps_ref, spread_ref, chunk_ref, twice_ref, all_ref):
    columns = small_ref[...].T
    twice_ref[0:CH, :] = columns[:CH]
    twice_ref[CH : 2 * CH, :] = columns[:CH]
    columns = columns[:CH]

    def one_of(codes, columns):
        value = jnp.zeros(codes.shape, F32)
        for k, offset in enumerate(OFFSETS):
            value = jnp.where(codes == offset, columns[:, k : k + 1], value)
        return value

    def bias_parts(columns):
        bias = columns[:, 9:10]
        first = high_part(bias)
        second = high_part(bias - first)
        return first, second, bias - first - second

    for g in range(BAND // CH):
        at = slice(CH * g, CH * g + CH)
        codes = offset_ref[at]
        low = codes >= LOW - 1
        value = one_of(jnp.where(low, codes - LOW, codes), columns)
        value = jnp.where(low, value - high_part(value), value)
        for part, column in enumerate(bias_parts(columns)):
            value = jnp.where(codes == BIAS_MARK + part, column, value)
        all_ref[at, :] = value
    whole = all_ref[...]
    taps_ref[...] = whole.astype(BF16)
    high = whole[:, :128].T[:WIN]
    low = pltpu.roll(whole, 256 - 2 * WIN, 1)[:, :128].T[:WIN]
    spread_ref[...] = jnp.concatenate([high, low], axis=0).astype(BF16)

    first = place_ref[0] * CHUNK
    base = place_ref[1] * IMG_W
    columns = twice_ref[pl.ds(pl.multiple_of((place_ref[0] % 4) * 8, 8), CH), :]
    parts = bias_parts(columns)
    lane = lax.broadcasted_iota(I32, (CH, 128), 1)
    for g in range(CHUNK // CH + 1):
        size = min(CH, CHUNK - CH * g)
        feature = lax.broadcasted_iota(I32, (CH, 128), 0) + (first + CH * g)
        place = feature >> 5
        row = ((place.astype(F32) + 0.5) * (1.0 / OUT_W)).astype(I32)
        origin = row * IMG_W + (place - row * OUT_W) - base
        value = jnp.where(lane < CHUNK_WIN, one_of(lane - origin, columns), 0.0)
        high = high_part(value)
        biased = high
        for part in range(3):
            biased = jnp.where(lane == CHUNK_WIN + part, parts[part], biased)
        whole = jnp.concatenate([biased, high, value - high], axis=1).astype(BF16)
        chunk_ref[CH * g : CH * g + size, :] = whole[:size]


def build_taps(place, small, offsets):
    vmem = pl.BlockSpec(memory_space=pltpu.VMEM)
    return pl.pallas_call(
        taps_kernel,
        in_specs=[pl.BlockSpec(memory_space=pltpu.SMEM), vmem, vmem],
        out_specs=(vmem,) * 3,
        out_shape=(
            jax.ShapeDtypeStruct((BAND, 256), BF16),
            jax.ShapeDtypeStruct((2 * WIN, BAND), BF16),
            jax.ShapeDtypeStruct((CHUNK, 384), BF16),
        ),
        scratch_shapes=[pltpu.VMEM((2 * CH, 128), F32), pltpu.VMEM((BAND, 256), F32)],
        compiler_params=params(),
        cost_estimate=cost(1 << 20, 3 << 20),
        name="build_taps",
    )(place, small, offsets)


def shards(
    table,
    accum,
    request,
    head_slot,
    rel_ids,
    tail_slot,
    relations,
    kernel,
    conv_bias,
    fc_weight,
    fc_bias,
):
    table_t = table.T
    asked = jnp.concatenate(
        [
            request[0],
            jnp.zeros((DEVS, SLOTS), I32),
            jnp.broadcast_to(rel_ids[None], (DEVS, TRIPS)),
        ],
        axis=1,
    )
    asked, rounded = lax.optimization_barrier((exchange(asked, AXES), round_table(table_t)))
    want = asked[:, :SLOTS].reshape(1, ALL_SLOTS)
    group = asked[:, 128:].reshape(N_EMB, N_SCORE, TRIPS)
    group = lax.dynamic_index_in_dim(group, lax.axis_index("score"), 1, keepdims=False)
    outgoing = gather_rows(want, rounded)
    incoming = exchange(outgoing, AXES)

    tails = jnp.pad(tail_slot, ((0, 0), (0, 128 - CAND)), constant_values=-1)
    counts = count_tails(tails)
    hot = (jnp.arange(NREL, dtype=I32)[:, None] == rel_ids[None, :]).astype(F32)
    rel_t = jnp.dot(relations.T, hot, precision=lax.Precision.HIGHEST)
    emb = lax.axis_index("emb")
    start = window_start(emb)
    small = jnp.concatenate([kernel, conv_bias[None]], axis=0)
    small = jnp.pad(small, ((0, 118), (0, 128 - CH)))
    offsets = jnp.asarray(offset_map())
    taps, spread, chunk_taps = build_taps(jnp.stack([emb, start]), small, offsets)
    weight = transpose_weight(fc_weight.T)
    rels = group_relations(
        group.reshape(1, N_EMB * TRIPS), jnp.pad(relations.T, ((0, 0), (0, RELP - NREL)))
    )
    true_row = tail_slot[:, :1].T
    head_row = head_slot[None, :]
    ready = (counts, rel_t, taps, spread, chunk_taps, weight, rels, true_row)
    incoming, ready = lax.optimization_barrier((incoming, ready))
    counts, rel_t, taps, spread, chunk_taps, weight, rels, true_row = ready

    part, send, state = front(
        incoming, head_row, rel_t, taps, fc_weight.T, counts, true_row, fc_bias[None, :]
    )
    groups = exchange(send, "emb")
    returned = exchange(
        back(state, taps, spread, weight, offsets, part, rel_ids[None, :], head_row), AXES
    )

    halves = projection(start.reshape(1), groups, rels, chunk_taps)
    halves = halves.reshape(N_SCORE // 2, 2, OWN_FEAT, D)
    here = lax.axis_index("score")
    side = here & 1
    kept = lax.dynamic_index_in_dim(halves, side, 1, keepdims=False)
    sent = lax.dynamic_index_in_dim(halves, 1 - side, 1, keepdims=False)
    left = kept + lax.ppermute(sent, "score", [(i, i ^ 1) for i in range(N_SCORE)])
    fc_grad = lax.dynamic_index_in_dim(left, here >> 1, 0, keepdims=False)
    pieces = []
    for step in range(1, 4):
        sent = lax.dynamic_index_in_dim(left, (here >> 1) ^ step, 0, keepdims=False)
        pairs = [(i, i ^ (2 * step)) for i in range(N_SCORE)]
        pieces.append(lax.ppermute(sent, "score", pairs))

    sums = exchange(sum_shares(returned), AXES)
    new_table, new_accum = update(want, returned, table_t, accum.T)
    pieces, sums = lax.optimization_barrier((pieces, sums))
    fc_grad = fc_grad + pieces[0] + pieces[1] + pieces[2]
    rel_sum, kernel_sum, conv_sum, fc_sum = spread_sums(sums)
    return (
        new_table.T,
        new_accum.T,
        fc_grad,
        kernel_sum,
        conv_sum[0],
        fc_sum[0],
        rel_sum.T,
    )


def solution(mesh):
    rows = P(AXES, None)
    in_specs = (rows, rows, P(AXES, None, None), P(AXES), P(AXES), rows) + (P(),) * 5
    out_specs = (rows, rows, rows) + (P(),) * 4
    return jax.shard_map(shards, mesh=mesh, in_specs=in_specs, out_specs=out_specs, check_vma=False)
```

```python
import jax
import jax.numpy as jnp
import numpy as np
from jax import lax
from jax.experimental import pallas as pl
from jax.experimental.pallas import tpu as pltpu
from jax.sharding import PartitionSpec as P

AXES = ("emb", "score")
DEVS = 128
N_EMB = 16
N_SCORE = 8
SLOTS = 64
ALL_SLOTS = DEVS * SLOTS
OWNED = 2048
D = 200
DP = 208
HALF = DP // 2
TRIPS = 128
CAND = 65
IMG_W = 20
OUT_W = 18
CH = 32
FEAT = 10368
BAND = 1152
BANDS = 9
WIN = 80
STEP = 40
NREL = 1345
RELP = 1408
REL_ROWS = 200 * 11
SHARE = 18
SHARE_ROWS = 24
SMALL_DEV = 124
MSG_ROWS = HALF + SHARE_ROWS
CHUNK = FEAT // N_EMB
OWN_FEAT = FEAT // DEVS
CHUNK_WIN = 80
LEARN = 0.1
EPS = 1e-10
F32 = jnp.float32
BF16 = jnp.bfloat16
I32 = jnp.int32
NT = (((1,), (1,)), ((), ()))
FILL = 0.9999

OFFSETS = [20 * a + b for a in range(3) for b in range(3)]
BIAS_MARK = 500
LOW = 1000


def offset_map():
    feature = np.arange(BAND)
    place = feature // CH
    origin = (place // OUT_W) * IMG_W + place % OUT_W
    lane = np.arange(256)
    offset = lane[None, :] % WIN - origin[:, None]
    offset = np.where((offset >= 0) & (offset < 43), offset, -1)
    offset = np.where(lane[None, :] < 2 * WIN, offset, offset + LOW)
    for part in range(16):
        offset[:, 3 * WIN + part] = BIAS_MARK + part
    return offset.astype(np.int32)


def window_start(emb):
    return emb * CHUNK // (OUT_W * CH)


def params(mib=40):
    return pltpu.CompilerParams(vmem_limit_bytes=mib << 20)


VMEM_SPEC = pl.BlockSpec()
HBM_SPEC = pl.BlockSpec(memory_space=pltpu.HBM)
ANY_SPEC = pl.BlockSpec(memory_space=pl.ANY)
AT_QUERY = 2 * D
AT_BIAS = AT_QUERY + DP
AT_DPRE = AT_BIAS + 16
STATE = AT_DPRE + D
GROUP = CHUNK_WIN + D


def cost(flops, moved):
    return pl.CostEstimate(flops=flops, bytes_accessed=moved, transcendentals=0)


def dot(a, b):
    return jnp.dot(a, b, preferred_element_type=F32)


def dot_nt(a, b):
    return lax.dot_general(a, b, NT, preferred_element_type=F32)


def split(x):
    high = x.astype(BF16)
    low = (x - high.astype(F32)).astype(BF16)
    return high, low


def sigmoid(value):
    return 0.5 * jnp.tanh(0.5 * value) + 0.5


def silu_slope(value):
    sig = sigmoid(value)
    return sig * (1.0 + value * (1.0 - sig))


def as_column(row):
    return jnp.broadcast_to(row, (128, row.shape[1])).T


def to_messages(x):
    top, bottom = x[:HALF], x[HALF:]
    left = lax.broadcasted_iota(I32, (HALF, 128), 1) < SLOTS
    first = jnp.where(left, top, pltpu.roll(bottom, SLOTS, 1))
    second = jnp.where(left, pltpu.roll(top, SLOTS, 1), bottom)
    return first, second


def from_messages(first, second):
    left = lax.broadcasted_iota(I32, (HALF, 128), 1) < SLOTS
    top = jnp.where(left, first, pltpu.roll(second, SLOTS, 1))
    bottom = jnp.where(left, pltpu.roll(first, SLOTS, 1), second)
    return jnp.concatenate([top, bottom], axis=0)


def code_share(x):
    most = jnp.max(jnp.abs(x), axis=0, keepdims=True)
    power = jnp.clip(jnp.ceil(jnp.log2(jnp.maximum(most, 1e-30))), -90.0, 90.0)
    scaled = x * (jnp.exp2(15.0 - power) * FILL)
    fixed = jnp.floor(scaled + 0.5)
    rest = jnp.floor((scaled - fixed) * 16384.0 + 0.5)
    row = lax.broadcasted_iota(I32, (SHARE_ROWS, 128), 0)
    tail = jnp.where(row == SHARE, power, pltpu.roll(rest, SHARE + 1, 0))
    return jnp.where(row < SHARE, fixed, tail)


def decode_share(coded):
    row = lax.broadcasted_iota(I32, (SHARE_ROWS, 128), 0)
    rest = pltpu.roll(coded, SHARE_ROWS - SHARE - 1, 0) * (1.0 / 16384.0)
    first = SHARE_ROWS - SHARE - 1
    value = coded + jnp.where(row < first, rest, 0.0)
    return jnp.where(row < SHARE, value, 0.0) * (jnp.exp2(coded[SHARE : SHARE + 1] - 15.0) * (1.0 / FILL))


def rounded_kernel(table_ref, out_ref):
    out_ref[...] = jnp.concatenate(
        [table_ref[...], jnp.zeros((DP - D, 512), F32)], axis=0
    ).astype(BF16)


def round_table(table_t):
    return pl.pallas_call(
        rounded_kernel,
        grid=(4,),
        in_specs=[pl.BlockSpec((D, 512), lambda i: (0, i))],
        out_specs=pl.BlockSpec((DP, 512), lambda i: (0, i)),
        out_shape=jax.ShapeDtypeStruct((DP, OWNED), BF16),
        compiler_params=params(60),
        cost_estimate=cost(1 << 20, 3 << 20),
        name="round_table",
    )(table_t)


def gather_kernel(want_ref, table_ref, out_ref, rows, outs, sems):
    table_copy = pltpu.make_async_copy(table_ref, rows, sems.at[4])
    table_copy.start()
    table_copy.wait()

    def out_copy(i):
        at = pl.ds(i * 32, 32)
        return pltpu.make_async_copy(outs.at[at], out_ref.at[at], sems.at[i])

    def block(i, carry):
        for q in range(8):
            want = want_ref[:, pl.ds(pl.multiple_of(i * 2048 + 256 * q, 256), 256)]
            total = jnp.zeros((DP, 256), F32)
            for kb in range(OWNED // 256):
                row = lax.broadcasted_iota(I32, (256, 256), 0) + 256 * kb
                hot = jnp.where(row == want, 1.0, 0.0).astype(BF16)
                total = total + dot(rows[:, 256 * kb : 256 * kb + 256], hot)
            for half in range(2):
                first, second = to_messages(total[:, 128 * half : 128 * half + 128])
                outs[32 * i + 4 * q + 2 * half] = first.astype(BF16)
                outs[32 * i + 4 * q + 2 * half + 1] = second.astype(BF16)
        out_copy(i).start()
        return carry

    lax.fori_loop(0, 4, block, 0, unroll=True)
    for i in range(4):
        out_copy(i).wait()


def gather_rows(want, table_t):
    return pl.pallas_call(
        gather_kernel,
        in_specs=[VMEM_SPEC, HBM_SPEC],
        out_specs=HBM_SPEC,
        out_shape=jax.ShapeDtypeStruct((DEVS, HALF, 128), BF16),
        scratch_shapes=[
            pltpu.VMEM((DP, OWNED), BF16),
            pltpu.VMEM((DEVS, HALF, 128), BF16),
            pltpu.SemaphoreType.DMA((5,)),
        ],
        compiler_params=params(60),
        cost_estimate=cost(2 * DP * OWNED * ALL_SLOTS, 6 << 20),
        name="gather_rows",
    )(want, table_t)


def counts_kernel(tail_ref, out_ref, buf_ref):
    high_row = lax.broadcasted_iota(I32, (64, 128), 0)
    low_row = lax.broadcasted_iota(I32, (128, 128), 0)

    def one(t, carry):
        slot = tail_ref[pl.ds(t, 1), :]
        high = jnp.where(high_row == (slot >> 7), 1.0, 0.0).astype(BF16)
        low = jnp.where(low_row == (slot & 127), 1.0, 0.0).astype(BF16)
        buf_ref[pl.ds(pl.multiple_of(t * 64, 64), 64), :] = dot_nt(high, low)
        return carry

    lax.fori_loop(0, TRIPS, one, 0, unroll=8)
    for high in range(64):
        out_ref[:, 128 * high : 128 * high + 128] = buf_ref[
            pl.ds(high, TRIPS, stride=64), :
        ].astype(BF16)


def count_tails(tails):
    return pl.pallas_call(
        counts_kernel,
        out_shape=jax.ShapeDtypeStruct((TRIPS, ALL_SLOTS), BF16),
        scratch_shapes=[pltpu.VMEM((ALL_SLOTS, 128), F32)],
        compiler_params=params(),
        cost_estimate=cost(TRIPS * 2 * 64 * 128 * 128, 2 << 20),
        name="count_tails",
    )(tails)


def window_parts(image_ref, p):
    win = image_ref[pl.ds(pl.multiple_of(p * STEP, 8), WIN), :]
    high = win.astype(BF16).astype(F32)
    ones = jnp.ones((256 - 3 * WIN, TRIPS), F32)
    return high, win - high, ones


def front_kernel(
    msg_ref, head_ref, rel_ref, taps_ref, weight_ref, count_ref, true_ref, bias_ref,
    part_ref, send_ref, state_ref,
    msgs, heads, taps, weights, counts, trues, biases, parts, rows_t, own, state, sems,
):
    def msg_copy(i):
        at = pl.ds(i * 32, 32)
        return pltpu.make_async_copy(msg_ref.at[at], msgs.at[at], sems.at[i])

    def part_copy(i):
        cols = pl.ds(pl.multiple_of(i * 2048, 2048), 2048)
        return pltpu.make_async_copy(parts.at[:, cols], part_ref.at[:, cols], sems.at[4 + i])

    rel_at = state.at[pl.ds(D, D)]
    pairs = [(head_ref, heads), (rel_ref, rel_at), (taps_ref, taps), (weight_ref, weights)]
    pairs += [(bias_ref, biases), (true_ref, trues), (count_ref, counts)]
    loads = [pltpu.make_async_copy(a, b, sems.at[8 + k]) for k, (a, b) in enumerate(pairs)]
    loads[0].start()
    for i in range(4):
        msg_copy(i).start()
    for load in loads[1:]:
        load.start()
    loads[0].wait()

    def unpack(i, head):
        msg_copy(i).wait()
        for k in range(8):
            both = []
            for pair in (16 * i + 2 * k, 16 * i + 2 * k + 1):
                first = msgs[2 * pair].astype(F32)
                second = msgs[2 * pair + 1].astype(F32)
                both.append(from_messages(first, second))
            both = jnp.concatenate(both, axis=1).astype(BF16)
            base = pl.multiple_of(i * 2048 + k * 256, 256)
            rows_t[:, pl.ds(base, 256)] = both
            slot = lax.broadcasted_iota(I32, (256, TRIPS), 0) + base
            hot = jnp.where(slot == heads[...], 1.0, 0.0).astype(BF16)
            head = head + dot(both, hot)
        return head

    head = lax.fori_loop(0, 4, unpack, jnp.zeros((DP, TRIPS), F32), unroll=True)
    state[0:D, :] = head[:D]

    for load in loads[1:4]:
        load.wait()
    pre = jnp.zeros((D, TRIPS), F32)
    for p in range(BANDS):
        high, low, ones = window_parts(state, p)
        stack = jnp.concatenate([high, low, high, ones], axis=0).astype(BF16)
        conv = dot(taps[...], stack)
        feat = (conv * sigmoid(conv)).astype(BF16)
        pre = pre + dot(weights[:, p * BAND : p * BAND + BAND], feat)

    for load in loads[4:]:
        load.wait()
    bias = jnp.concatenate([biases[...], jnp.zeros((1, 256 - D), F32)], axis=1)
    pre = pre + as_column(bias)[:D]
    true = as_column(trues[...])
    true = jnp.concatenate([true, true], axis=1)
    query = pre * sigmoid(pre)
    pad = jnp.zeros((DP - D, TRIPS), F32)
    query = jnp.concatenate([query, pad], axis=0)
    state[AT_QUERY:AT_BIAS, :] = query
    wide = jnp.concatenate([query, jnp.zeros((256 - DP, TRIPS), F32)], axis=0).T[:, :DP]
    high = wide.astype(BF16).astype(F32)
    both = jnp.concatenate([high, wide - high], axis=0).astype(BF16)

    def block(i, total):
        for k in range(8):
            base = pl.multiple_of(i * 2048 + k * 256, 256)
            cols = pl.ds(base, 256)
            rows = rows_t[:, cols]
            scores = dot(both, rows)
            scores = scores[:TRIPS] + scores[TRIPS:]
            lane = lax.broadcasted_iota(I32, (TRIPS, 256), 1) + base
            label = jnp.where(lane == true, 1.0, 0.0)
            grad = counts[:, cols].astype(F32) * sigmoid(scores) - label
            part = jnp.concatenate(split(grad), axis=0)
            parts[:, cols] = part
            total = total + dot_nt(rows, part)
        part_copy(i).start()
        return total

    total = lax.fori_loop(0, 4, block, jnp.zeros((DP, 256), F32), unroll=True)
    dquery = (total[:D, :TRIPS] + total[:D, TRIPS:]) * (1.0 / CAND)
    dpre = dquery * silu_slope(pre)
    total = jnp.concatenate(
        [jnp.sum(dpre, axis=1, keepdims=True), jnp.zeros((256 - D, 1), F32)], axis=0
    )
    total = jnp.broadcast_to(total, (256, 128)).T[:8]
    state[AT_BIAS:AT_DPRE, :] = jnp.concatenate([total[:, :128], total[:, 128:]], axis=0)
    state[AT_DPRE:, :] = dpre
    head = jnp.concatenate([head[:D], jnp.zeros((D + 32, TRIPS), F32)], axis=0)
    for e in range(N_EMB):
        at = window_start(e) * IMG_W
        own[e] = jnp.concatenate([head[at : at + CHUNK_WIN], dpre], axis=0).astype(BF16)
    sends = [pltpu.make_async_copy(own, send_ref, sems.at[15])]
    sends.append(pltpu.make_async_copy(state, state_ref, sems.at[16]))
    for send in sends:
        send.start()
    for send in sends:
        send.wait()
    for i in range(4):
        part_copy(i).wait()


def front(msgs, head_row, rel_t, taps, weight_t, counts, true_row, bias_row):
    return pl.pallas_call(
        front_kernel,
        in_specs=[ANY_SPEC] + [HBM_SPEC] * 7,
        out_specs=(HBM_SPEC,) * 3,
        out_shape=(
            jax.ShapeDtypeStruct((2 * TRIPS, ALL_SLOTS), BF16),
            jax.ShapeDtypeStruct((N_EMB, GROUP, TRIPS), BF16),
            jax.ShapeDtypeStruct((STATE, TRIPS), F32),
        ),
        scratch_shapes=[
            pltpu.VMEM((DEVS, HALF, 128), BF16),
            pltpu.VMEM((1, TRIPS), I32),
            pltpu.VMEM((BAND, 256), BF16),
            pltpu.VMEM((D, FEAT), BF16),
            pltpu.VMEM((TRIPS, ALL_SLOTS), BF16),
            pltpu.VMEM((1, TRIPS), I32),
            pltpu.VMEM((1, D), F32),
            pltpu.VMEM((2 * TRIPS, ALL_SLOTS), BF16),
            pltpu.VMEM((DP, ALL_SLOTS), BF16),
            pltpu.VMEM((N_EMB, GROUP, TRIPS), BF16),
            pltpu.VMEM((STATE, TRIPS), F32),
            pltpu.SemaphoreType.DMA((17,)),
        ],
        compiler_params=params(57),
        cost_estimate=cost(8 * 256 * DP * ALL_SLOTS, 20 << 20),
        name="front",
    )(msgs, head_row, rel_t, taps, weight_t, counts, true_row, bias_row)


def back_kernel(
    state_ref, taps_ref, spread_ref, weight_ref, offset_ref, part_ref, rel_ref, head_ref,
    out_ref,
    state, taps, spreads, weights, offsets, parts, outs, shares, dimage_ref, grad_ref, flat_ref,
    sems,
):
    def weight_copy(i):
        at = pl.ds(pl.multiple_of(i * 3 * BAND, BAND), 3 * BAND)
        return pltpu.make_async_copy(weight_ref.at[at], weights.at[at], sems.at[i])

    def out_copy(i):
        at = pl.ds(i * 32, 32)
        return pltpu.make_async_copy(outs.at[at], out_ref.at[at], sems.at[3 + i])

    pairs = [(state_ref, state), (taps_ref, taps), (spread_ref, spreads)]
    pairs += [(offset_ref, offsets), (part_ref, parts)]
    loads = [pltpu.make_async_copy(a, b, sems.at[7 + k]) for k, (a, b) in enumerate(pairs)]
    for load in loads[:2]:
        load.start()
    weight_copy(0).start()
    loads[2].start()
    for i in range(1, 3):
        weight_copy(i).start()
    for load in loads[3:]:
        load.start()
    for load in loads[:3]:
        load.wait()

    dimage_ref[...] = jnp.zeros_like(dimage_ref)
    grad_ref[...] = jnp.zeros_like(grad_ref)
    dpre = state[AT_DPRE:, :].astype(BF16)

    def bands(i, carry):
        weight_copy(i).wait()
        for k in range(3):
            p = 3 * i + k
            high, low, ones = window_parts(state, p)
            stack = jnp.concatenate([high, low, high, ones], axis=0).astype(BF16)
            none = jnp.zeros_like(low)
            stack_high = jnp.concatenate([high, none, high, ones], axis=0).astype(BF16)
            conv = dot(taps[...], stack)
            weight = weights[pl.ds(pl.multiple_of(p * BAND, BAND), BAND), :]
            dfeat = dot(weight, dpre)
            dconv = jnp.concatenate(split(dfeat * silu_slope(conv)), axis=1)
            grad_ref[...] += dot_nt(dconv, jnp.concatenate([stack, stack_high], axis=1))
            spread = dot(spreads[...], dconv)
            spread = spread[:WIN] + spread[WIN:]
            spread = spread[:, :TRIPS] + spread[:, TRIPS:]
            dimage_ref[pl.ds(pl.multiple_of(p * STEP, 8), WIN), :] += spread
        return carry

    lax.fori_loop(0, 3, bands, 0)
    for load in loads[3:]:
        load.wait()

    drel = dimage_ref[D : 2 * D, :]
    high = drel.astype(BF16).astype(F32)
    both = jnp.concatenate([high, drel - high], axis=0).astype(BF16)
    rel = as_column(rel_ref[...])
    for j in range(RELP // 128):
        lane = lax.broadcasted_iota(I32, (TRIPS, 128), 1) + 128 * j
        hot = jnp.where(lane == rel, 1.0, 0.0).astype(BF16)
        part = dot(both, hot)
        part = part[:D] + part[D:]
        for i in range(D // 8):
            tile = 11 * i + j
            flat_ref[8 * tile : 8 * tile + 8, :] = part[8 * i : 8 * i + 8]

    lane = lax.broadcasted_iota(I32, (CH, 128), 1)
    totals = [jnp.zeros((CH, 128), F32) for _ in range(10)]
    for g in range(BAND // CH):
        at = slice(CH * g, CH * g + CH)
        whole = grad_ref[at]
        both = whole[:, :128] + pltpu.roll(whole, 256 - WIN, 1)[:, :128]
        mark = offsets[at, 0:128]
        for k, offset in enumerate(OFFSETS):
            here = (mark == offset) & (lane < WIN)
            totals[k] = totals[k] + jnp.where(here, both, 0.0)
        totals[9] = totals[9] + jnp.where(lane == 3 * WIN - 128, whole[:, 128:], 0.0)
    small = jnp.zeros((CH, 128), F32)
    for k in range(10):
        small = jnp.where(lane == k, jnp.sum(totals[k], axis=1, keepdims=True), small)
    small = jnp.concatenate([small, jnp.zeros((128 - CH, 128), F32)], axis=0).T[:16]
    row = lax.broadcasted_iota(I32, (8, 128), 0)
    lane = lax.broadcasted_iota(I32, (8, 128), 1)
    tail = jnp.zeros((8, 128), F32)
    for k in range(10):
        at = CH * (k % 4)
        moved = small[k : k + 1] if at == 0 else pltpu.roll(small[k : k + 1], at, 1)
        here = (row == k // 4) & (lane >= at) & (lane < at + CH)
        tail = jnp.where(here, moved, tail)
    tail = jnp.where(row == 3, state[AT_BIAS : AT_BIAS + 1, :], tail)
    tail = jnp.where(row == 4, state[AT_BIAS + 8 : AT_BIAS + 9, :], tail)

    flat_ref[REL_ROWS:, :] = jnp.zeros((DEVS * SHARE - REL_ROWS, 128), F32)
    flat_ref[SMALL_DEV * SHARE : SMALL_DEV * SHARE + 8, :] = tail
    blank = jnp.zeros((SHARE_ROWS - SHARE, 128), F32)
    for dev in range(DEVS):
        mine = flat_ref[dev * SHARE : dev * SHARE + SHARE, :]
        shares[dev] = jnp.concatenate([mine, blank], axis=0)

    owner = as_column(head_ref[...])
    owner = jnp.concatenate([owner, owner], axis=1)
    q_high, q_low = split(state[AT_QUERY:AT_BIAS, :] * (1.0 / CAND))
    dhead = jnp.concatenate([dimage_ref[0:D, :], jnp.zeros((DP - D, TRIPS), F32)], axis=0)
    left = jnp.concatenate([q_high, q_low, q_high, *split(dhead)], axis=1)

    def slots(nb):
        base = pl.multiple_of(nb * 256, 256)
        cols = pl.ds(base, 256)
        high = parts[0:TRIPS, cols]
        low = parts[TRIPS:, cols]
        lane = lax.broadcasted_iota(I32, (TRIPS, 256), 1) + base
        hot = jnp.where(lane == owner, 1.0, 0.0).astype(BF16)
        grad = dot(left, jnp.concatenate([high, high, low, hot, hot], axis=0))
        most = jnp.max(jnp.abs(grad), axis=0, keepdims=True)
        power = jnp.clip(jnp.ceil(jnp.log2(jnp.maximum(most, 1e-30))), -90.0, 90.0)
        fixed = jnp.floor(grad * (jnp.exp2(15.0 - power) * FILL) + 0.5)
        row = lax.broadcasted_iota(I32, (DP, 256), 0)
        fixed = jnp.where(row == D, power, fixed)
        for half in range(2):
            pair = to_messages(fixed[:, 128 * half : 128 * half + 128])
            for k in range(2):
                dev = 4 * nb + 2 * half + k
                whole = jnp.concatenate([pair[k], code_share(shares[dev])], axis=0)
                outs[dev] = whole.astype(I32).astype(jnp.int16)

    def chunk(i, carry):
        for k in range(8):
            slots(8 * i + k)
        out_copy(i).start()
        return carry

    lax.fori_loop(0, 4, chunk, 0, unroll=True)
    for i in range(4):
        out_copy(i).wait()


def back(state, taps, spread, weight, offsets, part, rel_row, head_row):
    return pl.pallas_call(
        back_kernel,
        in_specs=[HBM_SPEC] * 6 + [VMEM_SPEC] * 2,
        out_specs=HBM_SPEC,
        out_shape=jax.ShapeDtypeStruct((DEVS, MSG_ROWS, 128), jnp.int16),
        scratch_shapes=[
            pltpu.VMEM((STATE, TRIPS), F32),
            pltpu.VMEM((BAND, 256), BF16),
            pltpu.VMEM((2 * WIN, BAND), BF16),
            pltpu.VMEM((FEAT, D), BF16),
            pltpu.VMEM((BAND, 256), I32),
            pltpu.VMEM((2 * TRIPS, ALL_SLOTS), BF16),
            pltpu.VMEM((DEVS, MSG_ROWS, 128), jnp.int16),
            pltpu.VMEM((DEVS, SHARE_ROWS, 128), F32),
            pltpu.VMEM((2 * D, TRIPS), F32),
            pltpu.VMEM((BAND, 256), F32),
            pltpu.VMEM((DEVS * SHARE, 128), F32),
            pltpu.SemaphoreType.DMA((12,)),
        ],
        compiler_params=params(60),
        cost_estimate=cost(8 * 256 * FEAT * TRIPS, 20 << 20),
        name="back",
    )(state, taps, spread, weight, offsets, part, rel_row, head_row)


def update_kernel(
    want_ref, msg_ref, table_ref, accum_ref, table_out, accum_out,
    part_ref, column_ref, total_ref, msgs, sems,
):
    nb = pl.program_id(0)

    def msg_copy(kb):
        at = pl.ds(32 * kb, 32)
        return pltpu.make_async_copy(msg_ref.at[at], msgs.at[at], sems.at[kb])

    def unpack(pair):
        cols = slice(pair * 128, pair * 128 + 128)
        fixed = from_messages(
            msgs[2 * pair].astype(I32).astype(F32)[:HALF],
            msgs[2 * pair + 1].astype(I32).astype(F32)[:HALF],
        )
        grad = fixed * (jnp.exp2(fixed[D : D + 1] - 15.0) * (1.0 / FILL))
        high = high_part(grad[:D])
        part_ref[:, cols] = jnp.concatenate([high, grad[:D] - high], axis=0).astype(BF16)
        column_ref[cols, :] = as_column(want_ref[:, cols])

    def block(kb):
        slots = slice(kb * 2048, kb * 2048 + 2048)
        lane = lax.broadcasted_iota(I32, (2048, 128), 1) + nb * 512
        column = column_ref[slots, :]
        hot = [jnp.where(column == lane + 128 * k, 1.0, 0.0).astype(BF16) for k in range(4)]
        return dot(part_ref[:, slots], jnp.concatenate(hot, axis=1))

    @pl.when(nb == 0)
    def _():
        for kb in range(4):
            msg_copy(kb).start()
        total = jnp.zeros((2 * D, 512), F32)
        for kb in range(4):
            msg_copy(kb).wait()
            for pair in range(16):
                unpack(16 * kb + pair)
            total = total + block(kb)
        total_ref[...] = total

    @pl.when(nb > 0)
    def _():
        total = jnp.zeros((2 * D, 512), F32)
        for kb in range(4):
            total = total + block(kb)
        total_ref[...] = total

    grad = total_ref[:D] + total_ref[D:]
    accum = accum_ref[...] + grad * grad
    accum_out[...] = accum
    table_out[...] = table_ref[...] - LEARN * grad / (jnp.sqrt(accum) + EPS)


def update(want, msgs, table_t, accum_t):
    rows = pl.BlockSpec((D, 512), lambda i: (0, i))
    return pl.pallas_call(
        update_kernel,
        grid=(OWNED // 512,),
        in_specs=[
            pl.BlockSpec((1, ALL_SLOTS), lambda i: (0, 0)),
            ANY_SPEC,
            rows,
            rows,
        ],
        out_specs=(rows, rows),
        out_shape=(
            jax.ShapeDtypeStruct((D, OWNED), F32),
            jax.ShapeDtypeStruct((D, OWNED), F32),
        ),
        scratch_shapes=[
            pltpu.VMEM((2 * D, ALL_SLOTS), BF16),
            pltpu.VMEM((ALL_SLOTS, 128), I32),
            pltpu.VMEM((2 * D, 512), F32),
            pltpu.VMEM((DEVS, MSG_ROWS, 128), jnp.int16),
            pltpu.SemaphoreType.DMA((4,)),
        ],
        compiler_params=params(60),
        cost_estimate=cost(4 * DP * OWNED * ALL_SLOTS, 10 << 20),
        name="update",
    )(want, msgs, table_t, accum_t)


def share_kernel(msg_ref, out_ref):
    def one(dev, total):
        coded = msg_ref[dev].astype(I32).astype(F32)
        return total + decode_share(coded[32 - SHARE_ROWS :])

    total = lax.fori_loop(0, DEVS, one, jnp.zeros((SHARE_ROWS, 128), F32), unroll=16)
    coded = code_share(total).astype(I32).astype(jnp.int16)
    for dev in range(DEVS):
        out_ref[dev] = coded


def sum_shares(msgs):
    return pl.pallas_call(
        share_kernel,
        grid=(1,),
        in_specs=[pl.BlockSpec((DEVS, 32, 128), lambda i: (0, MSG_ROWS // 32 - 1, 0))],
        out_specs=pl.BlockSpec((DEVS, SHARE_ROWS, 128), lambda i: (0, 0, 0)),
        out_shape=jax.ShapeDtypeStruct((DEVS, SHARE_ROWS, 128), jnp.int16),
        compiler_params=params(),
        cost_estimate=cost(1 << 20, 2 << 20),
        name="sum_shares",
    )(msgs)


def spread_kernel(sum_ref, rel_ref, kernel_ref, conv_ref, fc_ref, flat_ref):
    for dev in range(DEVS):
        value = decode_share(sum_ref[dev].astype(I32).astype(F32))
        flat_ref[dev * SHARE : dev * SHARE + SHARE, :] = value[:SHARE]
    for i in range(D // 8):
        for j in range(11):
            tile = flat_ref[8 * (11 * i + j) : 8 * (11 * i + j) + 8, :]
            last = min(128, NREL - 128 * j)
            rel_ref[8 * i : 8 * i + 8, 128 * j : 128 * j + last] = tile[:, :last]
    small = flat_ref[SMALL_DEV * SHARE : SMALL_DEV * SHARE + 8, :]
    for k in range(10):
        at = CH * (k % 4)
        row = small[k // 4 : k // 4 + 1]
        row = (row if at == 0 else pltpu.roll(row, 128 - at, 1))[:, :CH]
        if k < 9:
            kernel_ref[k : k + 1, :] = row
        else:
            conv_ref[...] = row
    fc_ref[...] = jnp.concatenate([small[3:4], small[4:5]], axis=1)[:, :D]


def spread_sums(sums):
    return pl.pallas_call(
        spread_kernel,
        out_shape=(
            jax.ShapeDtypeStruct((D, NREL), F32),
            jax.ShapeDtypeStruct((9, CH), F32),
            jax.ShapeDtypeStruct((1, CH), F32),
            jax.ShapeDtypeStruct((1, D), F32),
        ),
        scratch_shapes=[pltpu.VMEM((DEVS * SHARE, 128), F32)],
        compiler_params=params(),
        cost_estimate=cost(1 << 20, 2 << 20),
        name="spread_sums",
    )(sums)


def transpose_kernel(weight_ref, out_ref):
    wide = jnp.concatenate(
        [weight_ref[...].astype(F32), jnp.zeros((256 - D, BAND), F32)], axis=0
    ).T
    out_ref[...] = wide[:, :D].astype(BF16)


def transpose_weight(weight_t):
    return pl.pallas_call(
        transpose_kernel,
        grid=(BANDS,),
        in_specs=[pl.BlockSpec((D, BAND), lambda i: (0, i))],
        out_specs=pl.BlockSpec((BAND, D), lambda i: (i, 0)),
        out_shape=jax.ShapeDtypeStruct((FEAT, D), BF16),
        compiler_params=params(),
        cost_estimate=cost(1 << 20, 9 << 20),
        name="transpose_weight",
    )(weight_t)


def relations_kernel(ids_ref, rel_ref, out_ref):
    rel = rel_ref[...]
    high = rel.astype(BF16).astype(F32)
    both = jnp.concatenate([high, rel - high], axis=0).astype(BF16)
    for e in range(0, N_EMB, 2):
        cols = slice(128 * e, 128 * e + 256)
        row = lax.broadcasted_iota(I32, (RELP, 256), 0)
        hot = jnp.where(row == ids_ref[:, cols], 1.0, 0.0).astype(BF16)
        out_ref[:, cols] = dot(both, hot).astype(BF16)


def group_relations(ids, relations_t):
    return pl.pallas_call(
        relations_kernel,
        out_shape=jax.ShapeDtypeStruct((2 * D, N_EMB * TRIPS), BF16),
        compiler_params=params(),
        cost_estimate=cost(4 * D * RELP * N_EMB * TRIPS, 3 << 20),
        name="group_relations",
    )(ids, relations_t)


def projection_kernel(start_ref, group_ref, rel_ref, taps_ref, out_ref, high_ref, low_ref):
    start = pl.multiple_of((start_ref[0] >> 1) * STEP, 8)
    odd = (start_ref[0] & 1) == 1
    blank = jnp.zeros((24, 256), F32)
    total = jnp.zeros((CHUNK, D), F32)
    for e in range(0, N_EMB, 2):
        cols = slice(128 * e, 128 * e + 256)
        group = jnp.concatenate([group_ref[e], group_ref[e + 1]], axis=1).astype(F32)
        head = group[:CHUNK_WIN]
        rel = rel_ref[:, cols].astype(F32)
        high_ref[...] = jnp.concatenate([jnp.zeros((D, 256), F32), rel[:D], blank], axis=0)
        low_ref[...] = jnp.concatenate([jnp.zeros((D, 256), F32), rel[D:], blank], axis=0)
        high = high_ref[pl.ds(start, 104), :]
        high = head + jnp.where(odd, high[IMG_W : IMG_W + CHUNK_WIN], high[:CHUNK_WIN])
        low = low_ref[pl.ds(start, 104), :]
        low = jnp.where(odd, low[IMG_W : IMG_W + CHUNK_WIN], low[:CHUNK_WIN])
        rest = (128 - CHUNK_WIN, 256)
        ones, none = jnp.ones(rest, F32), jnp.zeros(rest, F32)
        stack = jnp.concatenate([high, ones, low, none, high, none], axis=0).astype(BF16)
        conv = dot(taps_ref[...], stack)
        feat = (conv * sigmoid(conv)).astype(BF16)
        total = total + dot_nt(feat, group[CHUNK_WIN:].astype(BF16))
    for s in range(N_SCORE):
        out_ref[s] = total[OWN_FEAT * s : OWN_FEAT * s + OWN_FEAT]


def projection(start, groups, rels, taps):
    vmem = pl.BlockSpec(memory_space=pltpu.VMEM)
    return pl.pallas_call(
        projection_kernel,
        in_specs=[pl.BlockSpec(memory_space=pltpu.SMEM), vmem, vmem, vmem],
        out_specs=vmem,
        out_shape=jax.ShapeDtypeStruct((N_SCORE, OWN_FEAT, D), F32),
        scratch_shapes=[pltpu.VMEM((2 * D + 24, 256), F32), pltpu.VMEM((2 * D + 24, 256), F32)],
        compiler_params=params(),
        cost_estimate=cost(2 * FEAT * TRIPS * 640, 4 << 20),
        name="projection",
    )(start, groups, rels, taps)


def exchange(x, axes):
    return lax.all_to_all(x, axes, split_axis=0, concat_axis=0, tiled=True)


def high_part(x):
    return x.astype(BF16).astype(F32)


def taps_kernel(place_ref, small_ref, offset_ref, taps_ref, spread_ref, chunk_ref, twice_ref, all_ref):
    columns = small_ref[...].T
    twice_ref[0:CH, :] = columns[:CH]
    twice_ref[CH : 2 * CH, :] = columns[:CH]
    columns = columns[:CH]

    def one_of(codes, columns):
        value = jnp.zeros(codes.shape, F32)
        for k, offset in enumerate(OFFSETS):
            value = jnp.where(codes == offset, columns[:, k : k + 1], value)
        return value

    def bias_parts(columns):
        bias = columns[:, 9:10]
        first = high_part(bias)
        second = high_part(bias - first)
        return first, second, bias - first - second

    for g in range(BAND // CH):
        at = slice(CH * g, CH * g + CH)
        codes = offset_ref[at]
        low = codes >= LOW - 1
        value = one_of(jnp.where(low, codes - LOW, codes), columns)
        value = jnp.where(low, value - high_part(value), value)
        for part, column in enumerate(bias_parts(columns)):
            value = jnp.where(codes == BIAS_MARK + part, column, value)
        all_ref[at, :] = value
    whole = all_ref[...]
    taps_ref[...] = whole.astype(BF16)
    high = whole[:, :128].T[:WIN]
    low = pltpu.roll(whole, 256 - 2 * WIN, 1)[:, :128].T[:WIN]
    spread_ref[...] = jnp.concatenate([high, low], axis=0).astype(BF16)

    first = place_ref[0] * CHUNK
    base = place_ref[1] * IMG_W
    columns = twice_ref[pl.ds(pl.multiple_of((place_ref[0] % 4) * 8, 8), CH), :]
    parts = bias_parts(columns)
    lane = lax.broadcasted_iota(I32, (CH, 128), 1)
    for g in range(CHUNK // CH + 1):
        size = min(CH, CHUNK - CH * g)
        feature = lax.broadcasted_iota(I32, (CH, 128), 0) + (first + CH * g)
        place = feature >> 5
        row = ((place.astype(F32) + 0.5) * (1.0 / OUT_W)).astype(I32)
        origin = row * IMG_W + (place - row * OUT_W) - base
        value = jnp.where(lane < CHUNK_WIN, one_of(lane - origin, columns), 0.0)
        high = high_part(value)
        biased = high
        for part in range(3):
            biased = jnp.where(lane == CHUNK_WIN + part, parts[part], biased)
        whole = jnp.concatenate([biased, high, value - high], axis=1).astype(BF16)
        chunk_ref[CH * g : CH * g + size, :] = whole[:size]


def build_taps(place, small, offsets):
    vmem = pl.BlockSpec(memory_space=pltpu.VMEM)
    return pl.pallas_call(
        taps_kernel,
        in_specs=[pl.BlockSpec(memory_space=pltpu.SMEM), vmem, vmem],
        out_specs=(vmem,) * 3,
        out_shape=(
            jax.ShapeDtypeStruct((BAND, 256), BF16),
            jax.ShapeDtypeStruct((2 * WIN, BAND), BF16),
            jax.ShapeDtypeStruct((CHUNK, 384), BF16),
        ),
        scratch_shapes=[pltpu.VMEM((2 * CH, 128), F32), pltpu.VMEM((BAND, 256), F32)],
        compiler_params=params(),
        cost_estimate=cost(1 << 20, 3 << 20),
        name="build_taps",
    )(place, small, offsets)


def shards(
    table,
    accum,
    request,
    head_slot,
    rel_ids,
    tail_slot,
    relations,
    kernel,
    conv_bias,
    fc_weight,
    fc_bias,
):
    table_t = table.T
    asked = jnp.concatenate(
        [
            request[0],
            jnp.zeros((DEVS, SLOTS), I32),
            jnp.broadcast_to(rel_ids[None], (DEVS, TRIPS)),
        ],
        axis=1,
    )
    asked, rounded = lax.optimization_barrier((exchange(asked, AXES), round_table(table_t)))
    want = asked[:, :SLOTS].reshape(1, ALL_SLOTS)
    group = asked[:, 128:].reshape(N_EMB, N_SCORE, TRIPS)
    group = lax.dynamic_index_in_dim(group, lax.axis_index("score"), 1, keepdims=False)
    outgoing = gather_rows(want, rounded)
    incoming = exchange(outgoing, AXES)

    tails = jnp.pad(tail_slot, ((0, 0), (0, 128 - CAND)), constant_values=-1)
    counts = count_tails(tails)
    hot = (jnp.arange(NREL, dtype=I32)[:, None] == rel_ids[None, :]).astype(F32)
    rel_t = jnp.dot(relations.T, hot, precision=lax.Precision.HIGHEST)
    emb = lax.axis_index("emb")
    start = window_start(emb)
    small = jnp.concatenate([kernel, conv_bias[None]], axis=0)
    small = jnp.pad(small, ((0, 118), (0, 128 - CH)))
    offsets = jnp.asarray(offset_map())
    taps, spread, chunk_taps = build_taps(jnp.stack([emb, start]), small, offsets)
    weight = transpose_weight(fc_weight.T)
    rels = group_relations(
        group.reshape(1, N_EMB * TRIPS), jnp.pad(relations.T, ((0, 0), (0, RELP - NREL)))
    )
    true_row = tail_slot[:, :1].T
    head_row = head_slot[None, :]
    ready = (counts, rel_t, taps, spread, chunk_taps, weight, rels, true_row)
    incoming, ready = lax.optimization_barrier((incoming, ready))
    counts, rel_t, taps, spread, chunk_taps, weight, rels, true_row = ready

    part, send, state = front(
        incoming, head_row, rel_t, taps, fc_weight.T, counts, true_row, fc_bias[None, :]
    )
    groups = exchange(send, "emb")
    returned = exchange(
        back(state, taps, spread, weight, offsets, part, rel_ids[None, :], head_row), AXES
    )

    halves = projection(start.reshape(1), groups, rels, chunk_taps)
    halves = halves.reshape(N_SCORE // 2, 2, OWN_FEAT, D)
    here = lax.axis_index("score")
    side = here & 1
    kept = lax.dynamic_index_in_dim(halves, side, 1, keepdims=False)
    sent = lax.dynamic_index_in_dim(halves, 1 - side, 1, keepdims=False)
    left = kept + lax.ppermute(sent, "score", [(i, i ^ 1) for i in range(N_SCORE)])
    fc_grad = lax.dynamic_index_in_dim(left, here >> 1, 0, keepdims=False)
    pieces = []
    for step in range(1, 4):
        sent = lax.dynamic_index_in_dim(left, (here >> 1) ^ step, 0, keepdims=False)
        pairs = [(i, i ^ (2 * step)) for i in range(N_SCORE)]
        pieces.append(lax.ppermute(sent, "score", pairs))

    sums = exchange(sum_shares(returned), AXES)
    new_table, new_accum = update(want, returned, table_t, accum.T)
    pieces, sums = lax.optimization_barrier((pieces, sums))
    fc_grad = fc_grad + pieces[0] + pieces[1] + pieces[2]
    rel_sum, kernel_sum, conv_sum, fc_sum = spread_sums(sums)
    return (
        new_table.T,
        new_accum.T,
        fc_grad,
        kernel_sum,
        conv_sum[0],
        fc_sum[0],
        rel_sum.T,
    )


def solution(mesh):
    rows = P(AXES, None)
    in_specs = (rows, rows, P(AXES, None, None), P(AXES), P(AXES), rows) + (P(),) * 5
    out_specs = (rows, rows, rows) + (P(),) * 4
    return jax.shard_map(shards, mesh=mesh, in_specs=in_specs, out_specs=out_specs, check_vma=False)
```
